256 devices in a mesh: worker: 32 (over x, z_hi, core), fsdp: 8 (over z_lo, y).
Axes of the slice: x: 4, y: 4, z: 8 (z_hi: 4, z_lo: 2; z = z_hi * 2 + z_lo), core: 2. Of those that a mesh axis runs over, the one named last changes fastest.
Arguments:
- token_ids: int32 [65536], P(('worker', 'fsdp')), may hold values from 0 to 128255, as said below
- layer_inputs: bfloat16 [2, 65536, 8192], P(None, ('worker', 'fsdp')), may hold values from -6 to 6
- key_grads: bfloat16 [2, 65536, 512], P(None, ('worker', 'fsdp')), may hold values from -0.125 to 0.125
- weights: bfloat16 [32, 2, 8192, 512], P('worker', None, 'fsdp'), may hold values from -6 to 6
- anchors: float32 [2, 8192, 512], P(None, ('fsdp', 'worker')), may hold values from -6 to 6
- momentum: float32 [8192, 512], P(('fsdp', 'worker')), may hold values from -3 to 3
- plan: int32 [1], replicated, may hold values from 0 to 1023
Outputs:
- weights_new: bfloat16 [32, 2, 8192, 512], P('worker', None, 'fsdp')
- anchor_new: float32 [8192, 512], P(('fsdp', 'worker'))
- momentum_new: float32 [8192, 512], P(('fsdp', 'worker'))
- pending: float32 [8192, 512], P(('fsdp', 'worker'))
The draws below stay inside these ranges and needn't reach their ends.
Inputs may be any that keep to these rules, and one draw needn't show every extreme that they name: `token_ids`: 0 marks a token left out of the loss; other values are vocabulary ids.
All inputs are finite; a program needn't handle non-finite values.
Results may differ from the reference program's by a relative error of at most 0.01.
Values may be sent and summed in bfloat16 or wider, within the bound.
No kernel may reach another device: no remote copies, remote signals or barrier semaphores. Data moves between devices by JAX's collectives and lax.ppermute only.
A program may use at most 128 MiB of HBM per device.

```python
import jax
import jax.numpy as jnp
from jax import lax

D = 8192
VOCAB = 128256
KVW = 512
TOK_DEV = 256
TOKENS = 65536
N_WORKER = 32
N_FSDP = 8


def draw_token_ids(key, part):
    key = jax.random.fold_in(key, 11)
    first_key, second_key = jax.random.split(key)
    words = jax.random.randint(first_key, (TOKENS,), 1, VOCAB)
    dropped = jax.random.randint(second_key, (TOKENS,), 0, 4)
    return jnp.where(dropped == 0, 0, words).astype(jnp.int32)


def with_spikes(result, stream_key, source, target, shards_of, factor):
    owner, partner = [(jnp.arange(result.shape[dim]) // (result.shape[dim] // shards_of)).reshape([-1 if axis == dim else 1 for axis in range(result.ndim)]) for dim in (source, target)]
    chosen = jax.random.permutation(stream_key, shards_of)[partner]
    strong = (owner == chosen) | (owner == (partner + shards_of // 2) % shards_of)
    return jnp.where(strong, factor * result, result)


def block_levels(stream_key, dims, cuts, smallest, largest):
    level, own = 1.0, jax.random.fold_in(stream_key, 6)
    for position, blocks in cuts:
        draws = jnp.exp(jax.random.uniform(jax.random.fold_in(own, position), (blocks,), jnp.float32, smallest / len(cuts), largest / len(cuts)))
        level = level * jnp.repeat(draws, dims[position] // blocks).reshape([-1 if axis == position else 1 for axis in range(len(dims))])
    return level


def centred(rng, dims, deviation, reach, cuts=(), kind=jnp.bfloat16):
    drawn = jax.random.normal(rng, dims, jnp.float32) * deviation
    if len(cuts) > 0:
        drawn = block_levels(rng, dims, cuts, -0.22, 0.18) * drawn
    return jnp.clip(drawn, min=-reach, max=reach).astype(kind)


def bell_draw_with(key, extent, scale, bound, cuts, heavy, kind=jnp.bfloat16):
    entries = scale * jax.random.normal(key, extent, jnp.float32)
    if cuts:
        entries = entries * block_levels(key, extent, cuts, -0.22, 0.18)
    return jnp.clip(with_spikes(entries, jax.random.fold_in(key, 3), *heavy), -bound, bound).astype(kind)


def setup_inputs(seed: int = 0) -> dict:
    keys = jax.random.split(jax.random.key(seed), 8)
    token_ids = draw_token_ids(jax.random.fold_in(keys[7], 71), 0)
    layer_inputs = centred(keys[1], (2, TOKENS, D), 1.0, 6.0, ((1, 256),))
    key_grads = centred(keys[2], (2, TOKENS, KVW), (TOK_DEV * N_FSDP) ** -0.5, 0.125, ((1, 256),))
    weights = bell_draw_with(keys[3], (N_WORKER, 2, D, KVW), 1.0, 6.0, ((0, 32), (2, 8)), (0, 2, 32, 2.75))
    anchors = centred(keys[4], (2, D, KVW), 1.0, 6.0, ((1, 256),), jnp.float32)
    momentum = centred(keys[5], (D, KVW), 0.5, 3.0, ((0, 256),), jnp.float32)
    plan = jax.random.randint(keys[6], (1,), 0, 1024).astype(jnp.int32)
    return dict(token_ids=token_ids, layer_inputs=layer_inputs, key_grads=key_grads, weights=weights, anchors=anchors, momentum=momentum, plan=plan)


inner_rate = 0.25
decay_rate = 0.1
outer_rate = 0.7
outer_beta = 0.9
mix_weight = 0.5


def reference(token_ids, layer_inputs, key_grads, weights, anchors, momentum, plan):
    groups = N_WORKER
    shards = N_FSDP
    chosen = jnp.remainder(plan[0], 2).astype(jnp.int32)
    other = (1 - chosen).astype(jnp.int32)
    kept_mask = (token_ids != 0).astype(jnp.bfloat16)
    masked = key_grads * kept_mask[None, :, None]
    inputs_split = layer_inputs.reshape(2, groups, shards, TOK_DEV, D)
    grads_split = masked.reshape(2, groups, shards, TOK_DEV, KVW)

    def one_worker(running, worker_index):
        worker_inputs = lax.dynamic_index_in_dim(inputs_split, worker_index, 1, keepdims=False)
        worker_grads = lax.dynamic_index_in_dim(grads_split, worker_index, 1, keepdims=False)

        def add_shard(total_grad, shard_index):
            piece_inputs = lax.dynamic_index_in_dim(worker_inputs, shard_index, 1, keepdims=False)
            piece_grads = lax.dynamic_index_in_dim(worker_grads, shard_index, 1, keepdims=False)
            partial_value = jnp.einsum("ltr,ltc->lrc", piece_inputs.astype(jnp.float32), piece_grads.astype(jnp.float32), precision=lax.Precision.HIGHEST)
            rounded = lax.optimization_barrier(partial_value.astype(jnp.bfloat16))
            return total_grad + rounded.astype(jnp.float32), None

        gradient, _ = lax.scan(add_shard, jnp.zeros((2, D, KVW), jnp.float32), jnp.arange(shards, dtype=jnp.int32))
        own_rows = lax.dynamic_index_in_dim(weights, worker_index, 0, keepdims=False)
        inner_new = (own_rows.astype(jnp.float32) * (1.0 - inner_rate * decay_rate) - inner_rate * gradient).astype(jnp.bfloat16)
        return running + inner_new.astype(jnp.float32), inner_new

    summed, inner_all = lax.scan(one_worker, jnp.zeros((2, D, KVW), jnp.float32), jnp.arange(groups, dtype=jnp.int32))
    sum_sync = lax.dynamic_index_in_dim(summed, chosen, 0, keepdims=False)
    sum_other = lax.dynamic_index_in_dim(summed, other, 0, keepdims=False)
    anchor_now = lax.dynamic_index_in_dim(anchors, chosen, 0, keepdims=False)
    anchor_other = lax.dynamic_index_in_dim(anchors, other, 0, keepdims=False)
    outer_grad = anchor_now - sum_sync / groups
    momentum_new = outer_beta * momentum + outer_grad
    anchor_new = anchor_now - outer_rate * (outer_grad + outer_beta * momentum_new)
    pending = anchor_other - sum_other / groups
    synced = lax.dynamic_index_in_dim(inner_all, chosen, 1, keepdims=False)
    mixed_rows = (mix_weight * synced.astype(jnp.float32) + (1.0 - mix_weight) * anchor_new[None]).astype(jnp.bfloat16)
    is_synced = jnp.arange(2, dtype=jnp.int32) == chosen
    weights_new = jnp.where(is_synced[None, :, None, None], mixed_rows[:, None], inner_all)
    return (weights_new, anchor_new, momentum_new, pending)
```

```python
import jax
import jax.numpy as jnp
from jax import lax
from jax.experimental import pallas as pl
from jax.experimental.pallas import tpu as pltpu
from jax.sharding import PartitionSpec as P

inner_rate = 0.25
decay_rate = 0.1
outer_rate = 0.7
outer_beta = 0.9
mix_weight = 0.5

TOK = 256
KV = 512
ROWS = 1024
HALF = 512
F32 = jnp.float32
BF16 = jnp.bfloat16

ANY = pl.BlockSpec(memory_space=pl.ANY)
VM = pl.BlockSpec(memory_space=pltpu.VMEM)
SM = pl.BlockSpec(memory_space=pltpu.SMEM)
PARAMS = pltpu.CompilerParams(vmem_limit_bytes=40 * 1024 * 1024)


def place():
    w = lax.axis_index("worker")
    f = lax.axis_index("fsdp")
    return w // 8, (w // 2) % 4, w % 2, f // 4, f % 4


def cost(flops, nbytes):
    return pl.CostEstimate(flops=flops, bytes_accessed=nbytes, transcendentals=0)


def shape(*dims, dtype=BF16):
    return jax.ShapeDtypeStruct(dims, dtype)


def call(kernel, outs, args, specs, out_specs, scratch=(), flops=0, nbytes=0, aliases=None, name=None):
    return pl.pallas_call(
        kernel,
        out_shape=outs,
        in_specs=specs,
        out_specs=out_specs,
        scratch_shapes=list(scratch),
        compiler_params=PARAMS,
        cost_estimate=cost(flops, nbytes),
        input_output_aliases=aliases or {},
        name=name,
    )(*args)


def columns(start, width):
    return pl.ds(pl.multiple_of(start, width), width)


def pack_kernel(plan, tok, x, g, buf_a, buf_b, buf_z, gt_out, gin, gt, sems, gsems):
    _, _, _, z, y = place()
    s = lax.rem(plan[0], 2)
    copies = []

    def send(layer, col, width, dst, at):
        copies.append(
            pltpu.make_async_copy(
                x.at[layer, :, columns(col, width)], dst.at[:, pl.ds(at, width)], sems.at[len(copies)]
            )
        )
        copies[-1].start()

    g_copies = [pltpu.make_async_copy(g.at[layer], gin.at[i], gsems.at[i]) for i, layer in enumerate((s, 1 - s))]
    for c in g_copies:
        c.start()
    for buf, first, second, offset in ((buf_a, y ^ 1, y ^ 2, 0), (buf_b, y ^ 3, y ^ 2, HALF)):
        for i, (zz, yy) in enumerate(((z, first), (1 - z, first), (z, second), (1 - z, second))):
            send(s, (zz * 4 + yy) * ROWS + offset, HALF, buf, i * HALF)
    for j in range(4):
        send(1 - s, ((1 - z) * 4 + (y ^ j)) * ROWS, ROWS, buf_z, j * ROWS)
    kept = (tok[...] != 0).astype(F32)
    for i in range(2):
        g_copies[i].wait()
        gt[i] = (gin[i].astype(F32).T * kept).astype(BF16)
    last = []

    def put(src, dst):
        last.append(pltpu.make_async_copy(src, dst, gsems.at[2 + len(last)]))
        last[-1].start()

    for i, bufs, at in ((0, (buf_a, buf_b), 4 * HALF), (1, (buf_z,), 4 * ROWS)):
        for buf in bufs:
            for h in range(2):
                put(gt.at[i, pl.ds(h * TOK, TOK)], buf.at[:, pl.ds(at + h * TOK, TOK)])
    put(gt, gt_out)
    for c in copies + last:
        c.wait()


def pack(plan, tok, x, g):
    return call(
        pack_kernel,
        (shape(TOK, 5 * HALF), shape(TOK, 5 * HALF), shape(TOK, 4 * ROWS + KV), shape(2, KV, TOK)),
        (plan, tok, x, g),
        [SM, VM, ANY, ANY],
        [ANY] * 4,
        [
            pltpu.VMEM((2, TOK, KV), BF16),
            pltpu.VMEM((2, KV, TOK), BF16),
            pltpu.SemaphoreType.DMA((12,)),
            pltpu.SemaphoreType.DMA((9,)),
        ],
        nbytes=10 * 2**20,
        name="pack",
    )


def product(name, fragment, pieces, out_shapes, g_at, plan, x, gt, recv):
    width = pieces[0][2]
    count = len(pieces)

    def kernel(plan_ref, x_ref, gt_ref, recv_ref, *rest):
        outs = rest[: len(out_shapes)]
        stage = rest[len(out_shapes) : 2 * len(out_shapes)]
        gts, xs, rs, sems, out_sems = rest[2 * len(out_shapes) :]
        _, _, _, z, y = place()
        s = lax.rem(plan_ref[0], 2)
        layer = s if fragment == 0 else 1 - s
        g_copies = [
            pltpu.make_async_copy(gt_ref.at[fragment], gts.at[:, pl.ds(0, TOK)], sems.at[2 * count]),
            *(
                pltpu.make_async_copy(
                    recv_ref.at[:, pl.ds(g_at + h * TOK, TOK)],
                    gts.at[pl.ds(h * TOK, TOK), pl.ds(TOK, TOK)],
                    sems.at[2 * count + 1 + h],
                )
                for h in range(2)
            ),
        ]
        copies = []
        for p, (own, at, _, _) in enumerate(pieces):
            copies.append(
                (
                    pltpu.make_async_copy(x_ref.at[layer, :, columns(own(z, y), width)], xs.at[p, pl.ds(0, TOK)], sems.at[2 * p]),
                    pltpu.make_async_copy(recv_ref.at[:, pl.ds(at, width)], xs.at[p, pl.ds(TOK, TOK)], sems.at[2 * p + 1]),
                )
            )
        for c in g_copies:
            c.start()
        for pair in copies:
            for c in pair:
                c.start()
        for c in g_copies:
            c.wait()
        done = []
        for p, (_, _, _, targets) in enumerate(pieces):
            for c in copies[p]:
                c.wait()
            for out, slot, k0, k1 in targets:
                stage[out][slot] = jnp.dot(gts[k0:k1], xs[p], preferred_element_type=F32).astype(BF16)
                c = pltpu.make_async_copy(stage[out].at[slot], outs[out].at[slot], out_sems.at[len(done)])
                c.start()
                done.append(c)
        for c in done:
            c.wait()

    total = sum(len(p[3]) for p in pieces)
    return call(
        kernel,
        tuple(shape(*d) for d in out_shapes),
        (plan, x, gt, recv),
        [SM, ANY, ANY, ANY],
        [ANY] * len(out_shapes),
        [
            *(pltpu.VMEM(d, BF16) for d in out_shapes),
            pltpu.VMEM((KV, 2 * TOK), BF16),
            pltpu.VMEM((count, 2 * TOK, width), BF16),
            pltpu.VMEM((8, 128), BF16),
            pltpu.SemaphoreType.DMA((2 * count + 3,)),
            pltpu.SemaphoreType.DMA((total,)),
        ],
        flops=sum(2 * 2 * TOK * width * (k1 - k0) for p in pieces for _, _, k0, k1 in p[3]),
        nbytes=sum(2 * 2 * TOK * width for _ in pieces) + sum(2 * a * b * c for a, b, c in out_shapes),
        name=name,
    )


def flip(*terms):
    return sum(t.astype(F32) for t in terms).T


def stepped(w, gradient):
    return (w.astype(F32) * (1.0 - inner_rate * decay_rate) - inner_rate * gradient).astype(BF16)


def inner_sync(plan, w, ka, ra, kb, rb):
    def kernel(plan_ref, w_ref, ka_ref, ra_ref, kb_ref, rb_ref, inner_ref, send_ref, wv, sem, sem2):
        s = lax.rem(plan_ref[0], 2)
        core = place()[2]
        load = pltpu.make_async_copy(w_ref.at[s], wv, sem)
        load.start()
        load.wait()
        for h, (k_ref, r_ref) in enumerate(((ka_ref, ra_ref), (kb_ref, rb_ref))):
            for q in range(4):
                cols = pl.ds(q * 128, 128)
                i = h * 8 + q * 2
                new = stepped(wv[i : i + 2].reshape(128, KV), flip(k_ref[:, cols], r_ref[:, cols]))
                inner_ref[i : i + 2] = new.reshape(2, 2, 32, KV)
        out = pltpu.make_async_copy(inner_ref.at[:, 1 - core], send_ref, sem2)
        out.start()
        out.wait()

    return call(
        kernel,
        (shape(16, 2, 32, KV), shape(16, 32, KV)),
        (plan, w, ka, ra, kb, rb),
        [SM, ANY, VM, VM, VM, VM],
        [VM, ANY],
        [pltpu.VMEM((16, 2, 32, KV), BF16), pltpu.SemaphoreType.DMA, pltpu.SemaphoreType.DMA],
        nbytes=5 * 2**20,
        name="inner_sync",
    )


def inner_other(plan, w, k0, r0, k1, r1):
    def kernel(plan_ref, w_ref, k0_ref, r0_ref, k1_ref, r1_ref, inner_ref, send_ref, new_ref, wv, sem, sem2):
        other = 1 - lax.rem(plan_ref[0], 2)
        core = place()[2]
        load = pltpu.make_async_copy(w_ref.at[other], wv, sem)
        load.start()
        load.wait()
        for q in range(8):
            cols = pl.ds(q * 128, 128)
            i = q * 2
            gradient = jnp.concatenate(
                [flip(k0_ref[:, cols], r0_ref[:, cols]), flip(k1_ref[:, cols], r1_ref[:, cols])], axis=1
            )
            inner_ref[i : i + 2] = stepped(wv[i : i + 2].reshape(128, KV), gradient).reshape(2, 2, 32, KV)
        out = pltpu.make_async_copy(inner_ref.at[:, 1 - core], send_ref, sem2.at[0])
        keep = pltpu.make_async_copy(inner_ref, new_ref.at[other], sem2.at[1])
        out.start()
        keep.start()
        out.wait()
        keep.wait()

    return call(
        kernel,
        (shape(16, 2, 32, KV), shape(16, 32, KV), shape(2, 16, 2, 32, KV)),
        (plan, w, k0, r0, k1, r1),
        [SM, ANY, VM, VM, VM, VM],
        [VM, ANY, ANY],
        [pltpu.VMEM((16, 2, 32, KV), BF16), pltpu.SemaphoreType.DMA, pltpu.SemaphoreType.DMA((2,))],
        nbytes=6 * 2**20,
        name="inner_other",
    )


def add_cores(inner, recv, name):
    def kernel(inner_ref, recv_ref, *outs):
        x, _, core, _, _ = place()
        for d in range(4):
            block = pl.ds(lax.rem(x + d, 4) * 4, 4)
            outs[d][...] = (inner_ref[block, core].astype(F32) + recv_ref[block].astype(F32)).astype(BF16)

    return call(
        kernel, (shape(4, 32, KV),) * 4, (inner, recv), [VM, VM], [VM] * 4, nbytes=2 * 2**20, name=name
    )


def add_x(parts, name):
    def kernel(a, b, c, d, *outs):
        zh = place()[1]
        for i in range(4):
            at = lax.rem(zh + i, 4)
            outs[i][...] = sum(t[at].astype(F32) for t in (a, b, c, d)).astype(BF16)

    return call(kernel, (shape(32, KV),) * 4, parts, [VM] * 4, [VM] * 4, nbytes=2**20, name=name)


def outer_sync(plan, anchors, momentum, parts):
    def kernel(plan_ref, anchor_ref, momentum_ref, a, b, c, d, new_ref, moment_ref, short_ref):
        s = lax.rem(plan_ref[0], 2)
        mean = sum(t[...].astype(F32) for t in (a, b, c, d)) / 32
        anchor = anchor_ref[s]
        outer_grad = anchor - mean
        moment = outer_beta * momentum_ref[...] + outer_grad
        new = anchor - outer_rate * (outer_grad + outer_beta * moment)
        new_ref[...] = new
        moment_ref[...] = moment
        short_ref[...] = new.astype(BF16)

    return call(
        kernel,
        (shape(32, KV, dtype=F32), shape(32, KV, dtype=F32), shape(32, KV)),
        (plan, anchors, momentum, *parts),
        [SM] + [VM] * 6,
        [VM] * 3,
        nbytes=2**19,
        name="outer_sync",
    )


def outer_other(plan, anchors, parts):
    def kernel(plan_ref, anchor_ref, a, b, c, d, out_ref):
        other = 1 - lax.rem(plan_ref[0], 2)
        out_ref[...] = anchor_ref[other] - sum(t[...].astype(F32) for t in (a, b, c, d)) / 32

    return call(
        kernel, shape(32, KV, dtype=F32), (plan, anchors, *parts), [SM] + [VM] * 5, VM, nbytes=2**19, name="outer_other"
    )


def gather_z(parts):
    def kernel(a, b, c, d, out_ref):
        zh = place()[1]
        for i, t in enumerate((a, b, c, d)):
            out_ref[lax.rem(zh + 4 - i, 4)] = t[...]

    return call(kernel, shape(4, 32, KV), parts, [VM] * 4, VM, nbytes=2**18, name="gather_z")


def gather_x(parts):
    def kernel(a, b, c, d, out_ref):
        x = place()[0]
        for i, t in enumerate((a, b, c, d)):
            out_ref[pl.ds(lax.rem(x + 4 - i, 4) * 4, 4)] = t[...]

    return call(kernel, shape(16, 32, KV), parts, [VM] * 4, VM, nbytes=2**20, name="gather_x")


def mix(plan, inner, own, recv, new):
    def kernel(plan_ref, inner_ref, own_ref, recv_ref, _, out_ref, stage, sems):
        s = lax.rem(plan_ref[0], 2)
        core = place()[2]
        for i, (t, c) in enumerate(((own_ref, core), (recv_ref, 1 - core))):
            stage[:, c] = (
                mix_weight * inner_ref[:, c].astype(F32) + (1.0 - mix_weight) * t[...].astype(F32)
            ).astype(BF16)
        out = pltpu.make_async_copy(stage, out_ref.at[s], sems)
        out.start()
        out.wait()

    return call(
        kernel,
        shape(2, 16, 2, 32, KV),
        (plan, inner, own, recv, new),
        [SM, VM, VM, VM, ANY],
        ANY,
        [pltpu.VMEM((16, 2, 32, KV), BF16), pltpu.SemaphoreType.DMA],
        nbytes=4 * 2**20,
        aliases={4: 0},
        name="mix",
    )


def along_fsdp(move):
    return [(z * 4 + y, move(z, y)) for z in range(2) for y in range(4)]


TO_A = along_fsdp(lambda z, y: z * 4 + (y ^ 1))
TO_B = along_fsdp(lambda z, y: z * 4 + (y ^ 3))
TO_Z = along_fsdp(lambda z, y: (1 - z) * 4 + y)


def along_worker(dx, dz, dc):
    return [
        ((x * 4 + z) * 2 + c, (((x + dx) % 4) * 4 + (z + dz) % 4) * 2 + (c + dc) % 2)
        for x in range(4)
        for z in range(4)
        for c in range(2)
    ]


def from_x(parts):
    return [lax.ppermute(parts[d - 1], "worker", along_worker(d, 0, 0)) for d in (1, 2, 3)]


def from_z(parts):
    return [lax.ppermute(parts[d - 1], "worker", along_worker(0, d, 0)) for d in (1, 2, 3)]


def add(a, b):
    return (a.astype(F32) + b.astype(F32)).astype(BF16)


def over_workers(inner, send, tag):
    recv = lax.ppermute(send, "worker", along_worker(0, 0, 1))
    parts = add_cores(inner, recv, "add_cores_" + tag)
    sums = add_x((parts[0], *from_x(parts[1:])), "add_x_" + tag)
    return (sums[0], *from_z(sums[1:]))


def body(token_ids, layer_inputs, key_grads, weights, anchors, momentum, plan):
    x = layer_inputs
    w = weights.reshape(2, 16, 2, 32, KV)
    buf_a, buf_b, buf_z, gt = pack(plan, token_ids.reshape(1, TOK), x, key_grads)
    got_a = lax.ppermute(buf_a, "fsdp", TO_A)
    got_b = lax.ppermute(buf_b, "fsdp", TO_B)
    got_z = lax.ppermute(buf_z, "fsdp", TO_Z)

    def pieces(flip_y, offset, first):
        return [
            (lambda z, y: (z * 4 + (y ^ flip_y)) * ROWS + offset, first * HALF, HALF, [(0, 0, 0, KV)]),
            (lambda z, y: ((1 - z) * 4 + (y ^ flip_y)) * ROWS + offset, (first + 1) * HALF, HALF, [(0, 1, 0, KV)]),
        ]

    sync = [(2, KV, HALF)]
    (send_a,) = product("send_a", 0, pieces(3, 0, 2), sync, 4 * HALF, plan, x, gt, got_a)
    next_a = lax.ppermute(send_a, "fsdp", TO_B)
    (send_b,) = product("send_b", 0, pieces(1, HALF, 2), sync, 4 * HALF, plan, x, gt, got_b)
    next_b = lax.ppermute(send_b, "fsdp", TO_A)
    (keep_a,) = product("keep_a", 0, pieces(0, 0, 0), sync, 4 * HALF, plan, x, gt, got_a)
    (keep_b,) = product("keep_b", 0, pieces(0, HALF, 0), sync, 4 * HALF, plan, x, gt, got_b)
    last_a = lax.ppermute(add(keep_a[1], next_a[1]), "fsdp", TO_Z)
    last_b = lax.ppermute(add(keep_b[1], next_b[1]), "fsdp", TO_Z)
    inner_s, send_s = inner_sync(plan, w, add(keep_a[0], next_a[0]), last_a, add(keep_b[0], next_b[0]), last_b)

    def dest(j, targets):
        return (lambda z, y: (z * 4 + (y ^ j)) * ROWS, j * ROWS, ROWS, targets)

    other = [(2, 256, ROWS), (2, 256, ROWS)]
    send_0, send_1 = product(
        "send_o",
        1,
        [dest(1, [(0, 0, 0, 256)]), dest(2, [(0, 1, 0, 256), (1, 1, 256, 512)]), dest(3, [(1, 0, 256, 512)])],
        other, 4 * ROWS, plan, x, gt, got_z,
    )
    got_0 = lax.ppermute(send_0, "fsdp", TO_A)
    got_1 = lax.ppermute(send_1, "fsdp", TO_B)
    keep_0, keep_1 = product(
        "keep_o",
        1,
        [dest(3, [(0, 1, 0, 256)]), dest(1, [(1, 1, 256, 512)]), dest(0, [(0, 0, 0, 256), (1, 0, 256, 512)])],
        other, 4 * ROWS, plan, x, gt, got_z,
    )
    last_0 = lax.ppermute(add(keep_0[1], got_0[1]), "fsdp", TO_B)
    last_1 = lax.ppermute(add(keep_1[1], got_1[1]), "fsdp", TO_A)
    inner_o, send_o, new = inner_other(
        plan, w, add(keep_0[0], got_0[0]), last_0, add(keep_1[0], got_1[0]), last_1
    )

    anchor_new, momentum_new, short = outer_sync(plan, anchors, momentum, over_workers(inner_s, send_s, "s"))
    pending = outer_other(plan, anchors, over_workers(inner_o, send_o, "o"))
    row = gather_z((short, *from_z((short,) * 3)))
    block = gather_x((row, *from_x((row,) * 3)))
    across = lax.ppermute(block, "worker", along_worker(0, 0, 1))
    new = mix(plan, inner_s, block, across, new)
    return (new.reshape(1, 2, ROWS, KV), anchor_new, momentum_new, pending)


def solution(mesh):
    return jax.shard_map(
        body,
        mesh=mesh,
        in_specs=(
            P(("worker", "fsdp")),
            P(None, ("worker", "fsdp"), None),
            P(None, ("worker", "fsdp"), None),
            P("worker", None, "fsdp", None),
            P(None, ("fsdp", "worker"), None),
            P(("fsdp", "worker"), None),
            P(),
        ),
        out_specs=(
            P("worker", None, "fsdp", None),
            P(("fsdp", "worker"), None),
            P(("fsdp", "worker"), None),
            P(("fsdp", "worker"), None),
        ),
        check_vma=False,
    )
```

```python
import jax
import jax.numpy as jnp
from jax import lax
from jax.experimental import pallas as pl
from jax.experimental.pallas import tpu as pltpu
from jax.sharding import PartitionSpec as P

inner_rate = 0.25
decay_rate = 0.1
outer_rate = 0.7
outer_beta = 0.9
mix_weight = 0.5

TOK = 256
KV = 512
ROWS = 1024
HALF = 512
F32 = jnp.float32
BF16 = jnp.bfloat16

HBM = pl.BlockSpec(memory_space=pltpu.HBM)
ANY = pl.BlockSpec(memory_space=pl.ANY)
VM = pl.BlockSpec(memory_space=pltpu.VMEM)
SM = pl.BlockSpec(memory_space=pltpu.SMEM)
MIB = 1024 * 1024
BIG = 24


def place():
    w = lax.axis_index("worker")
    f = lax.axis_index("fsdp")
    return w // 8, (w // 2) % 4, w % 2, f // 4, f % 4


def shape(*dims, dtype=BF16):
    return jax.ShapeDtypeStruct(dims, dtype)


def in_vmem(*dims):
    return pltpu.VMEM(dims, BF16)


def in_hbm(*dims):
    return pltpu.HBM(dims, BF16)


def pinned(value):
    return pltpu.with_memory_space_constraint(value, pltpu.HBM)


class Chain:
    def __init__(self):
        self.token = None


CHAIN = Chain()


def call(kernel, outs, args, specs, out_specs, scratch=(), aliases=None, name=None, vmem=16, hint=0):
    outs, out_specs = list(outs), list(out_specs)
    tokens = [] if CHAIN.token is None else [CHAIN.token]
    count = len(args)

    def chained(*refs):
        rest = refs[count + len(tokens) :]
        kernel(*refs[:count], *rest[: len(outs)], *rest[len(outs) + 1 :])

    *results, CHAIN.token = pl.pallas_call(
        chained,
        out_shape=outs + [in_hbm(8, 128)],
        in_specs=list(specs) + [HBM] * len(tokens),
        out_specs=out_specs + [HBM],
        scratch_shapes=list(scratch),
        compiler_params=pltpu.CompilerParams(vmem_limit_bytes=vmem * MIB),
        cost_estimate=pl.CostEstimate(flops=hint, bytes_accessed=0, transcendentals=0),
        input_output_aliases=aliases or {},
        name=name,
    )(*(pinned(a) if spec is HBM else a for a, spec in zip(args, specs)), *(pinned(t) for t in tokens))
    return results[0] if len(results) == 1 else results


def columns(start, width):
    return pl.ds(pl.multiple_of(start, width), width)


def pack_kernel(plan, tok, x, g, a1, b1, z1, a2, b2, z2, z3, gt_out, gin, gt, sems, gsems):
    _, _, _, z, y = place()
    s = lax.rem(plan[0], 2)
    copies = []

    def send(layer, col, width, dst, at):
        copies.append(
            pltpu.make_async_copy(
                x.at[layer, :, columns(col, width)], dst.at[:, pl.ds(at, width)], sems.at[len(copies)]
            )
        )
        copies[-1].start()

    g_copies = [pltpu.make_async_copy(g.at[layer], gin.at[i], gsems.at[i]) for i, layer in enumerate((s, 1 - s))]
    for c in g_copies:
        c.start()
    for zz, bufs in ((1 - z, (a1, b1)), (z, (a2, b2))):
        for buf, first, offset in ((bufs[0], y ^ 1, 0), (bufs[1], y ^ 3, HALF)):
            for i, yy in enumerate((first, y ^ 2)):
                send(s, (zz * 4 + yy) * ROWS + offset, HALF, buf, i * HALF)
    for j, buf, at in ((1, z1, 0), (2, z1, ROWS), (3, z2, 0), (0, z3, 0)):
        send(1 - s, ((1 - z) * 4 + (y ^ j)) * ROWS, ROWS, buf, at)
    kept = (tok[...] != 0).astype(F32)
    last = []

    def put(src, dst):
        last.append(pltpu.make_async_copy(src, dst, gsems.at[2 + len(last)]))
        last[-1].start()

    for i, bufs, at in ((0, (a1, b1), 2 * HALF), (1, (z1,), 2 * ROWS)):
        g_copies[i].wait()
        gt[i] = (gin[i].astype(F32).T * kept).astype(BF16)
        for buf in bufs:
            for h in range(2):
                put(gt.at[i, pl.ds(h * TOK, TOK)], buf.at[:, pl.ds(at + h * TOK, TOK)])
    put(gt, gt_out)
    for c in copies + last:
        c.wait()


def pack(plan, tok, x, g):
    wide = in_vmem(TOK, 2 * HALF + KV)
    half = in_vmem(TOK, 2 * HALF)
    return call(
        pack_kernel,
        (wide, wide, in_vmem(TOK, 2 * ROWS + KV), half, half, half, half, in_vmem(2, KV, TOK)),
        (plan, tok, x, g),
        [SM, VM, HBM, HBM],
        [VM] * 8,
        [
            pltpu.VMEM((2, TOK, KV), BF16),
            pltpu.VMEM((2, KV, TOK), BF16),
            pltpu.SemaphoreType.DMA((12,)),
            pltpu.SemaphoreType.DMA((9,)),
        ],
        name="pack",
        vmem=BIG,
    )


def product(name, fragment, pieces, width, out_shapes, g_at, plan, x, gt, recvs, hint=0):
    count = len(pieces)
    number = len(recvs)
    total = sum(len(p[3]) for p in pieces)

    def kernel(plan_ref, x_ref, gt_ref, *rest):
        recv_refs = rest[:number]
        outs = rest[number : number + len(out_shapes)]
        stage = rest[number + len(out_shapes) : number + 2 * len(out_shapes)]
        gts, xs, sems, out_sems = rest[number + 2 * len(out_shapes) :]
        _, _, _, z, y = place()
        s = lax.rem(plan_ref[0], 2)
        layer = s if fragment == 0 else 1 - s
        g_copies = [
            pltpu.make_async_copy(gt_ref.at[fragment], gts.at[:, pl.ds(0, TOK)], sems.at[2 * count]),
            *(
                pltpu.make_async_copy(
                    recv_refs[0].at[:, pl.ds(g_at + h * TOK, TOK)],
                    gts.at[pl.ds(h * TOK, TOK), pl.ds(TOK, TOK)],
                    sems.at[2 * count + 1 + h],
                )
                for h in range(2)
            ),
        ]
        copies = []
        for p, (own, source, at, _) in enumerate(pieces):
            copies.append(
                (
                    pltpu.make_async_copy(
                        x_ref.at[layer, :, columns(own(z, y), width)], xs.at[p, pl.ds(0, TOK)], sems.at[2 * p]
                    ),
                    pltpu.make_async_copy(
                        recv_refs[source].at[:, pl.ds(at, width)], xs.at[p, pl.ds(TOK, TOK)], sems.at[2 * p + 1]
                    ),
                )
            )
        for c in g_copies:
            c.start()
        for pair in copies:
            for c in pair:
                c.start()
        for c in g_copies:
            c.wait()
        done = []
        for p, (_, _, _, targets) in enumerate(pieces):
            for c in copies[p]:
                c.wait()
            for out, slot, k0, k1 in targets:
                src = stage[out] if slot is None else stage[out].at[slot]
                dst = outs[out] if slot is None else outs[out].at[slot]
                src[...] = jnp.dot(gts[k0:k1], xs[p], preferred_element_type=F32).astype(BF16)
                c = pltpu.make_async_copy(src, dst, out_sems.at[len(done)])
                c.start()
                done.append(c)
        for c in done:
            c.wait()

    return call(
        kernel,
        tuple(shape(*d) for d in out_shapes),
        (plan, x, gt, *recvs),
        [SM, ANY, ANY] + [ANY] * number,
        [ANY] * len(out_shapes),
        [
            *(pltpu.VMEM(d, BF16) for d in out_shapes),
            pltpu.VMEM((KV, 2 * TOK), BF16),
            pltpu.VMEM((count, 2 * TOK, width), BF16),
            pltpu.SemaphoreType.DMA((2 * count + 3,)),
            pltpu.SemaphoreType.DMA((total,)),
        ],
        name=name,
        vmem=BIG,
        hint=hint,
    )


def flip(*terms):
    return sum(t.astype(F32) for t in terms).T


def stepped(w, gradient):
    return (w.astype(F32) * (1.0 - inner_rate * decay_rate) - inner_rate * gradient).astype(BF16)


WORKERS = (16, 2, 32, KV)


def inner_sync(plan, w, near, across):
    def kernel(plan_ref, w_ref, near_ref, za_ref, zb_ref, inner_ref, send_ref, wv, sem, sem2):
        s = lax.rem(plan_ref[0], 2)
        core = place()[2]
        load = pltpu.make_async_copy(w_ref.at[s], wv, sem)
        load.start()
        load.wait()
        for h, z_ref in enumerate((za_ref, zb_ref)):
            for q in range(4):
                cols = pl.ds(q * 128, 128)
                i = h * 8 + q * 2
                gradient = flip(near_ref[h, :, cols], z_ref[:, cols])
                inner_ref[i : i + 2] = stepped(wv[i : i + 2].reshape(128, KV), gradient).reshape(2, 2, 32, KV)
        out = pltpu.make_async_copy(inner_ref.at[:, 1 - core], send_ref, sem2)
        out.start()
        out.wait()

    return call(
        kernel,
        (shape(*WORKERS), shape(16, 32, KV)),
        (plan, w, near, *across),
        [SM, HBM] + [VM] * 3,
        [VM, ANY],
        [pltpu.VMEM(WORKERS, BF16), pltpu.SemaphoreType.DMA, pltpu.SemaphoreType.DMA],
        name="inner_sync",
    )


def inner_other(plan, w, first, second):
    def kernel(plan_ref, w_ref, *rest):
        k0, r0, l0, k1, r1, l1, inner_ref, send_ref, new_ref, wv, sem, sem2 = rest
        other = 1 - lax.rem(plan_ref[0], 2)
        core = place()[2]
        load = pltpu.make_async_copy(w_ref.at[other], wv, sem)
        load.start()
        load.wait()
        for q in range(8):
            cols = pl.ds(q * 128, 128)
            i = q * 2
            gradient = jnp.concatenate(
                [flip(k[:, cols], r[0, :, cols], l[:, cols]) for k, r, l in ((k0, r0, l0), (k1, r1, l1))], axis=1
            )
            inner_ref[i : i + 2] = stepped(wv[i : i + 2].reshape(128, KV), gradient).reshape(2, 2, 32, KV)
        out = pltpu.make_async_copy(inner_ref.at[:, 1 - core], send_ref, sem2.at[0])
        keep = pltpu.make_async_copy(inner_ref, new_ref.at[other], sem2.at[1])
        out.start()
        keep.start()
        out.wait()
        keep.wait()

    return call(
        kernel,
        (shape(*WORKERS), shape(16, 32, KV), shape(2, *WORKERS)),
        (plan, w, *first, *second),
        [SM, HBM] + [VM] * 6,
        [VM, ANY, ANY],
        [pltpu.VMEM(WORKERS, BF16), pltpu.SemaphoreType.DMA, pltpu.SemaphoreType.DMA((2,))],
        name="inner_other",
    )


def plus(a, b):
    return (a.astype(F32) + b.astype(F32)).astype(BF16)


def to_x(inner_ref, recv_ref, send_ref, keep_ref):
    x, _, core, _, _ = place()
    for ref, at, j in ((send_ref, 0, 1), (send_ref, 1, 2), (keep_ref, 0, 0), (keep_ref, 1, 3)):
        block = pl.ds((x ^ j) * 4, 4)
        ref[at] = plus(inner_ref[block, core], recv_ref[block])


def to_z(keep_ref, recv_ref, send_ref, stay_ref):
    zh = place()[1]
    for ref, at, j in ((send_ref, 0, 1), (send_ref, 1, 2), (stay_ref, 0, 0), (stay_ref, 1, 3)):
        ref[at] = plus(keep_ref[zh ^ j], recv_ref[zh ^ j])


QUAD = (4, 32, KV)


def sums(name, outs, pairs, extra=()):
    def kernel(*refs):
        out_refs = refs[2 * len(pairs) + len(extra) :]
        for i, (_, _, at_a, at_b, out, slot) in enumerate(pairs):
            a, b = refs[2 * i], refs[2 * i + 1]
            total = plus(a[...] if at_a is None else a[at_a], b[...] if at_b is None else b[at_b])
            if slot is None:
                out_refs[out][...] = total
            else:
                out_refs[out][slot] = total

    args = [t for p in pairs for t in p[:2]]
    return call(
        kernel,
        [shape(*d) for d in outs],
        (*args, *extra),
        [VM] * len(args) + [ANY] * len(extra),
        [VM] * len(outs),
        name=name,
    )


def halve(name, dims, keep, recv):
    return sums(name, [dims] * 2, [(keep, recv, 1, 1, 0, None), (keep, recv, 0, 0, 1, None)])


def join(a, b):
    def kernel(a_ref, b_ref, out_ref):
        out_ref[0] = a_ref[...]
        out_ref[1] = b_ref[...]

    return call(kernel, (shape(2, *a.shape),), (a, b), [VM] * 2, [VM], name="join")


def sum_x(inner, recv, name):
    return call(to_x, (shape(2, *QUAD),) * 2, (inner, recv), [VM] * 2, [VM] * 2, name=name)


def sum_z(keep, recv, name):
    return call(to_z, (shape(2, 32, KV),) * 2, (keep, recv), [VM] * 2, [VM] * 2, name=name)


def row_of(own, got):
    def kernel(own_ref, got_ref, out_ref):
        zh = place()[1]
        for ref, at, j in ((own_ref, 0, 0), (own_ref, 1, 1), (got_ref, 0, 3), (got_ref, 1, 2)):
            out_ref[zh ^ j] = ref[at]

    return call(kernel, (shape(*QUAD),), (own, got), [VM] * 2, [VM], name="row")


def block_of(own, got):
    def kernel(own_ref, got_ref, out_ref):
        x = place()[0]
        for ref, at, j in ((own_ref, 0, 0), (own_ref, 1, 3), (got_ref, 0, 1), (got_ref, 1, 2)):
            out_ref[pl.ds((x ^ j) * 4, 4)] = ref[at]

    return call(kernel, (shape(16, 32, KV),), (own, got), [VM] * 2, [VM], name="block")


def outer_sync(plan, anchors, momentum, keep, recv):
    def kernel(plan_ref, anchor_ref, momentum_ref, a, b, new_ref, moment_ref, short_ref):
        s = lax.rem(plan_ref[0], 2)
        mean = (a[...].astype(F32) + b[...].astype(F32)) / 32
        anchor = anchor_ref[s]
        outer_grad = anchor - mean
        moment = outer_beta * momentum_ref[...] + outer_grad
        new = anchor - outer_rate * (outer_grad + outer_beta * moment)
        new_ref[...] = new
        moment_ref[...] = moment
        short_ref[...] = new.astype(BF16)

    return call(
        kernel,
        (shape(32, KV, dtype=F32), shape(32, KV, dtype=F32), shape(32, KV)),
        (plan, anchors, momentum, keep, recv),
        [SM] + [VM] * 4,
        [VM] * 3,
        name="outer_sync",
    )


def outer_other(plan, anchors, keep, recv):
    def kernel(plan_ref, anchor_ref, a, b, out_ref):
        other = 1 - lax.rem(plan_ref[0], 2)
        out_ref[...] = anchor_ref[other] - (a[...].astype(F32) + b[...].astype(F32)) / 32

    return call(
        kernel,
        (shape(32, KV, dtype=F32),),
        (plan, anchors, keep, recv),
        [SM] + [VM] * 3,
        [VM],
        name="outer_other",
    )


def mix(plan, inner, own, recv, new):
    def kernel(plan_ref, inner_ref, own_ref, recv_ref, _, out_ref, stage, sems):
        s = lax.rem(plan_ref[0], 2)
        core = place()[2]
        for t, c in ((own_ref, core), (recv_ref, 1 - core)):
            stage[:, c] = (
                mix_weight * inner_ref[:, c].astype(F32) + (1.0 - mix_weight) * t[...].astype(F32)
            ).astype(BF16)
        out = pltpu.make_async_copy(stage, out_ref.at[s], sems)
        out.start()
        out.wait()

    return call(
        kernel,
        (shape(2, *WORKERS),),
        (plan, inner, own, recv, new),
        [SM, VM, VM, VM, ANY],
        [ANY],
        [pltpu.VMEM(WORKERS, BF16), pltpu.SemaphoreType.DMA],
        aliases={4: 0},
        name="mix",
    )


def along_fsdp(move):
    return [(z * 4 + y, move(z, y)) for z in range(2) for y in range(4)]


def along_worker(move):
    def index(x, z, c):
        return (x * 4 + z) * 2 + c

    return [(index(x, z, c), index(*move(x, z, c))) for x in range(4) for z in range(4) for c in range(2)]


MOVES = {
    "a": ("fsdp", along_fsdp(lambda z, y: z * 4 + (y ^ 1))),
    "b": ("fsdp", along_fsdp(lambda z, y: z * 4 + (y ^ 3))),
    "z": ("fsdp", along_fsdp(lambda z, y: (1 - z) * 4 + y)),
    "core": ("worker", along_worker(lambda x, z, c: (x, z, 1 - c))),
    "x1": ("worker", along_worker(lambda x, z, c: (x ^ 1, z, c))),
    "x3": ("worker", along_worker(lambda x, z, c: (x ^ 3, z, c))),
    "z1": ("worker", along_worker(lambda x, z, c: (x, z ^ 1, c))),
    "z3": ("worker", along_worker(lambda x, z, c: (x, z ^ 3, c))),
}


def swap(value, move):
    return lax.ppermute(value, *MOVES[move])


def body(token_ids, layer_inputs, key_grads, weights, anchors, momentum, plan):
    CHAIN.token = None
    x = layer_inputs
    w = weights.reshape(2, *WORKERS)
    a1, b1, z1, a2, b2, z2, z3, gt = pack(plan, token_ids.reshape(1, TOK), x, key_grads)
    got_a1 = swap(a1, "a")
    got_b1 = swap(b1, "b")
    got_z1 = swap(z1, "z")
    got_a2 = swap(a2, "a")
    got_b2 = swap(b2, "b")
    got_z2 = swap(z2, "z")
    got_z3 = swap(z3, "z")

    def tile(name, far, flip_y, offset, at, recvs):
        piece = (
            lambda z, y: ((1 - z if far else z) * 4 + (y ^ flip_y)) * ROWS + offset,
            len(recvs) - 1,
            at * HALF,
            [(0, None, 0, KV)],
        )
        return product(name, 0, [piece], HALF, [(KV, HALF)], 2 * HALF, plan, x, gt, recvs)

    def dest(j, source, at, targets):
        return (lambda z, y: (z * 4 + (y ^ j)) * ROWS, source, at, targets)

    def other(name, pieces, outs, recvs, hint=0):
        return product(name, 1, pieces, ROWS, outs, 2 * ROWS, plan, x, gt, recvs, hint)

    lo, hi = (0, 256), (256, 512)
    half, pair = (256, ROWS), (2, 256, ROWS)

    far_a = swap(tile("send_a1", True, 3, 0, 1, (got_a1,)), "b")
    far_b = swap(tile("send_b1", True, 1, HALF, 1, (got_b1,)), "a")
    keep_a1 = tile("keep_a1", True, 0, 0, 0, (got_a1,))
    keep_b1 = tile("keep_b1", True, 0, HALF, 0, (got_b1,))
    near_a = swap(tile("send_a2", False, 3, 0, 1, (got_a1, got_a2)), "b")
    near_b = swap(tile("send_b2", False, 1, HALF, 1, (got_b1, got_b2)), "a")
    keep_a2 = tile("keep_a2", False, 0, 0, 0, (got_a1, got_a2))
    keep_b2 = tile("keep_b2", False, 0, HALF, 0, (got_b1, got_b2))
    send_0, stay_1 = other(
        "other_1",
        [dest(2, 0, ROWS, [(0, 1, *lo)]), dest(1, 0, 0, [(0, 0, *lo), (1, None, *hi)])],
        [pair, half],
        (got_z1,),
    )
    got_0 = swap(send_0, "a")
    across = sums(
        "far", [(KV, HALF)] * 2, [(keep_a1, far_a, None, None, 0, None), (keep_b1, far_b, None, None, 1, None)]
    )
    across = [swap(t, "z") for t in across]
    near = sums("near", [(2, KV, HALF)], [(keep_a2, near_a, None, None, 0, 0), (keep_b2, near_b, None, None, 0, 1)])
    send_1, stay_0 = other(
        "other_2",
        [dest(2, 0, ROWS, [(0, 1, *hi)]), dest(3, 1, 0, [(0, 0, *hi), (1, None, *lo)])],
        [pair, half],
        (got_z1, got_z2),
        10**10,
    )
    got_1 = swap(send_1, "b")

    inner_s, send_s = inner_sync(plan, w, near, across)
    send, keep = sum_x(inner_s, swap(send_s, "core"), "sync_x1")
    recv = swap(send, "x1")
    send, keep = halve("sync_x3", QUAD, keep, recv)
    last_0, last_1 = sums(
        "last", [half, half], [(stay_0, got_0, None, 1, 0, None), (stay_1, got_1, None, 1, 1, None)]
    )
    last_0, last_1 = swap(last_0, "b"), swap(last_1, "a")
    send, keep = sum_z(keep, swap(send, "x3"), "sync_z1")
    recv = swap(send, "z1")
    mine_0, mine_1 = other("other_3", [dest(0, 1, 0, [(0, None, *lo), (1, None, *hi)])], [half, half], (got_z1, got_z3))
    send, keep = halve("sync_z3", (32, KV), keep, recv)
    anchor_new, momentum_new, short = outer_sync(plan, anchors, momentum, keep, swap(send, "z3"))
    short_far = swap(short, "z1")

    inner_o, send_o, new = inner_other(plan, w, (mine_0, got_0, last_0), (mine_1, got_1, last_1))
    core_o = swap(send_o, "core")
    own = join(short, short_far)
    send, keep = sum_x(inner_o, core_o, "other_x1")
    recv = swap(send, "x1")
    row = row_of(own, swap(own, "z3"))
    row_far = swap(row, "x3")
    send, keep = halve("other_x3", QUAD, keep, recv)
    recv = swap(send, "x3")
    own = join(row, row_far)
    got = swap(own, "x1")
    send, keep = sum_z(keep, recv, "other_z1")
    recv = swap(send, "z1")
    block = block_of(own, got)
    block_far = swap(block, "core")
    send, keep = halve("other_z3", (32, KV), keep, recv)
    recv = swap(send, "z3")
    new = mix(plan, inner_s, block, block_far, new)
    pending = outer_other(plan, anchors, keep, recv)
    return (new.reshape(1, 2, ROWS, KV), anchor_new, momentum_new, pending)


def solution(mesh):
    return jax.shard_map(
        body,
        mesh=mesh,
        in_specs=(
            P(("worker", "fsdp")),
            P(None, ("worker", "fsdp"), None),
            P(None, ("worker", "fsdp"), None),
            P("worker", None, "fsdp", None),
            P(None, ("fsdp", "worker"), None),
            P(("fsdp", "worker"), None),
            P(),
        ),
        out_specs=(
            P("worker", None, "fsdp", None),
            P(("fsdp", "worker"), None),
            P(("fsdp", "worker"), None),
            P(("fsdp", "worker"), None),
        ),
        check_vma=False,
    )
```

```python
import jax
import jax.numpy as jnp
from jax import lax
from jax.experimental import pallas as pl
from jax.experimental.pallas import tpu as pltpu
from jax.sharding import PartitionSpec as P

inner_rate = 0.25
decay_rate = 0.1
outer_rate = 0.7
outer_beta = 0.9
mix_weight = 0.5

TOK = 256
KV = 512
ROWS = 1024
HALF = 512
QUARTER = 256
TAGS = ("s", "o")
F32 = jnp.float32
BF16 = jnp.bfloat16

HBM = pl.BlockSpec(memory_space=pltpu.HBM)
ANY = pl.BlockSpec(memory_space=pl.ANY)
VM = pl.BlockSpec(memory_space=pltpu.VMEM)
SM = pl.BlockSpec(memory_space=pltpu.SMEM)
MIB = 1024 * 1024
BIG = 24


def place():
    w = lax.axis_index("worker")
    f = lax.axis_index("fsdp")
    return w // 8, (w // 2) % 4, w % 2, f // 4, f % 4


def shape(*dims, dtype=BF16):
    return jax.ShapeDtypeStruct(dims, dtype)


def in_vmem(*dims):
    return pltpu.VMEM(dims, BF16)


def in_hbm(*dims):
    return pltpu.HBM(dims, BF16)


def pinned(value):
    return pltpu.with_memory_space_constraint(value, pltpu.HBM)


class Chain:
    def __init__(self):
        self.token = None


CHAIN = Chain()


def call(kernel, outs, args, specs, out_specs, scratch=(), aliases=None, name=None, vmem=16):
    outs, out_specs = list(outs), list(out_specs)
    tokens = [] if CHAIN.token is None else [CHAIN.token]
    count = len(args)

    def chained(*refs):
        rest = refs[count + len(tokens) :]
        kernel(*refs[:count], *rest[: len(outs)], *rest[len(outs) + 1 :])

    *results, CHAIN.token = pl.pallas_call(
        chained,
        out_shape=outs + [in_hbm(8, 128)],
        in_specs=list(specs) + [HBM] * len(tokens),
        out_specs=out_specs + [HBM],
        scratch_shapes=list(scratch),
        compiler_params=pltpu.CompilerParams(vmem_limit_bytes=vmem * MIB),
        cost_estimate=pl.CostEstimate(flops=0, bytes_accessed=0, transcendentals=0),
        input_output_aliases=aliases or {},
        name=name,
    )(*(pinned(a) if spec is HBM else a for a, spec in zip(args, specs)), *(pinned(t) for t in tokens))
    return results[0] if len(results) == 1 else results


def columns(start, width):
    return pl.ds(pl.multiple_of(start, width), width)


def pack(fragment, plan, tok, x, g):
    def kernel(plan_ref, tok_ref, x_ref, g_ref, a, b, c, gt_ref, gin, sems):
        _, _, _, z, y = place()
        s = lax.rem(plan_ref[0], 2)
        layer = s if fragment == 0 else 1 - s
        g_copy = pltpu.make_async_copy(g_ref.at[layer], gin, sems.at[12])
        g_copy.start()
        copies = []

        def send(zz, yy, offset, width, dst, at):
            col = pl.multiple_of((zz * 4 + yy) * ROWS + offset, QUARTER)
            copies.append(
                pltpu.make_async_copy(
                    x_ref.at[layer, :, pl.ds(col, width)], dst.at[:, pl.ds(at, width)], sems.at[len(copies)]
                )
            )
            copies[-1].start()

        for buf, first, offset in ((a, y ^ 1, HALF), (b, y ^ 3, HALF + QUARTER)):
            for i, (zz, yy) in enumerate(((1 - z, first), (z, first), (1 - z, y ^ 2), (z, y ^ 2))):
                send(zz, yy, offset, QUARTER, buf, i * QUARTER)
        for j in range(4):
            send(1 - z, y ^ j, 0, HALF, c, j * HALF)
        kept = (tok_ref[...] != 0).astype(F32)
        g_copy.wait()
        gt = (gin[...].astype(F32).T * kept).astype(BF16)
        gt_ref[...] = gt
        for buf, at in ((a, ROWS), (b, ROWS), (c, 4 * HALF)):
            for h in range(2):
                buf[:, at + h * TOK : at + (h + 1) * TOK] = gt[h * TOK : (h + 1) * TOK]
        for c in copies:
            c.wait()

    return call(
        kernel,
        (in_vmem(TOK, ROWS + KV), in_vmem(TOK, ROWS + KV), in_vmem(TOK, 4 * HALF + KV), in_vmem(KV, TOK)),
        (plan, tok, x, g),
        [SM, VM, HBM, HBM],
        [VM] * 4,
        [pltpu.VMEM((TOK, KV), BF16), pltpu.SemaphoreType.DMA((13,))],
        name="pack_" + TAGS[fragment],
        vmem=BIG,
    )


def product(name, fragment, pieces, width, out_shapes, g_at, plan, x, gt, recvs):
    count = len(pieces)
    number = len(recvs)
    total = sum(len(p[3]) for p in pieces)

    def kernel(plan_ref, x_ref, gt_ref, *rest):
        recv_refs = rest[:number]
        outs = rest[number : number + len(out_shapes)]
        stage = rest[number + len(out_shapes) : number + 2 * len(out_shapes)]
        gts, xs, sems, out_sems = rest[number + 2 * len(out_shapes) :]
        _, _, _, z, y = place()
        s = lax.rem(plan_ref[0], 2)
        layer = s if fragment == 0 else 1 - s
        g_copies = [
            pltpu.make_async_copy(gt_ref, gts.at[:, pl.ds(0, TOK)], sems.at[2 * count]),
            *(
                pltpu.make_async_copy(
                    recv_refs[0].at[:, pl.ds(g_at + h * TOK, TOK)],
                    gts.at[pl.ds(h * TOK, TOK), pl.ds(TOK, TOK)],
                    sems.at[2 * count + 1 + h],
                )
                for h in range(2)
            ),
        ]
        copies = []
        for p, (own, source, at, _) in enumerate(pieces):
            copies.append(
                (
                    pltpu.make_async_copy(
                        x_ref.at[layer, :, columns(own(z, y), width)], xs.at[p, pl.ds(0, TOK)], sems.at[2 * p]
                    ),
                    pltpu.make_async_copy(
                        recv_refs[source].at[:, pl.ds(at, width)], xs.at[p, pl.ds(TOK, TOK)], sems.at[2 * p + 1]
                    ),
                )
            )
        for c in g_copies:
            c.start()
        for pair in copies:
            for c in pair:
                c.start()
        for c in g_copies:
            c.wait()
        done = []
        for p, (_, _, _, targets) in enumerate(pieces):
            for c in copies[p]:
                c.wait()
            for out, slot, k0, k1 in targets:
                src = stage[out] if slot is None else stage[out].at[slot]
                dst = outs[out] if slot is None else outs[out].at[slot]
                src[...] = jnp.dot(gts[k0:k1], xs[p], preferred_element_type=F32).astype(BF16)
                c = pltpu.make_async_copy(src, dst, out_sems.at[len(done)])
                c.start()
                done.append(c)
        for c in done:
            c.wait()

    return call(
        kernel,
        tuple(shape(*d) for d in out_shapes),
        (plan, x, gt, *recvs),
        [SM, ANY, ANY] + [ANY] * number,
        [ANY] * len(out_shapes),
        [
            *(pltpu.VMEM(d, BF16) for d in out_shapes),
            pltpu.VMEM((KV, 2 * TOK), BF16),
            pltpu.VMEM((count, 2 * TOK, width), BF16),
            pltpu.SemaphoreType.DMA((2 * count + 3,)),
            pltpu.SemaphoreType.DMA((total,)),
        ],
        name=name,
        vmem=BIG,
    )


def flip(*terms):
    return sum(t.astype(F32) for t in terms).T


def stepped(w, gradient):
    return (w.astype(F32) * (1.0 - inner_rate * decay_rate) - inner_rate * gradient).astype(BF16)


WORKERS = (16, 2, 32, KV)


def inner_step(fragment, plan, w, first, second, third, fourth, across):
    def kernel(plan_ref, w_ref, *rest):
        k0, r0, l0, k1, r1, l1, ka, ra, kb, rb, z_ref, inner_ref, send_ref = rest[:13]
        wv, sems = rest[-2:]
        s = lax.rem(plan_ref[0], 2)
        layer = s if fragment == 0 else 1 - s
        core = place()[2]
        load = pltpu.make_async_copy(w_ref.at[layer], wv, sems.at[0])
        load.start()
        load.wait()
        for q in range(4):
            cols = pl.ds(q * 128, 128)
            halves = [flip(k[:, cols], r[0, :, cols], l[:, cols]) for k, r, l in ((k0, r0, l0), (k1, r1, l1))]
            put(inner_ref, wv, 2 * q, jnp.concatenate(halves, axis=1))
        for h, (k, r) in enumerate(((ka, ra), (kb, rb))):
            for q in range(2):
                cols = pl.ds(q * 128, 128)
                put(inner_ref, wv, 8 + 4 * h + 2 * q, flip(k[1, :, cols], r[1, :, cols], z_ref[h, :, cols]))
        copies = [pltpu.make_async_copy(inner_ref.at[:, 1 - core], send_ref, sems.at[1])]
        if fragment == 1:
            copies.append(pltpu.make_async_copy(inner_ref, rest[13].at[layer], sems.at[2]))
        for c in copies:
            c.start()
        for c in copies:
            c.wait()

    def put(inner_ref, wv, i, gradient):
        inner_ref[i : i + 2] = stepped(wv[i : i + 2].reshape(128, KV), gradient).reshape(2, 2, 32, KV)

    return call(
        kernel,
        (shape(*WORKERS), shape(16, 32, KV), shape(2, *WORKERS))[: 2 + fragment],
        (plan, w, *first, *second, *third, *fourth, across),
        [SM, HBM] + [VM] * 11,
        [VM, ANY, ANY][: 2 + fragment],
        [pltpu.VMEM(WORKERS, BF16), pltpu.SemaphoreType.DMA((3,))],
        name="inner_" + TAGS[fragment],
    )


def plus(a, b):
    return (a.astype(F32) + b.astype(F32)).astype(BF16)


def to_x(inner_ref, recv_ref, send_ref, keep_ref):
    x, _, core, _, _ = place()
    for ref, at, j in ((send_ref, 0, 1), (send_ref, 1, 2), (keep_ref, 0, 0), (keep_ref, 1, 3)):
        block = pl.ds((x ^ j) * 4, 4)
        ref[at] = plus(inner_ref[block, core], recv_ref[block])


def to_z(keep_ref, recv_ref, send_ref, stay_ref):
    zh = place()[1]
    for ref, at, j in ((send_ref, 0, 1), (send_ref, 1, 2), (stay_ref, 0, 0), (stay_ref, 1, 3)):
        ref[at] = plus(keep_ref[zh ^ j], recv_ref[zh ^ j])


QUAD = (4, 32, KV)


def sums(name, outs, pairs, extra=()):
    def kernel(*refs):
        out_refs = refs[2 * len(pairs) + len(extra) :]
        for i, (_, _, at_a, at_b, out, slot) in enumerate(pairs):
            a, b = refs[2 * i], refs[2 * i + 1]
            total = plus(a[...] if at_a is None else a[at_a], b[...] if at_b is None else b[at_b])
            if slot is None:
                out_refs[out][...] = total
            else:
                out_refs[out][slot] = total

    args = [t for p in pairs for t in p[:2]]
    return call(
        kernel,
        [shape(*d) for d in outs],
        (*args, *extra),
        [VM] * len(args) + [ANY] * len(extra),
        [VM] * len(outs),
        name=name,
    )


def halve(name, dims, keep, recv):
    return sums(name, [dims] * 2, [(keep, recv, 1, 1, 0, None), (keep, recv, 0, 0, 1, None)])


def join(a, b):
    def kernel(a_ref, b_ref, out_ref):
        out_ref[0] = a_ref[...]
        out_ref[1] = b_ref[...]

    return call(kernel, (shape(2, *a.shape),), (a, b), [VM] * 2, [VM], name="join")


def sum_x(inner, recv, name):
    return call(to_x, (shape(2, *QUAD),) * 2, (inner, recv), [VM] * 2, [VM] * 2, name=name)


def sum_z(keep, recv, name):
    return call(to_z, (shape(2, 32, KV),) * 2, (keep, recv), [VM] * 2, [VM] * 2, name=name)


def row_of(own, got):
    def kernel(own_ref, got_ref, out_ref):
        zh = place()[1]
        for ref, at, j in ((own_ref, 0, 0), (own_ref, 1, 1), (got_ref, 0, 3), (got_ref, 1, 2)):
            out_ref[zh ^ j] = ref[at]

    return call(kernel, (shape(*QUAD),), (own, got), [VM] * 2, [VM], name="row")


def block_of(own, got):
    def kernel(own_ref, got_ref, out_ref):
        x = place()[0]
        for ref, at, j in ((own_ref, 0, 0), (own_ref, 1, 3), (got_ref, 0, 1), (got_ref, 1, 2)):
            out_ref[pl.ds((x ^ j) * 4, 4)] = ref[at]

    return call(kernel, (shape(16, 32, KV),), (own, got), [VM] * 2, [VM], name="block")


def outer_sync(plan, anchors, momentum, keep, recv):
    def kernel(plan_ref, anchor_ref, momentum_ref, a, b, new_ref, moment_ref, short_ref):
        s = lax.rem(plan_ref[0], 2)
        mean = (a[...].astype(F32) + b[...].astype(F32)) / 32
        anchor = anchor_ref[s]
        outer_grad = anchor - mean
        moment = outer_beta * momentum_ref[...] + outer_grad
        new = anchor - outer_rate * (outer_grad + outer_beta * moment)
        new_ref[...] = new
        moment_ref[...] = moment
        short_ref[...] = new.astype(BF16)

    return call(
        kernel,
        (shape(32, KV, dtype=F32), shape(32, KV, dtype=F32), shape(32, KV)),
        (plan, anchors, momentum, keep, recv),
        [SM] + [VM] * 4,
        [VM] * 3,
        name="outer_sync",
    )


def outer_other(plan, anchors, keep, recv):
    def kernel(plan_ref, anchor_ref, a, b, out_ref):
        other = 1 - lax.rem(plan_ref[0], 2)
        out_ref[...] = anchor_ref[other] - (a[...].astype(F32) + b[...].astype(F32)) / 32

    return call(
        kernel,
        (shape(32, KV, dtype=F32),),
        (plan, anchors, keep, recv),
        [SM] + [VM] * 3,
        [VM],
        name="outer_other",
    )


def mix(plan, inner, own, recv, new):
    def kernel(plan_ref, inner_ref, own_ref, recv_ref, _, out_ref, stage, sems):
        s = lax.rem(plan_ref[0], 2)
        core = place()[2]
        for t, c in ((own_ref, core), (recv_ref, 1 - core)):
            stage[:, c] = (
                mix_weight * inner_ref[:, c].astype(F32) + (1.0 - mix_weight) * t[...].astype(F32)
            ).astype(BF16)
        out = pltpu.make_async_copy(stage, out_ref.at[s], sems)
        out.start()
        out.wait()

    return call(
        kernel,
        (shape(2, *WORKERS),),
        (plan, inner, own, recv, new),
        [SM, VM, VM, VM, ANY],
        [ANY],
        [pltpu.VMEM(WORKERS, BF16), pltpu.SemaphoreType.DMA],
        aliases={4: 0},
        name="mix",
    )


def along_fsdp(move):
    return [(z * 4 + y, move(z, y)) for z in range(2) for y in range(4)]


def along_worker(move):
    def index(x, z, c):
        return (x * 4 + z) * 2 + c

    return [(index(x, z, c), index(*move(x, z, c))) for x in range(4) for z in range(4) for c in range(2)]


MOVES = {
    "a": ("fsdp", along_fsdp(lambda z, y: z * 4 + (y ^ 1))),
    "b": ("fsdp", along_fsdp(lambda z, y: z * 4 + (y ^ 3))),
    "z": ("fsdp", along_fsdp(lambda z, y: (1 - z) * 4 + y)),
    "core": ("worker", along_worker(lambda x, z, c: (x, z, 1 - c))),
    "x1": ("worker", along_worker(lambda x, z, c: (x ^ 1, z, c))),
    "x3": ("worker", along_worker(lambda x, z, c: (x ^ 3, z, c))),
    "z1": ("worker", along_worker(lambda x, z, c: (x, z ^ 1, c))),
    "z3": ("worker", along_worker(lambda x, z, c: (x, z ^ 3, c))),
}


def swap(value, move):
    return lax.ppermute(value, *MOVES[move])


class Fragment:
    def __init__(self, index, plan, x, packed):
        self.index, self.plan, self.x = index, plan, x
        self.a, self.b, self.c, self.gt = packed

    def start_y(self):
        self.got_a, self.got_b = swap(self.a, "a"), swap(self.b, "b")

    def start_z(self):
        self.got_c = swap(self.c, "z")

    def make(self, name, pieces, width, outs, recv):
        name = name + "_" + TAGS[self.index]
        g_at = ROWS if width == QUARTER else 4 * HALF
        return product(name, self.index, pieces, width, outs, g_at, self.plan, self.x, self.gt, (recv,))

    def quarter(self, name, flip_y, offset, at, recv):
        pieces = [
            (
                lambda z, y, far=far: ((1 - z if far else z) * 4 + (y ^ flip_y)) * ROWS + offset,
                0,
                (at + i) * QUARTER,
                [(0, i, 0, KV)],
            )
            for i, far in enumerate((True, False))
        ]
        return self.make(name, pieces, QUARTER, [(2, KV, QUARTER)], recv)

    def quarters(self):
        self.next_a = swap(self.quarter("send_a", 3, HALF, 2, self.got_a), "b")
        self.next_b = swap(self.quarter("send_b", 1, HALF + QUARTER, 2, self.got_b), "a")
        self.keep_a = self.quarter("keep_a", 0, HALF, 0, self.got_a)
        self.keep_b = self.quarter("keep_b", 0, HALF + QUARTER, 0, self.got_b)

    def halves(self):
        lo, hi = (0, 256), (256, 512)
        one, two = (256, HALF), (2, 256, HALF)

        def dest(j, targets):
            return (lambda z, y: (z * 4 + (y ^ j)) * ROWS, 0, j * HALF, targets)

        send_0, send_1, self.stay_0, self.stay_1 = self.make(
            "halves",
            [
                dest(2, [(0, 1, *lo), (1, 1, *hi)]),
                dest(1, [(0, 0, *lo), (3, None, *hi)]),
                dest(3, [(1, 0, *hi), (2, None, *lo)]),
            ],
            HALF,
            [two, two, one, one],
            self.got_c,
        )
        self.got_0, self.got_1 = swap(send_0, "a"), swap(send_1, "b")
        self.mine_0, self.mine_1 = self.make(
            "mine", [dest(0, [(0, None, *lo), (1, None, *hi)])], HALF, [one, one], self.got_c
        )

    def far(self):
        pairs = [(self.keep_a, self.next_a, 0, 0, 0, 0), (self.keep_b, self.next_b, 0, 0, 0, 1)]
        self.across = swap(sums("far_" + TAGS[self.index], [(2, KV, QUARTER)], pairs), "z")

    def last(self, extra=()):
        pairs = [(self.stay_0, self.got_0, None, 1, 0, None), (self.stay_1, self.got_1, None, 1, 1, None)]
        last_0, last_1 = sums("last_" + TAGS[self.index], [(256, HALF)] * 2, pairs, extra)
        self.last_0, self.last_1 = swap(last_0, "b"), swap(last_1, "a")

    def inner(self, w):
        return inner_step(
            self.index,
            self.plan,
            w,
            (self.mine_0, self.got_0, self.last_0),
            (self.mine_1, self.got_1, self.last_1),
            (self.keep_a, self.next_a),
            (self.keep_b, self.next_b),
            self.across,
        )


def body(token_ids, layer_inputs, key_grads, weights, anchors, momentum, plan):
    CHAIN.token = None
    x = layer_inputs
    w = weights.reshape(2, *WORKERS)
    tok = token_ids.reshape(1, TOK)
    s = Fragment(0, plan, x, pack(0, plan, tok, x, key_grads))
    s.start_y()
    s.start_z()
    o = Fragment(1, plan, x, pack(1, plan, tok, x, key_grads))
    s.quarters()
    s.halves()
    s.far()
    o.start_z()
    s.last((s.across,))
    o.start_y()

    inner_s, send_s = s.inner(w)
    send, keep = sum_x(inner_s, swap(send_s, "core"), "sync_x1")
    recv = swap(send, "x1")
    o.quarters()
    send, keep = halve("sync_x3", QUAD, keep, recv)
    recv = swap(send, "x3")
    send, keep = sum_z(keep, recv, "sync_z1")
    recv = swap(send, "z1")
    o.halves()
    send, keep = halve("sync_z3", (32, KV), keep, recv)
    recv = swap(send, "z3")
    o.far()
    anchor_new, momentum_new, short = outer_sync(plan, anchors, momentum, keep, recv)
    short_far = swap(short, "z1")
    own = join(short, short_far)
    got = swap(own, "z3")
    o.last()
    row = row_of(own, got)
    row_far = swap(row, "x3")
    inner_o, send_o, new = o.inner(w)
    core_o = swap(send_o, "core")
    own = join(row, row_far)
    got = swap(own, "x1")
    send, keep = sum_x(inner_o, core_o, "other_x1")
    recv = swap(send, "x1")
    block = block_of(own, got)
    block_far = swap(block, "core")
    send, keep = halve("other_x3", QUAD, keep, recv)
    recv = swap(send, "x3")
    new = mix(plan, inner_s, block, block_far, new)
    send, keep = sum_z(keep, recv, "other_z1")
    recv = swap(send, "z1")
    send, keep = halve("other_z3", (32, KV), keep, recv)
    recv = swap(send, "z3")
    pending = outer_other(plan, anchors, keep, recv)
    return (new.reshape(1, 2, ROWS, KV), anchor_new, momentum_new, pending)


def solution(mesh):
    return jax.shard_map(
        body,
        mesh=mesh,
        in_specs=(
            P(("worker", "fsdp")),
            P(None, ("worker", "fsdp"), None),
            P(None, ("worker", "fsdp"), None),
            P("worker", None, "fsdp", None),
            P(None, ("fsdp", "worker"), None),
            P(("fsdp", "worker"), None),
            P(),
        ),
        out_specs=(
            P("worker", None, "fsdp", None),
            P(("fsdp", "worker"), None),
            P(("fsdp", "worker"), None),
            P(("fsdp", "worker"), None),
        ),
        check_vma=False,
    )
```

```python
import jax
import jax.numpy as jnp
from jax import lax
from jax.experimental import pallas as pl
from jax.experimental.pallas import tpu as pltpu
from jax.sharding import PartitionSpec as P

inner_rate = 0.25
decay_rate = 0.1
outer_rate = 0.7
outer_beta = 0.9
mix_weight = 0.5

TOK = 256
KV = 512
ROWS = 1024
HALF = 512
F32 = jnp.float32
BF16 = jnp.bfloat16

HBM = pl.BlockSpec(memory_space=pltpu.HBM)
ANY = pl.BlockSpec(memory_space=pl.ANY)
VM = pl.BlockSpec(memory_space=pltpu.VMEM)
SM = pl.BlockSpec(memory_space=pltpu.SMEM)
MIB = 1024 * 1024
BIG = 24


def place():
    w = lax.axis_index("worker")
    f = lax.axis_index("fsdp")
    return w // 8, (w // 2) % 4, w % 2, f // 4, f % 4


def shape(*dims, dtype=BF16):
    return jax.ShapeDtypeStruct(dims, dtype)


def in_vmem(*dims):
    return pltpu.VMEM(dims, BF16)


def in_hbm(*dims):
    return pltpu.HBM(dims, BF16)


def pinned(value):
    return pltpu.with_memory_space_constraint(value, pltpu.HBM)


class Chain:
    def __init__(self):
        self.token = None


CHAIN = Chain()


def call(kernel, outs, args, specs, out_specs, scratch=(), aliases=None, name=None, vmem=16, hint=0):
    outs, out_specs = list(outs), list(out_specs)
    tokens = [] if CHAIN.token is None else [CHAIN.token]
    count = len(args)

    def chained(*refs):
        rest = refs[count + len(tokens) :]
        kernel(*refs[:count], *rest[: len(outs)], *rest[len(outs) + 1 :])

    *results, CHAIN.token = pl.pallas_call(
        chained,
        out_shape=outs + [in_hbm(8, 128)],
        in_specs=list(specs) + [HBM] * len(tokens),
        out_specs=out_specs + [HBM],
        scratch_shapes=list(scratch),
        compiler_params=pltpu.CompilerParams(vmem_limit_bytes=vmem * MIB),
        cost_estimate=pl.CostEstimate(flops=hint, bytes_accessed=0, transcendentals=0),
        input_output_aliases=aliases or {},
        name=name,
    )(*(pinned(a) if spec is HBM else a for a, spec in zip(args, specs)), *(pinned(t) for t in tokens))
    return results[0] if len(results) == 1 else results


def columns(start, width):
    return pl.ds(pl.multiple_of(start, width), width)


def pack_kernel(plan, ids, x, g, a1, b1, z1, a2, b2, z3, gt_out, gin, gt, tok, sems, gsems):
    _, _, _, z, y = place()
    s = lax.rem(plan[0], 2)
    copies = []

    def send(layer, col, width, dst, at):
        copies.append(
            pltpu.make_async_copy(
                x.at[layer, :, columns(col, width)], dst.at[:, pl.ds(at, width)], sems.at[len(copies)]
            )
        )
        copies[-1].start()

    g_copies = [pltpu.make_async_copy(g.at[layer], gin.at[i], gsems.at[i]) for i, layer in enumerate((s, 1 - s))]
    ids_copy = pltpu.make_async_copy(ids, tok, gsems.at[9])
    for c in (*g_copies, ids_copy):
        c.start()
    for zz, bufs in ((1 - z, (a1, b1)), (z, (a2, b2))):
        for buf, first, offset in ((bufs[0], y ^ 1, 0), (bufs[1], y ^ 3, HALF)):
            for i, yy in enumerate((first, y ^ 2)):
                send(s, (zz * 4 + yy) * ROWS + offset, HALF, buf, i * HALF)
    for j, buf, at in ((1, z1, 0), (2, z1, ROWS), (3, z1, 2 * ROWS), (0, z3, 0)):
        send(1 - s, ((1 - z) * 4 + (y ^ j)) * ROWS, ROWS, buf, at)
    ids_copy.wait()
    kept = (tok[...] != 0).astype(F32)
    last = []

    def put(src, dst):
        last.append(pltpu.make_async_copy(src, dst, gsems.at[2 + len(last)]))
        last[-1].start()

    for i, bufs, at in ((0, (a1, b1), 2 * HALF), (1, (z1,), 3 * ROWS)):
        g_copies[i].wait()
        gt[i] = (gin[i].astype(F32).T * kept).astype(BF16)
        for buf in bufs:
            for h in range(2):
                put(gt.at[i, pl.ds(h * TOK, TOK)], buf.at[:, pl.ds(at + h * TOK, TOK)])
    put(gt, gt_out)
    for c in copies + last:
        c.wait()


def pack(plan, tok, x, g):
    wide = in_vmem(TOK, 2 * HALF + KV)
    half = in_vmem(TOK, 2 * HALF)
    return call(
        pack_kernel,
        (wide, wide, in_vmem(TOK, 3 * ROWS + KV), half, half, half, in_vmem(2, KV, TOK)),
        (plan, tok, x, g),
        [SM, HBM, HBM, HBM],
        [VM] * 7,
        [
            pltpu.VMEM((2, TOK, KV), BF16),
            pltpu.VMEM((2, KV, TOK), BF16),
            pltpu.VMEM((1, TOK), jnp.int32),
            pltpu.SemaphoreType.DMA((12,)),
            pltpu.SemaphoreType.DMA((10,)),
        ],
        name="pack",
        vmem=BIG,
    )


def product(name, fragment, pieces, width, out_shapes, g_at, plan, x, gt, recvs, hint=0):
    count = len(pieces)
    number = len(recvs)
    total = sum(len(p[3]) for p in pieces)

    def kernel(plan_ref, x_ref, gt_ref, *rest):
        recv_refs = rest[:number]
        outs = rest[number : number + len(out_shapes)]
        stage = rest[number + len(out_shapes) : number + 2 * len(out_shapes)]
        gts, xs, sems, out_sems = rest[number + 2 * len(out_shapes) :]
        _, _, _, z, y = place()
        s = lax.rem(plan_ref[0], 2)
        layer = s if fragment == 0 else 1 - s
        g_copies = [
            pltpu.make_async_copy(gt_ref.at[fragment], gts.at[:, pl.ds(0, TOK)], sems.at[2 * count]),
            *(
                pltpu.make_async_copy(
                    recv_refs[0].at[:, pl.ds(g_at + h * TOK, TOK)],
                    gts.at[pl.ds(h * TOK, TOK), pl.ds(TOK, TOK)],
                    sems.at[2 * count + 1 + h],
                )
                for h in range(2)
            ),
        ]
        copies = []
        for p, (own, source, at, _) in enumerate(pieces):
            copies.append(
                (
                    pltpu.make_async_copy(
                        x_ref.at[layer, :, columns(own(z, y), width)], xs.at[p, pl.ds(0, TOK)], sems.at[2 * p]
                    ),
                    pltpu.make_async_copy(
                        recv_refs[source].at[:, pl.ds(at, width)], xs.at[p, pl.ds(TOK, TOK)], sems.at[2 * p + 1]
                    ),
                )
            )
        for c in g_copies:
            c.start()
        for pair in copies:
            for c in pair:
                c.start()
        for c in g_copies:
            c.wait()
        done = []
        for p, (_, _, _, targets) in enumerate(pieces):
            for c in copies[p]:
                c.wait()
            for out, slot, k0, k1 in targets:
                src = stage[out] if slot is None else stage[out].at[slot]
                dst = outs[out] if slot is None else outs[out].at[slot]
                src[...] = jnp.dot(gts[k0:k1], xs[p], preferred_element_type=F32).astype(BF16)
                c = pltpu.make_async_copy(src, dst, out_sems.at[len(done)])
                c.start()
                done.append(c)
        for c in done:
            c.wait()

    return call(
        kernel,
        tuple(shape(*d) for d in out_shapes),
        (plan, x, gt, *recvs),
        [SM, ANY, ANY] + [ANY] * number,
        [ANY] * len(out_shapes),
        [
            *(pltpu.VMEM(d, BF16) for d in out_shapes),
            pltpu.VMEM((KV, 2 * TOK), BF16),
            pltpu.VMEM((count, 2 * TOK, width), BF16),
            pltpu.SemaphoreType.DMA((2 * count + 3,)),
            pltpu.SemaphoreType.DMA((total,)),
        ],
        name=name,
        vmem=BIG,
        hint=hint,
    )


def flip(*terms):
    return sum(t.astype(F32) for t in terms).T


def stepped(w, gradient):
    return (w.astype(F32) * (1.0 - inner_rate * decay_rate) - inner_rate * gradient).astype(BF16)


WORKERS = (16, 2, 32, KV)


def inner_sync(plan, w, near, across):
    def kernel(plan_ref, w_ref, near_ref, z_ref, inner_ref, send_ref, wv, sem, sem2):
        s = lax.rem(plan_ref[0], 2)
        core = place()[2]
        load = pltpu.make_async_copy(w_ref.at[s], wv, sem)
        load.start()
        load.wait()
        for h in range(2):
            for q in range(4):
                cols = pl.ds(q * 128, 128)
                i = h * 8 + q * 2
                gradient = flip(near_ref[h, :, cols], z_ref[h, :, cols])
                inner_ref[i : i + 2] = stepped(wv[i : i + 2].reshape(128, KV), gradient).reshape(2, 2, 32, KV)
        out = pltpu.make_async_copy(inner_ref.at[:, 1 - core], send_ref, sem2)
        out.start()
        out.wait()

    return call(
        kernel,
        (shape(*WORKERS), shape(16, 32, KV)),
        (plan, w, near, across),
        [SM, HBM] + [VM] * 2,
        [VM, ANY],
        [pltpu.VMEM(WORKERS, BF16), pltpu.SemaphoreType.DMA, pltpu.SemaphoreType.DMA],
        name="inner_sync",
    )


def inner_other(plan, w, first, second):
    def kernel(plan_ref, w_ref, *rest):
        k0, r0, l0, k1, r1, l1, inner_ref, send_ref, new_ref, wv, sem, sem2 = rest
        other = 1 - lax.rem(plan_ref[0], 2)
        core = place()[2]
        load = pltpu.make_async_copy(w_ref.at[other], wv, sem)
        load.start()
        load.wait()
        for q in range(8):
            cols = pl.ds(q * 128, 128)
            i = q * 2
            gradient = jnp.concatenate(
                [flip(k[:, cols], r[0, :, cols], l[:, cols]) for k, r, l in ((k0, r0, l0), (k1, r1, l1))], axis=1
            )
            inner_ref[i : i + 2] = stepped(wv[i : i + 2].reshape(128, KV), gradient).reshape(2, 2, 32, KV)
        out = pltpu.make_async_copy(inner_ref.at[:, 1 - core], send_ref, sem2.at[0])
        keep = pltpu.make_async_copy(inner_ref, new_ref.at[other], sem2.at[1])
        out.start()
        keep.start()
        out.wait()
        keep.wait()

    return call(
        kernel,
        (shape(*WORKERS), shape(16, 32, KV), shape(2, *WORKERS)),
        (plan, w, *first, *second),
        [SM, HBM] + [VM] * 6,
        [VM, ANY, ANY],
        [pltpu.VMEM(WORKERS, BF16), pltpu.SemaphoreType.DMA, pltpu.SemaphoreType.DMA((2,))],
        name="inner_other",
    )


def plus(a, b):
    return (a.astype(F32) + b.astype(F32)).astype(BF16)


def to_x(inner_ref, recv_ref, send_ref, keep_ref):
    x, _, core, _, _ = place()
    for ref, at, j in ((send_ref, 0, 1), (send_ref, 1, 2), (keep_ref, 0, 0), (keep_ref, 1, 3)):
        block = pl.ds((x ^ j) * 4, 4)
        ref[at] = plus(inner_ref[block, core], recv_ref[block])


def to_z(keep_ref, recv_ref, send_ref, stay_ref):
    zh = place()[1]
    for ref, at, j in ((send_ref, 0, 1), (send_ref, 1, 2), (stay_ref, 0, 0), (stay_ref, 1, 3)):
        ref[at] = plus(keep_ref[zh ^ j], recv_ref[zh ^ j])


QUAD = (4, 32, KV)


def sums(name, outs, pairs, extra=()):
    def kernel(*refs):
        out_refs = refs[2 * len(pairs) + len(extra) :]
        for i, (_, _, at_a, at_b, out, slot) in enumerate(pairs):
            a, b = refs[2 * i], refs[2 * i + 1]
            total = plus(a[...] if at_a is None else a[at_a], b[...] if at_b is None else b[at_b])
            if slot is None:
                out_refs[out][...] = total
            else:
                out_refs[out][slot] = total

    args = [t for p in pairs for t in p[:2]]
    return call(
        kernel,
        [shape(*d) for d in outs],
        (*args, *extra),
        [VM] * len(args) + [ANY] * len(extra),
        [VM] * len(outs),
        name=name,
    )


def halve(name, dims, keep, recv):
    return sums(name, [dims] * 2, [(keep, recv, 1, 1, 0, None), (keep, recv, 0, 0, 1, None)])


def join(a, b):
    def kernel(a_ref, b_ref, out_ref):
        out_ref[0] = a_ref[...]
        out_ref[1] = b_ref[...]

    return call(kernel, (shape(2, *a.shape),), (a, b), [VM] * 2, [VM], name="join")


def sum_x(inner, recv, name):
    return call(to_x, (shape(2, *QUAD),) * 2, (inner, recv), [VM] * 2, [VM] * 2, name=name)


def sum_z(keep, recv, name):
    return call(to_z, (shape(2, 32, KV),) * 2, (keep, recv), [VM] * 2, [VM] * 2, name=name)


def row_of(own, got):
    def kernel(own_ref, got_ref, out_ref):
        zh = place()[1]
        for ref, at, j in ((own_ref, 0, 0), (own_ref, 1, 1), (got_ref, 0, 3), (got_ref, 1, 2)):
            out_ref[zh ^ j] = ref[at]

    return call(kernel, (shape(*QUAD),), (own, got), [VM] * 2, [VM], name="row")


def block_of(own, got):
    def kernel(own_ref, got_ref, out_ref):
        x = place()[0]
        for ref, at, j in ((own_ref, 0, 0), (own_ref, 1, 3), (got_ref, 0, 1), (got_ref, 1, 2)):
            out_ref[pl.ds((x ^ j) * 4, 4)] = ref[at]

    return call(kernel, (shape(16, 32, KV),), (own, got), [VM] * 2, [VM], name="block")


def ahead(plan, anchors, momentum):
    def kernel(plan_ref, anchor_ref, momentum_ref, out_ref):
        anchor = anchor_ref[lax.rem(plan_ref[0], 2)]
        out_ref[...] = (
            (1.0 - outer_rate * (1.0 + outer_beta)) * anchor - outer_rate * outer_beta**2 * momentum_ref[...]
        ).astype(BF16)

    return call(kernel, (shape(32, KV),), (plan, anchors, momentum), [SM] + [VM] * 2, [VM], name="ahead")


def new_rows(known, keep, recv):
    def kernel(known_ref, a, b, out_ref):
        mean = (a[...].astype(F32) + b[...].astype(F32)) / 32
        out_ref[...] = (known_ref[...].astype(F32) + outer_rate * (1.0 + outer_beta) * mean).astype(BF16)

    return call(kernel, (shape(*QUAD),), (known, keep, recv), [VM] * 3, [VM], name="new_rows")


def outer_sync(plan, anchors, momentum, keep, recv):
    def kernel(plan_ref, anchor_ref, momentum_ref, a, b, new_ref, moment_ref):
        s = lax.rem(plan_ref[0], 2)
        zh = place()[1]
        mean = (a[zh].astype(F32) + b[zh].astype(F32)) / 32
        anchor = anchor_ref[s]
        outer_grad = anchor - mean
        moment = outer_beta * momentum_ref[...] + outer_grad
        new_ref[...] = anchor - outer_rate * (outer_grad + outer_beta * moment)
        moment_ref[...] = moment

    return call(
        kernel,
        (shape(32, KV, dtype=F32), shape(32, KV, dtype=F32)),
        (plan, anchors, momentum, keep, recv),
        [SM] + [VM] * 4,
        [VM] * 2,
        name="outer_sync",
    )


def outer_other(plan, anchors, keep, recv):
    def kernel(plan_ref, anchor_ref, a, b, out_ref):
        other = 1 - lax.rem(plan_ref[0], 2)
        out_ref[...] = anchor_ref[other] - (a[...].astype(F32) + b[...].astype(F32)) / 32

    return call(
        kernel,
        (shape(32, KV, dtype=F32),),
        (plan, anchors, keep, recv),
        [SM] + [VM] * 3,
        [VM],
        name="outer_other",
    )


def mix(plan, inner, own, recv, new):
    def kernel(plan_ref, inner_ref, own_ref, recv_ref, _, out_ref, stage, sems):
        s = lax.rem(plan_ref[0], 2)
        core = place()[2]
        for t, c in ((own_ref, core), (recv_ref, 1 - core)):
            stage[:, c] = (
                mix_weight * inner_ref[:, c].astype(F32) + (1.0 - mix_weight) * t[...].astype(F32)
            ).astype(BF16)
        out = pltpu.make_async_copy(stage, out_ref.at[s], sems)
        out.start()
        out.wait()

    return call(
        kernel,
        (shape(2, *WORKERS),),
        (plan, inner, own, recv, new),
        [SM, VM, VM, VM, ANY],
        [ANY],
        [pltpu.VMEM(WORKERS, BF16), pltpu.SemaphoreType.DMA],
        aliases={4: 0},
        name="mix",
    )


def along_fsdp(move):
    return [(z * 4 + y, move(z, y)) for z in range(2) for y in range(4)]


def along_worker(move):
    def index(x, z, c):
        return (x * 4 + z) * 2 + c

    return [(index(x, z, c), index(*move(x, z, c))) for x in range(4) for z in range(4) for c in range(2)]


MOVES = {
    "a": ("fsdp", along_fsdp(lambda z, y: z * 4 + (y ^ 1))),
    "b": ("fsdp", along_fsdp(lambda z, y: z * 4 + (y ^ 3))),
    "z": ("fsdp", along_fsdp(lambda z, y: (1 - z) * 4 + y)),
    "core": ("worker", along_worker(lambda x, z, c: (x, z, 1 - c))),
    "x1": ("worker", along_worker(lambda x, z, c: (x ^ 1, z, c))),
    "x3": ("worker", along_worker(lambda x, z, c: (x ^ 3, z, c))),
    "z1": ("worker", along_worker(lambda x, z, c: (x, z ^ 1, c))),
    "z3": ("worker", along_worker(lambda x, z, c: (x, z ^ 3, c))),
}


def swap(value, move):
    return lax.ppermute(value, *MOVES[move])


def body(token_ids, layer_inputs, key_grads, weights, anchors, momentum, plan):
    CHAIN.token = None
    x = layer_inputs
    w = weights.reshape(2, *WORKERS)
    a1, b1, z1, a2, b2, z3, gt = pack(plan, token_ids.reshape(1, TOK), x, key_grads)
    got_a1 = swap(a1, "a")
    got_b1 = swap(b1, "b")
    got_z1 = swap(z1, "z")
    got_a2 = swap(a2, "a")
    got_b2 = swap(b2, "b")
    got_z3 = swap(z3, "z")

    def tile(name, far, flip_y, offset, at, recvs):
        piece = (
            lambda z, y: ((1 - z if far else z) * 4 + (y ^ flip_y)) * ROWS + offset,
            len(recvs) - 1,
            at * HALF,
            [(0, None, 0, KV)],
        )
        return product(name, 0, [piece], HALF, [(KV, HALF)], 2 * HALF, plan, x, gt, recvs)

    def dest(j, source, at, targets):
        return (lambda z, y: (z * 4 + (y ^ j)) * ROWS, source, at, targets)

    def other(name, pieces, outs, recvs, hint=0):
        return product(name, 1, pieces, ROWS, outs, 3 * ROWS, plan, x, gt, recvs, hint)

    lo, hi = (0, 256), (256, 512)
    half, pair = (256, ROWS), (2, 256, ROWS)

    far_a = swap(tile("send_a1", True, 3, 0, 1, (got_a1,)), "b")
    far_b = swap(tile("send_b1", True, 1, HALF, 1, (got_b1,)), "a")
    keep_a1 = tile("keep_a1", True, 0, 0, 0, (got_a1,))
    keep_b1 = tile("keep_b1", True, 0, HALF, 0, (got_b1,))
    near_a = swap(tile("send_a2", False, 3, 0, 1, (got_a1, got_a2)), "b")
    near_b = swap(tile("send_b2", False, 1, HALF, 1, (got_b1, got_b2)), "a")
    keep_a2 = tile("keep_a2", False, 0, 0, 0, (got_a1, got_a2))
    keep_b2 = tile("keep_b2", False, 0, HALF, 0, (got_b1, got_b2))
    across = swap(
        sums("far", [(2, KV, HALF)], [(keep_a1, far_a, None, None, 0, 0), (keep_b1, far_b, None, None, 0, 1)]), "z"
    )
    send_0, send_1, stay_0, stay_1 = other(
        "other_1",
        [
            dest(2, 0, ROWS, [(0, 1, *lo), (1, 1, *hi)]),
            dest(1, 0, 0, [(0, 0, *lo), (3, None, *hi)]),
            dest(3, 0, 2 * ROWS, [(1, 0, *hi), (2, None, *lo)]),
        ],
        [pair, pair, half, half],
        (got_z1,),
        10**10,
    )
    got_0, got_1 = swap(send_0, "a"), swap(send_1, "b")
    near = sums("near", [(2, KV, HALF)], [(keep_a2, near_a, None, None, 0, 0), (keep_b2, near_b, None, None, 0, 1)])
    known = ahead(plan, anchors, momentum)
    known = join(known, swap(known, "z1"))
    known = row_of(known, swap(known, "z3"))

    inner_s, send_s = inner_sync(plan, w, near, across)
    send, keep = sum_x(inner_s, swap(send_s, "core"), "sync_x1")
    recv = swap(send, "x1")
    send, keep = halve("sync_x3", QUAD, keep, recv)
    last_0, last_1 = sums(
        "last", [half, half], [(stay_0, got_0, None, 1, 0, None), (stay_1, got_1, None, 1, 1, None)]
    )
    last_0, last_1 = swap(last_0, "b"), swap(last_1, "a")
    keep = sums("sync_z1", [QUAD], [(keep, swap(send, "x3"), None, None, 0, None)])
    recv = swap(keep, "z1")
    mine_0, mine_1 = other("other_3", [dest(0, 1, 0, [(0, None, *lo), (1, None, *hi)])], [half, half], (got_z1, got_z3))
    keep = sums("sync_z3", [QUAD], [(keep, recv, None, None, 0, None)])
    recv = swap(keep, "z3")
    row = new_rows(known, keep, recv)
    row_far = swap(row, "x3")
    anchor_new, momentum_new = outer_sync(plan, anchors, momentum, keep, recv)

    own = join(row, row_far)
    got = swap(own, "x1")
    inner_o, send_o, new = inner_other(plan, w, (mine_0, got_0, last_0), (mine_1, got_1, last_1))
    core_o = swap(send_o, "core")
    send, keep = sum_x(inner_o, core_o, "other_x1")
    recv = swap(send, "x1")
    block = block_of(own, got)
    block_far = swap(block, "core")
    send, keep = halve("other_x3", QUAD, keep, recv)
    recv = swap(send, "x3")
    new = mix(plan, inner_s, block, block_far, new)
    send, keep = sum_z(keep, recv, "other_z1")
    recv = swap(send, "z1")
    send, keep = halve("other_z3", (32, KV), keep, recv)
    recv = swap(send, "z3")
    pending = outer_other(plan, anchors, keep, recv)
    return (new.reshape(1, 2, ROWS, KV), anchor_new, momentum_new, pending)


def solution(mesh):
    return jax.shard_map(
        body,
        mesh=mesh,
        in_specs=(
            P(("worker", "fsdp")),
            P(None, ("worker", "fsdp"), None),
            P(None, ("worker", "fsdp"), None),
            P("worker", None, "fsdp", None),
            P(None, ("fsdp", "worker"), None),
            P(("fsdp", "worker"), None),
            P(),
        ),
        out_specs=(
            P("worker", None, "fsdp", None),
            P(("fsdp", "worker"), None),
            P(("fsdp", "worker"), None),
            P(("fsdp", "worker"), None),
        ),
        check_vma=False,
    )
```

```python
import jax
import jax.numpy as jnp
from jax import lax
from jax.experimental import pallas as pl
from jax.experimental.pallas import tpu as pltpu
from jax.sharding import PartitionSpec as P

inner_rate = 0.25
decay_rate = 0.1
outer_rate = 0.7
outer_beta = 0.9
mix_weight = 0.5

TOK = 256
KV = 512
ROWS = 1024
HALF = 512
F32 = jnp.float32
BF16 = jnp.bfloat16

HBM = pl.BlockSpec(memory_space=pltpu.HBM)
ANY = pl.BlockSpec(memory_space=pl.ANY)
VM = pl.BlockSpec(memory_space=pltpu.VMEM)
SM = pl.BlockSpec(memory_space=pltpu.SMEM)
MIB = 1024 * 1024
BIG = 24


def place():
    w = lax.axis_index("worker")
    f = lax.axis_index("fsdp")
    return w // 8, (w // 2) % 4, w % 2, f // 4, f % 4


def shape(*dims, dtype=BF16):
    return jax.ShapeDtypeStruct(dims, dtype)


def in_vmem(*dims):
    return pltpu.VMEM(dims, BF16)


def in_hbm(*dims):
    return pltpu.HBM(dims, BF16)


def pinned(value):
    return pltpu.with_memory_space_constraint(value, pltpu.HBM)


class Chain:
    def __init__(self):
        self.token = None


CHAIN = Chain()


def call(kernel, outs, args, specs, out_specs, scratch=(), aliases=None, name=None, vmem=16, hint=0):
    outs, out_specs = list(outs), list(out_specs)
    tokens = [] if CHAIN.token is None else [CHAIN.token]
    count = len(args)

    def chained(*refs):
        rest = refs[count + len(tokens) :]
        kernel(*refs[:count], *rest[: len(outs)], *rest[len(outs) + 1 :])

    *results, CHAIN.token = pl.pallas_call(
        chained,
        out_shape=outs + [in_hbm(8, 128)],
        in_specs=list(specs) + [HBM] * len(tokens),
        out_specs=out_specs + [HBM],
        scratch_shapes=list(scratch),
        compiler_params=pltpu.CompilerParams(vmem_limit_bytes=vmem * MIB),
        cost_estimate=pl.CostEstimate(flops=hint, bytes_accessed=0, transcendentals=0),
        input_output_aliases=aliases or {},
        name=name,
    )(*(pinned(a) if spec is HBM else a for a, spec in zip(args, specs)), *(pinned(t) for t in tokens))
    return results[0] if len(results) == 1 else results


def columns(start, width):
    return pl.ds(pl.multiple_of(start, width), width)


def pack_kernel(plan, ids, x, g, a1, b1, z1, a2, b2, z3, gt_out, gin, gt, tok, sems, gsems):
    _, _, _, z, y = place()
    s = lax.rem(plan[0], 2)
    copies = []

    def send(layer, col, width, dst, at):
        copies.append(
            pltpu.make_async_copy(
                x.at[layer, :, columns(col, width)], dst.at[:, pl.ds(at, width)], sems.at[len(copies)]
            )
        )
        copies[-1].start()

    g_copies = [pltpu.make_async_copy(g.at[layer], gin.at[i], gsems.at[i]) for i, layer in enumerate((s, 1 - s))]
    ids_copy = pltpu.make_async_copy(ids, tok, gsems.at[9])
    for c in (*g_copies, ids_copy):
        c.start()
    for zz, bufs in ((1 - z, (a1, b1)), (z, (a2, b2))):
        for buf, first, offset in ((bufs[0], y ^ 1, 0), (bufs[1], y ^ 3, HALF)):
            for i, yy in enumerate((first, y ^ 2)):
                send(s, (zz * 4 + yy) * ROWS + offset, HALF, buf, i * HALF)
    for j, buf, at in ((1, z1, 0), (2, z1, ROWS), (3, z1, 2 * ROWS), (0, z3, 0)):
        send(1 - s, ((1 - z) * 4 + (y ^ j)) * ROWS, ROWS, buf, at)
    ids_copy.wait()
    kept = (tok[...] != 0).astype(F32)
    last = []

    def put(src, dst):
        last.append(pltpu.make_async_copy(src, dst, gsems.at[2 + len(last)]))
        last[-1].start()

    for i, bufs, at in ((0, (a1, b1), 2 * HALF), (1, (z1,), 3 * ROWS)):
        g_copies[i].wait()
        gt[i] = (gin[i].astype(F32).T * kept).astype(BF16)
        for buf in bufs:
            for h in range(2):
                put(gt.at[i, pl.ds(h * TOK, TOK)], buf.at[:, pl.ds(at + h * TOK, TOK)])
    put(gt, gt_out)
    for c in copies + last:
        c.wait()


def pack(plan, tok, x, g):
    wide = in_vmem(TOK, 2 * HALF + KV)
    half = in_vmem(TOK, 2 * HALF)
    return call(
        pack_kernel,
        (wide, wide, in_vmem(TOK, 3 * ROWS + KV), half, half, half, in_vmem(2, KV, TOK)),
        (plan, tok, x, g),
        [SM, HBM, HBM, HBM],
        [VM] * 7,
        [
            pltpu.VMEM((2, TOK, KV), BF16),
            pltpu.VMEM((2, KV, TOK), BF16),
            pltpu.VMEM((1, TOK), jnp.int32),
            pltpu.SemaphoreType.DMA((12,)),
            pltpu.SemaphoreType.DMA((10,)),
        ],
        name="pack",
        vmem=BIG,
    )


def product(name, fragment, pieces, width, out_shapes, g_at, plan, x, gt, recvs, hint=0):
    count = len(pieces)
    number = len(recvs)
    total = sum(len(p[3]) for p in pieces)

    def kernel(plan_ref, x_ref, gt_ref, *rest):
        recv_refs = rest[:number]
        outs = rest[number : number + len(out_shapes)]
        stage = rest[number + len(out_shapes) : number + 2 * len(out_shapes)]
        gts, xs, sems, out_sems = rest[number + 2 * len(out_shapes) :]
        _, _, _, z, y = place()
        s = lax.rem(plan_ref[0], 2)
        layer = s if fragment == 0 else 1 - s
        g_copies = [
            pltpu.make_async_copy(gt_ref.at[fragment], gts.at[:, pl.ds(0, TOK)], sems.at[2 * count]),
            *(
                pltpu.make_async_copy(
                    recv_refs[0].at[:, pl.ds(g_at + h * TOK, TOK)],
                    gts.at[pl.ds(h * TOK, TOK), pl.ds(TOK, TOK)],
                    sems.at[2 * count + 1 + h],
                )
                for h in range(2)
            ),
        ]
        copies = []
        for p, (own, source, at, _) in enumerate(pieces):
            copies.append(
                (
                    pltpu.make_async_copy(
                        x_ref.at[layer, :, columns(own(z, y), width)], xs.at[p, pl.ds(0, TOK)], sems.at[2 * p]
                    ),
                    pltpu.make_async_copy(
                        recv_refs[source].at[:, pl.ds(at, width)], xs.at[p, pl.ds(TOK, TOK)], sems.at[2 * p + 1]
                    ),
                )
            )
        for c in g_copies:
            c.start()
        for pair in copies:
            for c in pair:
                c.start()
        for c in g_copies:
            c.wait()
        done = []
        for p, (_, _, _, targets) in enumerate(pieces):
            for c in copies[p]:
                c.wait()
            for out, slot, k0, k1 in targets:
                src = stage[out] if slot is None else stage[out].at[slot]
                dst = outs[out] if slot is None else outs[out].at[slot]
                src[...] = jnp.dot(gts[k0:k1], xs[p], preferred_element_type=F32).astype(BF16)
                c = pltpu.make_async_copy(src, dst, out_sems.at[len(done)])
                c.start()
                done.append(c)
        for c in done:
            c.wait()

    return call(
        kernel,
        tuple(shape(*d) for d in out_shapes),
        (plan, x, gt, *recvs),
        [SM, ANY, ANY] + [ANY] * number,
        [ANY] * len(out_shapes),
        [
            *(pltpu.VMEM(d, BF16) for d in out_shapes),
            pltpu.VMEM((KV, 2 * TOK), BF16),
            pltpu.VMEM((count, 2 * TOK, width), BF16),
            pltpu.SemaphoreType.DMA((2 * count + 3,)),
            pltpu.SemaphoreType.DMA((total,)),
        ],
        name=name,
        vmem=BIG,
        hint=hint,
    )


def flip(*terms):
    return sum(t.astype(F32) for t in terms).T


def stepped(w, gradient):
    return (w.astype(F32) * (1.0 - inner_rate * decay_rate) - inner_rate * gradient).astype(BF16)


WORKERS = (16, 2, 32, KV)


def inner_sync(plan, w, near, across):
    def kernel(plan_ref, w_ref, near_ref, z_ref, inner_ref, send_ref, wv, sem, sem2):
        s = lax.rem(plan_ref[0], 2)
        core = place()[2]
        load = pltpu.make_async_copy(w_ref.at[s], wv, sem)
        load.start()
        load.wait()
        for h in range(2):
            for q in range(4):
                cols = pl.ds(q * 128, 128)
                i = h * 8 + q * 2
                gradient = flip(near_ref[h, :, cols], z_ref[h, :, cols])
                inner_ref[i : i + 2] = stepped(wv[i : i + 2].reshape(128, KV), gradient).reshape(2, 2, 32, KV)
        out = pltpu.make_async_copy(inner_ref.at[:, 1 - core], send_ref, sem2)
        out.start()
        out.wait()

    return call(
        kernel,
        (shape(*WORKERS), shape(16, 32, KV)),
        (plan, w, near, across),
        [SM, HBM] + [VM] * 2,
        [VM, ANY],
        [pltpu.VMEM(WORKERS, BF16), pltpu.SemaphoreType.DMA, pltpu.SemaphoreType.DMA],
        name="inner_sync",
    )


def inner_other(plan, w, first, second):
    def kernel(plan_ref, w_ref, *rest):
        k0, r0, l0, k1, r1, l1, inner_ref, send_ref, new_ref, wv, sem, sem2 = rest
        other = 1 - lax.rem(plan_ref[0], 2)
        core = place()[2]
        load = pltpu.make_async_copy(w_ref.at[other], wv, sem)
        load.start()
        load.wait()
        for q in range(8):
            cols = pl.ds(q * 128, 128)
            i = q * 2
            gradient = jnp.concatenate(
                [flip(k[:, cols], r[0, :, cols], l[:, cols]) for k, r, l in ((k0, r0, l0), (k1, r1, l1))], axis=1
            )
            inner_ref[i : i + 2] = stepped(wv[i : i + 2].reshape(128, KV), gradient).reshape(2, 2, 32, KV)
        out = pltpu.make_async_copy(inner_ref.at[:, 1 - core], send_ref, sem2.at[0])
        keep = pltpu.make_async_copy(inner_ref, new_ref.at[other], sem2.at[1])
        out.start()
        keep.start()
        out.wait()
        keep.wait()

    return call(
        kernel,
        (shape(*WORKERS), shape(16, 32, KV), shape(2, *WORKERS)),
        (plan, w, *first, *second),
        [SM, HBM] + [VM] * 6,
        [VM, ANY, ANY],
        [pltpu.VMEM(WORKERS, BF16), pltpu.SemaphoreType.DMA, pltpu.SemaphoreType.DMA((2,))],
        name="inner_other",
    )


def plus(a, b):
    return (a.astype(F32) + b.astype(F32)).astype(BF16)


def to_x(inner_ref, recv_ref, send_ref, keep_ref):
    x, _, core, _, _ = place()
    for ref, at, j in ((send_ref, 0, 1), (send_ref, 1, 2), (keep_ref, 0, 0), (keep_ref, 1, 3)):
        block = pl.ds((x ^ j) * 4, 4)
        ref[at] = plus(inner_ref[block, core], recv_ref[block])


QUAD = (4, 32, KV)


def sums(name, outs, pairs, extra=()):
    def kernel(*refs):
        out_refs = refs[2 * len(pairs) + len(extra) :]
        for i, (_, _, at_a, at_b, out, slot) in enumerate(pairs):
            a, b = refs[2 * i], refs[2 * i + 1]
            total = plus(a[...] if at_a is None else a[at_a], b[...] if at_b is None else b[at_b])
            if slot is None:
                out_refs[out][...] = total
            else:
                out_refs[out][slot] = total

    args = [t for p in pairs for t in p[:2]]
    return call(
        kernel,
        [shape(*d) for d in outs],
        (*args, *extra),
        [VM] * len(args) + [ANY] * len(extra),
        [VM] * len(outs),
        name=name,
    )


def halve(name, dims, keep, recv):
    return sums(name, [dims] * 2, [(keep, recv, 1, 1, 0, None), (keep, recv, 0, 0, 1, None)])


def sum_x(inner, recv, name):
    return call(to_x, (shape(2, *QUAD),) * 2, (inner, recv), [VM] * 2, [VM] * 2, name=name)


def spread_x(inner, recv, name):
    def kernel(inner_ref, recv_ref, *outs):
        x, _, core, _, _ = place()
        for j in range(4):
            block = pl.ds((x ^ j) * 4, 4)
            outs[j][...] = plus(inner_ref[block, core], recv_ref[block])

    return call(kernel, (shape(*QUAD),) * 4, (inner, recv), [VM] * 2, [VM] * 4, name=name)


def spread_z(parts, name):
    def kernel(*refs):
        zh = place()[1]
        terms, outs = refs[: len(parts)], refs[len(parts) :]
        for j in range(4):
            outs[j][...] = sum(t[zh ^ j].astype(F32) for t in terms).astype(BF16)

    return call(kernel, (shape(32, KV),) * 4, parts, [VM] * len(parts), [VM] * 4, name=name)


def row_of(parts):
    def kernel(*refs):
        zh = place()[1]
        for j in range(4):
            refs[4][zh ^ j] = refs[j][...]

    return call(kernel, (shape(*QUAD),), parts, [VM] * 4, [VM], name="row")


def block_of(parts):
    def kernel(*refs):
        x = place()[0]
        for j in range(4):
            refs[4][pl.ds((x ^ j) * 4, 4)] = refs[j][...]

    return call(kernel, (shape(16, 32, KV),), parts, [VM] * 4, [VM], name="block")


def total(*refs):
    return sum(r[...].astype(F32) for r in refs)


def outer_sync(plan, anchors, momentum, parts):
    def kernel(plan_ref, anchor_ref, momentum_ref, a, b, c, d, new_ref, moment_ref, short_ref):
        s = lax.rem(plan_ref[0], 2)
        mean = total(a, b, c, d) / 32
        anchor = anchor_ref[s]
        outer_grad = anchor - mean
        moment = outer_beta * momentum_ref[...] + outer_grad
        new = anchor - outer_rate * (outer_grad + outer_beta * moment)
        new_ref[...] = new
        moment_ref[...] = moment
        short_ref[...] = new.astype(BF16)

    return call(
        kernel,
        (shape(32, KV, dtype=F32), shape(32, KV, dtype=F32), shape(32, KV)),
        (plan, anchors, momentum, *parts),
        [SM] + [VM] * 6,
        [VM] * 3,
        name="outer_sync",
    )


def outer_other(plan, anchors, parts):
    def kernel(plan_ref, anchor_ref, a, b, c, d, out_ref):
        other = 1 - lax.rem(plan_ref[0], 2)
        out_ref[...] = anchor_ref[other] - total(a, b, c, d) / 32

    return call(
        kernel,
        (shape(32, KV, dtype=F32),),
        (plan, anchors, *parts),
        [SM] + [VM] * 5,
        [VM],
        name="outer_other",
    )


def mix(plan, inner, own, recv, new):
    def kernel(plan_ref, inner_ref, own_ref, recv_ref, _, out_ref, stage, sems):
        s = lax.rem(plan_ref[0], 2)
        core = place()[2]
        for t, c in ((own_ref, core), (recv_ref, 1 - core)):
            stage[:, c] = (
                mix_weight * inner_ref[:, c].astype(F32) + (1.0 - mix_weight) * t[...].astype(F32)
            ).astype(BF16)
        out = pltpu.make_async_copy(stage, out_ref.at[s], sems)
        out.start()
        out.wait()

    return call(
        kernel,
        (shape(2, *WORKERS),),
        (plan, inner, own, recv, new),
        [SM, VM, VM, VM, ANY],
        [ANY],
        [pltpu.VMEM(WORKERS, BF16), pltpu.SemaphoreType.DMA],
        aliases={4: 0},
        name="mix",
    )


def along_fsdp(move):
    return [(z * 4 + y, move(z, y)) for z in range(2) for y in range(4)]


def along_worker(move):
    def index(x, z, c):
        return (x * 4 + z) * 2 + c

    return [(index(x, z, c), index(*move(x, z, c))) for x in range(4) for z in range(4) for c in range(2)]


MOVES = {
    "a": ("fsdp", along_fsdp(lambda z, y: z * 4 + (y ^ 1))),
    "b": ("fsdp", along_fsdp(lambda z, y: z * 4 + (y ^ 3))),
    "z": ("fsdp", along_fsdp(lambda z, y: (1 - z) * 4 + y)),
    "core": ("worker", along_worker(lambda x, z, c: (x, z, 1 - c))),
    "x1": ("worker", along_worker(lambda x, z, c: (x ^ 1, z, c))),
    "x2": ("worker", along_worker(lambda x, z, c: (x ^ 2, z, c))),
    "x3": ("worker", along_worker(lambda x, z, c: (x ^ 3, z, c))),
    "z1": ("worker", along_worker(lambda x, z, c: (x, z ^ 1, c))),
    "z2": ("worker", along_worker(lambda x, z, c: (x, z ^ 2, c))),
    "z3": ("worker", along_worker(lambda x, z, c: (x, z ^ 3, c))),
}


def swap(value, move):
    return lax.ppermute(value, *MOVES[move])


def shared(value, axis):
    return (value, *(swap(value, axis + j) for j in "123"))


def dealt(parts, axis):
    return (parts[0], *(swap(parts[j], axis + str(j)) for j in (1, 2, 3)))


def body(token_ids, layer_inputs, key_grads, weights, anchors, momentum, plan):
    CHAIN.token = None
    x = layer_inputs
    w = weights.reshape(2, *WORKERS)
    a1, b1, z1, a2, b2, z3, gt = pack(plan, token_ids.reshape(1, TOK), x, key_grads)
    got_a1 = swap(a1, "a")
    got_b1 = swap(b1, "b")
    got_z1 = swap(z1, "z")
    got_a2 = swap(a2, "a")
    got_b2 = swap(b2, "b")
    got_z3 = swap(z3, "z")

    def tile(name, far, flip_y, offset, at, recvs):
        piece = (
            lambda z, y: ((1 - z if far else z) * 4 + (y ^ flip_y)) * ROWS + offset,
            len(recvs) - 1,
            at * HALF,
            [(0, None, 0, KV)],
        )
        return product(name, 0, [piece], HALF, [(KV, HALF)], 2 * HALF, plan, x, gt, recvs)

    def dest(j, source, at, targets):
        return (lambda z, y: (z * 4 + (y ^ j)) * ROWS, source, at, targets)

    def other(name, pieces, outs, recvs, hint=0):
        return product(name, 1, pieces, ROWS, outs, 3 * ROWS, plan, x, gt, recvs, hint)

    lo, hi = (0, 256), (256, 512)
    half, pair = (256, ROWS), (2, 256, ROWS)

    far_a = swap(tile("send_a1", True, 3, 0, 1, (got_a1,)), "b")
    far_b = swap(tile("send_b1", True, 1, HALF, 1, (got_b1,)), "a")
    keep_a1 = tile("keep_a1", True, 0, 0, 0, (got_a1,))
    keep_b1 = tile("keep_b1", True, 0, HALF, 0, (got_b1,))
    near_a = swap(tile("send_a2", False, 3, 0, 1, (got_a1, got_a2)), "b")
    near_b = swap(tile("send_b2", False, 1, HALF, 1, (got_b1, got_b2)), "a")
    keep_a2 = tile("keep_a2", False, 0, 0, 0, (got_a1, got_a2))
    keep_b2 = tile("keep_b2", False, 0, HALF, 0, (got_b1, got_b2))
    across = swap(
        sums("far", [(2, KV, HALF)], [(keep_a1, far_a, None, None, 0, 0), (keep_b1, far_b, None, None, 0, 1)]), "z"
    )
    send_0, send_1, stay_0, stay_1 = other(
        "other_1",
        [
            dest(2, 0, ROWS, [(0, 1, *lo), (1, 1, *hi)]),
            dest(1, 0, 0, [(0, 0, *lo), (3, None, *hi)]),
            dest(3, 0, 2 * ROWS, [(1, 0, *hi), (2, None, *lo)]),
        ],
        [pair, pair, half, half],
        (got_z1,),
        10**10,
    )
    got_0, got_1 = swap(send_0, "a"), swap(send_1, "b")
    near = sums("near", [(2, KV, HALF)], [(keep_a2, near_a, None, None, 0, 0), (keep_b2, near_b, None, None, 0, 1)])

    inner_s, send_s = inner_sync(plan, w, near, across)
    send, keep = sum_x(inner_s, swap(send_s, "core"), "sync_x1")
    recv = swap(send, "x1")
    send, keep = halve("sync_x3", QUAD, keep, recv)
    recv = swap(send, "x3")
    last_0, last_1 = sums(
        "last", [half, half], [(stay_0, got_0, None, 1, 0, None), (stay_1, got_1, None, 1, 1, None)]
    )
    last_0, last_1 = swap(last_0, "b"), swap(last_1, "a")
    parts = dealt(spread_z((keep, recv), "sync_z"), "z")
    mine_0, mine_1 = other("other_3", [dest(0, 1, 0, [(0, None, *lo), (1, None, *hi)])], [half, half], (got_z1, got_z3))
    anchor_new, momentum_new, short = outer_sync(plan, anchors, momentum, parts)
    parts = shared(short, "z")

    inner_o, send_o, new = inner_other(plan, w, (mine_0, got_0, last_0), (mine_1, got_1, last_1))
    core_o = swap(send_o, "core")
    blocks = shared(row_of(parts), "x")
    parts = dealt(spread_x(inner_o, core_o, "other_x"), "x")
    block = block_of(blocks)
    block_far = swap(block, "core")
    parts = dealt(spread_z(parts, "other_z"), "z")
    new = mix(plan, inner_s, block, block_far, new)
    pending = outer_other(plan, anchors, parts)
    return (new.reshape(1, 2, ROWS, KV), anchor_new, momentum_new, pending)


def solution(mesh):
    return jax.shard_map(
        body,
        mesh=mesh,
        in_specs=(
            P(("worker", "fsdp")),
            P(None, ("worker", "fsdp"), None),
            P(None, ("worker", "fsdp"), None),
            P("worker", None, "fsdp", None),
            P(None, ("fsdp", "worker"), None),
            P(("fsdp", "worker"), None),
            P(),
        ),
        out_specs=(
            P("worker", None, "fsdp", None),
            P(("fsdp", "worker"), None),
            P(("fsdp", "worker"), None),
            P(("fsdp", "worker"), None),
        ),
        check_vma=False,
    )
```

```python
import jax
import jax.numpy as jnp
from jax import lax
from jax.experimental import pallas as pl
from jax.experimental.pallas import tpu as pltpu
from jax.sharding import PartitionSpec as P

inner_rate = 0.25
decay_rate = 0.1
outer_rate = 0.7
outer_beta = 0.9
mix_weight = 0.5

TOK = 256
KV = 512
ROWS = 1024
HALF = 512
F32 = jnp.float32
BF16 = jnp.bfloat16

HBM = pl.BlockSpec(memory_space=pltpu.HBM)
ANY = pl.BlockSpec(memory_space=pl.ANY)
VM = pl.BlockSpec(memory_space=pltpu.VMEM)
SM = pl.BlockSpec(memory_space=pltpu.SMEM)
MIB = 1024 * 1024
BIG = 24


def place():
    w = lax.axis_index("worker")
    f = lax.axis_index("fsdp")
    return w // 8, (w // 2) % 4, w % 2, f // 4, f % 4


def shape(*dims, dtype=BF16):
    return jax.ShapeDtypeStruct(dims, dtype)


def in_vmem(*dims):
    return pltpu.VMEM(dims, BF16)


def in_hbm(*dims):
    return pltpu.HBM(dims, BF16)


def pinned(value):
    return pltpu.with_memory_space_constraint(value, pltpu.HBM)


class Chain:
    def __init__(self):
        self.token = None


CHAIN = Chain()


def call(kernel, outs, args, specs, out_specs, scratch=(), aliases=None, name=None, vmem=16, hint=0):
    outs, out_specs = list(outs), list(out_specs)
    tokens = [] if CHAIN.token is None else [CHAIN.token]
    count = len(args)

    def chained(*refs):
        rest = refs[count + len(tokens) :]
        kernel(*refs[:count], *rest[: len(outs)], *rest[len(outs) + 1 :])

    *results, CHAIN.token = pl.pallas_call(
        chained,
        out_shape=outs + [in_hbm(8, 128)],
        in_specs=list(specs) + [HBM] * len(tokens),
        out_specs=out_specs + [HBM],
        scratch_shapes=list(scratch),
        compiler_params=pltpu.CompilerParams(vmem_limit_bytes=vmem * MIB),
        cost_estimate=pl.CostEstimate(flops=hint, bytes_accessed=0, transcendentals=0),
        input_output_aliases=aliases or {},
        name=name,
    )(*(pinned(a) if spec is HBM else a for a, spec in zip(args, specs)), *(pinned(t) for t in tokens))
    return results[0] if len(results) == 1 else results


def columns(start, width):
    return pl.ds(pl.multiple_of(start, width), width)


def pack(name, fragment, plan, ids, x, g, outs, pieces, g_to):
    def kernel(plan_ref, ids_ref, x_ref, g_ref, *rest):
        bufs, gt_ref = rest[: len(outs)], rest[len(outs)]
        gin, tok, sems = rest[len(outs) + 1 :]
        _, _, _, z, y = place()
        s = lax.rem(plan_ref[0], 2)
        layers = (s, 1 - s)
        first = [
            pltpu.make_async_copy(ids_ref, tok, sems.at[0]),
            pltpu.make_async_copy(g_ref.at[layers[fragment]], gin, sems.at[1]),
        ]
        copies = []
        for layer, start, width, out, at in pieces:
            col = pl.multiple_of(start(z, y), HALF)
            copies.append(
                pltpu.make_async_copy(
                    x_ref.at[layers[layer], :, pl.ds(col, width)],
                    bufs[out].at[:, pl.ds(at, width)],
                    sems.at[2 + len(copies)],
                )
            )
        for c in first + copies:
            c.start()
        for c in first:
            c.wait()
        gt = (gin[...].astype(F32).T * (tok[...] != 0).astype(F32)).astype(BF16)
        gt_ref[...] = gt
        for out, at in g_to:
            for h in range(2):
                bufs[out][:, at + h * TOK : at + (h + 1) * TOK] = gt[h * TOK : (h + 1) * TOK]
        for c in copies:
            c.wait()

    return call(
        kernel,
        [in_vmem(TOK, n) for n in outs] + [in_vmem(KV, TOK)],
        (plan, ids, x, g),
        [SM, HBM, HBM, HBM],
        [VM] * (len(outs) + 1),
        [
            pltpu.VMEM((TOK, KV), BF16),
            pltpu.VMEM((1, TOK), jnp.int32),
            pltpu.SemaphoreType.DMA((2 + len(pieces),)),
        ],
        name=name,
        vmem=BIG,
    )


def pack_all(plan, ids, x, g):
    def sync(far, flip_y, offset, out, at):
        return (0, lambda z, y: ((1 - z if far else z) * 4 + (y ^ flip_y)) * ROWS + offset, HALF, out, at * HALF)

    def other(j, out, at):
        return (1, lambda z, y: ((1 - z) * 4 + (y ^ j)) * ROWS, ROWS, out, at * ROWS)

    def pair(far, out):
        return [
            sync(far, 1, 0, out, 0),
            sync(far, 2, 0, out, 1),
            sync(far, 3, HALF, out + 1, 0),
            sync(far, 2, HALF, out + 1, 1),
        ]

    wide, half = 2 * HALF + KV, 2 * HALF
    a1, b1, gt_s = pack("pack_1", 0, plan, ids, x, g, [wide, wide], pair(True, 0), [(0, half), (1, half)])
    z1, a2, b2, z3, gt_o = pack(
        "pack_2",
        1,
        plan,
        ids,
        x,
        g,
        [3 * ROWS + KV, half, half, ROWS],
        [other(1, 0, 0), other(2, 0, 1), other(3, 0, 2), *pair(False, 1), other(0, 3, 0)],
        [(0, 3 * ROWS)],
    )
    return a1, b1, z1, a2, b2, z3, gt_s, gt_o


def product(name, fragment, pieces, width, out_shapes, g_at, plan, x, gt, recvs, hint=0):
    count = len(pieces)
    number = len(recvs)
    total = sum(len(p[3]) for p in pieces)

    def kernel(plan_ref, x_ref, gt_ref, *rest):
        recv_refs = rest[:number]
        outs = rest[number : number + len(out_shapes)]
        stage = rest[number + len(out_shapes) : number + 2 * len(out_shapes)]
        gts, xs, sems, out_sems = rest[number + 2 * len(out_shapes) :]
        _, _, _, z, y = place()
        s = lax.rem(plan_ref[0], 2)
        layer = s if fragment == 0 else 1 - s
        g_copies = [
            pltpu.make_async_copy(gt_ref, gts.at[:, pl.ds(0, TOK)], sems.at[2 * count]),
            *(
                pltpu.make_async_copy(
                    recv_refs[0].at[:, pl.ds(g_at + h * TOK, TOK)],
                    gts.at[pl.ds(h * TOK, TOK), pl.ds(TOK, TOK)],
                    sems.at[2 * count + 1 + h],
                )
                for h in range(2)
            ),
        ]
        copies = []
        for p, (own, source, at, _) in enumerate(pieces):
            copies.append(
                (
                    pltpu.make_async_copy(
                        x_ref.at[layer, :, columns(own(z, y), width)], xs.at[p, pl.ds(0, TOK)], sems.at[2 * p]
                    ),
                    pltpu.make_async_copy(
                        recv_refs[source].at[:, pl.ds(at, width)], xs.at[p, pl.ds(TOK, TOK)], sems.at[2 * p + 1]
                    ),
                )
            )
        for c in g_copies:
            c.start()
        for pair in copies:
            for c in pair:
                c.start()
        for c in g_copies:
            c.wait()
        done = []
        for p, (_, _, _, targets) in enumerate(pieces):
            for c in copies[p]:
                c.wait()
            for out, slot, k0, k1 in targets:
                src = stage[out] if slot is None else stage[out].at[slot]
                dst = outs[out] if slot is None else outs[out].at[slot]
                src[...] = jnp.dot(gts[k0:k1], xs[p], preferred_element_type=F32).astype(BF16)
                c = pltpu.make_async_copy(src, dst, out_sems.at[len(done)])
                c.start()
                done.append(c)
        for c in done:
            c.wait()

    return call(
        kernel,
        tuple(shape(*d) for d in out_shapes),
        (plan, x, gt, *recvs),
        [SM, ANY, ANY] + [ANY] * number,
        [ANY] * len(out_shapes),
        [
            *(pltpu.VMEM(d, BF16) for d in out_shapes),
            pltpu.VMEM((KV, 2 * TOK), BF16),
            pltpu.VMEM((count, 2 * TOK, width), BF16),
            pltpu.SemaphoreType.DMA((2 * count + 3,)),
            pltpu.SemaphoreType.DMA((total,)),
        ],
        name=name,
        vmem=BIG,
        hint=hint,
    )


def flip(*terms):
    return sum(t.astype(F32) for t in terms).T


def stepped(w, gradient):
    return (w.astype(F32) * (1.0 - inner_rate * decay_rate) - inner_rate * gradient).astype(BF16)


WORKERS = (16, 2, 32, KV)


def inner_sync(plan, w, near, across):
    def kernel(plan_ref, w_ref, near_ref, z_ref, inner_ref, send_ref, wv, sem, sem2):
        s = lax.rem(plan_ref[0], 2)
        core = place()[2]
        load = pltpu.make_async_copy(w_ref.at[s], wv, sem)
        load.start()
        load.wait()
        for h in range(2):
            for q in range(4):
                cols = pl.ds(q * 128, 128)
                i = h * 8 + q * 2
                gradient = flip(near_ref[h, :, cols], z_ref[h, :, cols])
                inner_ref[i : i + 2] = stepped(wv[i : i + 2].reshape(128, KV), gradient).reshape(2, 2, 32, KV)
        out = pltpu.make_async_copy(inner_ref.at[:, 1 - core], send_ref, sem2)
        out.start()
        out.wait()

    return call(
        kernel,
        (shape(*WORKERS), shape(16, 32, KV)),
        (plan, w, near, across),
        [SM, HBM] + [VM] * 2,
        [VM, ANY],
        [pltpu.VMEM(WORKERS, BF16), pltpu.SemaphoreType.DMA, pltpu.SemaphoreType.DMA],
        name="inner_sync",
    )


def inner_other(plan, w, first, second):
    def kernel(plan_ref, w_ref, *rest):
        k0, r0, l0, k1, r1, l1, inner_ref, send_ref, new_ref, wv, sem, sem2 = rest
        other = 1 - lax.rem(plan_ref[0], 2)
        core = place()[2]
        load = pltpu.make_async_copy(w_ref.at[other], wv, sem)
        load.start()
        load.wait()
        for q in range(8):
            cols = pl.ds(q * 128, 128)
            i = q * 2
            gradient = jnp.concatenate(
                [flip(k[:, cols], r[0, :, cols], l[:, cols]) for k, r, l in ((k0, r0, l0), (k1, r1, l1))], axis=1
            )
            inner_ref[i : i + 2] = stepped(wv[i : i + 2].reshape(128, KV), gradient).reshape(2, 2, 32, KV)
        out = pltpu.make_async_copy(inner_ref.at[:, 1 - core], send_ref, sem2.at[0])
        keep = pltpu.make_async_copy(inner_ref, new_ref.at[other], sem2.at[1])
        out.start()
        keep.start()
        out.wait()
        keep.wait()

    return call(
        kernel,
        (shape(*WORKERS), shape(16, 32, KV), shape(2, *WORKERS)),
        (plan, w, *first, *second),
        [SM, HBM] + [VM] * 6,
        [VM, ANY, ANY],
        [pltpu.VMEM(WORKERS, BF16), pltpu.SemaphoreType.DMA, pltpu.SemaphoreType.DMA((2,))],
        name="inner_other",
    )


def plus(a, b):
    return (a.astype(F32) + b.astype(F32)).astype(BF16)


def to_x(inner_ref, recv_ref, send_ref, keep_ref):
    x, _, core, _, _ = place()
    for ref, at, j in ((send_ref, 0, 1), (send_ref, 1, 2), (keep_ref, 0, 0), (keep_ref, 1, 3)):
        block = pl.ds((x ^ j) * 4, 4)
        ref[at] = plus(inner_ref[block, core], recv_ref[block])


def to_z(keep_ref, recv_ref, send_ref, stay_ref):
    zh = place()[1]
    for ref, at, j in ((send_ref, 0, 1), (send_ref, 1, 2), (stay_ref, 0, 0), (stay_ref, 1, 3)):
        ref[at] = plus(keep_ref[zh ^ j], recv_ref[zh ^ j])


QUAD = (4, 32, KV)


def sums(name, outs, pairs, extra=()):
    def kernel(*refs):
        out_refs = refs[2 * len(pairs) + len(extra) :]
        for i, (_, _, at_a, at_b, out, slot) in enumerate(pairs):
            a, b = refs[2 * i], refs[2 * i + 1]
            total = plus(a[...] if at_a is None else a[at_a], b[...] if at_b is None else b[at_b])
            if slot is None:
                out_refs[out][...] = total
            else:
                out_refs[out][slot] = total

    args = [t for p in pairs for t in p[:2]]
    return call(
        kernel,
        [shape(*d) for d in outs],
        (*args, *extra),
        [VM] * len(args) + [ANY] * len(extra),
        [VM] * len(outs),
        name=name,
    )


def halve(name, dims, keep, recv):
    return sums(name, [dims] * 2, [(keep, recv, 1, 1, 0, None), (keep, recv, 0, 0, 1, None)])


def sum_x(inner, recv, name):
    return call(to_x, (shape(2, *QUAD),) * 2, (inner, recv), [VM] * 2, [VM] * 2, name=name)


def sum_z(keep, recv, name):
    return call(to_z, (shape(2, 32, KV),) * 2, (keep, recv), [VM] * 2, [VM] * 2, name=name)


def sync_z1(plan, anchors, momentum, keep, recv):
    def kernel(plan_ref, anchor_ref, momentum_ref, keep_ref, recv_ref, out_ref):
        out_ref[:4] = plus(keep_ref[...], recv_ref[...])
        anchor = anchor_ref[lax.rem(plan_ref[0], 2)]
        q = (1.0 - outer_rate * (1.0 + outer_beta)) * anchor - outer_rate * outer_beta**2 * momentum_ref[...]
        out_ref[4] = q.astype(BF16)

    return call(
        kernel,
        (shape(5, 32, KV),),
        (plan, anchors, momentum, keep, recv),
        [SM] + [VM] * 4,
        [VM],
        name="sync_z1",
    )


def sync_z3(sent, recv):
    def kernel(sent_ref, recv_ref, out_ref):
        out_ref[:4] = plus(sent_ref[:4], recv_ref[:4])
        out_ref[4] = sent_ref[4]
        out_ref[5] = recv_ref[4]

    return call(kernel, (shape(6, 32, KV),), (sent, recv), [VM] * 2, [VM], name="sync_z3")


def new_rows(sent, recv):
    def kernel(sent_ref, recv_ref, out_ref):
        zh = place()[1]
        for ref, at, j in ((sent_ref, 4, 0), (sent_ref, 5, 1), (recv_ref, 4, 3), (recv_ref, 5, 2)):
            i = zh ^ j
            mean = (sent_ref[i].astype(F32) + recv_ref[i].astype(F32)) / 32
            out_ref[i] = (ref[at].astype(F32) + outer_rate * (1.0 + outer_beta) * mean).astype(BF16)

    return call(kernel, (shape(*QUAD),), (sent, recv), [VM] * 2, [VM], name="new_rows")


def join(a, b, hint=0):
    def kernel(a_ref, b_ref, out_ref):
        out_ref[0] = a_ref[...]
        out_ref[1] = b_ref[...]

    return call(kernel, (shape(2, *a.shape),), (a, b), [VM] * 2, [VM], name="join", hint=hint)


def block_of(own, got):
    def kernel(own_ref, got_ref, out_ref):
        x = place()[0]
        for ref, at, j in ((own_ref, 0, 0), (own_ref, 1, 3), (got_ref, 0, 1), (got_ref, 1, 2)):
            out_ref[pl.ds((x ^ j) * 4, 4)] = ref[at]

    return call(kernel, (shape(16, 32, KV),), (own, got), [VM] * 2, [VM], name="block")


def outer_sync(plan, anchors, momentum, keep, recv):
    def kernel(plan_ref, anchor_ref, momentum_ref, a, b, new_ref, moment_ref):
        s = lax.rem(plan_ref[0], 2)
        zh = place()[1]
        mean = (a[zh].astype(F32) + b[zh].astype(F32)) / 32
        anchor = anchor_ref[s]
        outer_grad = anchor - mean
        moment = outer_beta * momentum_ref[...] + outer_grad
        new_ref[...] = anchor - outer_rate * (outer_grad + outer_beta * moment)
        moment_ref[...] = moment

    return call(
        kernel,
        (shape(32, KV, dtype=F32), shape(32, KV, dtype=F32)),
        (plan, anchors, momentum, keep, recv),
        [SM] + [VM] * 4,
        [VM] * 2,
        name="outer_sync",
    )


def outer_other(plan, anchors, keep, recv):
    def kernel(plan_ref, anchor_ref, a, b, out_ref):
        other = 1 - lax.rem(plan_ref[0], 2)
        out_ref[...] = anchor_ref[other] - (a[...].astype(F32) + b[...].astype(F32)) / 32

    return call(
        kernel,
        (shape(32, KV, dtype=F32),),
        (plan, anchors, keep, recv),
        [SM] + [VM] * 3,
        [VM],
        name="outer_other",
    )


def mix(plan, inner, own, recv, new):
    def kernel(plan_ref, inner_ref, own_ref, recv_ref, _, out_ref, stage, sems):
        s = lax.rem(plan_ref[0], 2)
        core = place()[2]
        for t, c in ((own_ref, core), (recv_ref, 1 - core)):
            stage[:, c] = (
                mix_weight * inner_ref[:, c].astype(F32) + (1.0 - mix_weight) * t[...].astype(F32)
            ).astype(BF16)
        out = pltpu.make_async_copy(stage, out_ref.at[s], sems)
        out.start()
        out.wait()

    return call(
        kernel,
        (shape(2, *WORKERS),),
        (plan, inner, own, recv, new),
        [SM, VM, VM, VM, ANY],
        [ANY],
        [pltpu.VMEM(WORKERS, BF16), pltpu.SemaphoreType.DMA],
        aliases={4: 0},
        name="mix",
    )


def along_fsdp(move):
    return [(z * 4 + y, move(z, y)) for z in range(2) for y in range(4)]


def along_worker(move):
    def index(x, z, c):
        return (x * 4 + z) * 2 + c

    return [(index(x, z, c), index(*move(x, z, c))) for x in range(4) for z in range(4) for c in range(2)]


MOVES = {
    "a": ("fsdp", along_fsdp(lambda z, y: z * 4 + (y ^ 1))),
    "b": ("fsdp", along_fsdp(lambda z, y: z * 4 + (y ^ 3))),
    "z": ("fsdp", along_fsdp(lambda z, y: (1 - z) * 4 + y)),
    "core": ("worker", along_worker(lambda x, z, c: (x, z, 1 - c))),
    "x1": ("worker", along_worker(lambda x, z, c: (x ^ 1, z, c))),
    "x3": ("worker", along_worker(lambda x, z, c: (x ^ 3, z, c))),
    "z1": ("worker", along_worker(lambda x, z, c: (x, z ^ 1, c))),
    "z3": ("worker", along_worker(lambda x, z, c: (x, z ^ 3, c))),
}


def swap(value, move):
    return lax.ppermute(value, *MOVES[move])


def body(token_ids, layer_inputs, key_grads, weights, anchors, momentum, plan):
    CHAIN.token = None
    x = layer_inputs
    w = weights.reshape(2, *WORKERS)
    a1, b1, z1, a2, b2, z3, gt_s, gt_o = pack_all(plan, token_ids.reshape(1, TOK), x, key_grads)
    got_a1 = swap(a1, "a")
    got_b1 = swap(b1, "b")
    got_z1 = swap(z1, "z")
    got_a2 = swap(a2, "a")
    got_b2 = swap(b2, "b")
    got_z3 = swap(z3, "z")

    def tile(name, far, flip_y, offset, at, recvs, hint=0):
        piece = (
            lambda z, y: ((1 - z if far else z) * 4 + (y ^ flip_y)) * ROWS + offset,
            len(recvs) - 1,
            at * HALF,
            [(0, None, 0, KV)],
        )
        return product(name, 0, [piece], HALF, [(KV, HALF)], 2 * HALF, plan, x, gt_s, recvs, hint)

    def dest(j, source, at, targets):
        return (lambda z, y: (z * 4 + (y ^ j)) * ROWS, source, at, targets)

    def other(name, pieces, outs, recvs, hint=0):
        return product(name, 1, pieces, ROWS, outs, 3 * ROWS, plan, x, gt_o, recvs, hint)

    lo, hi = (0, 256), (256, 512)
    half, pair = (256, ROWS), (2, 256, ROWS)

    far_a = swap(tile("send_a1", True, 3, 0, 1, (got_a1,)), "b")
    far_b = swap(tile("send_b1", True, 1, HALF, 1, (got_b1,)), "a")
    keep_a1 = tile("keep_a1", True, 0, 0, 0, (got_a1,))
    keep_b1 = tile("keep_b1", True, 0, HALF, 0, (got_b1,))
    near_a = swap(tile("send_a2", False, 3, 0, 1, (got_a1, got_a2)), "b")
    near_b = swap(tile("send_b2", False, 1, HALF, 1, (got_b1, got_b2)), "a")
    keep_a2 = tile("keep_a2", False, 0, 0, 0, (got_a1, got_a2))
    keep_b2 = tile("keep_b2", False, 0, HALF, 0, (got_b1, got_b2), 4 * 10**10)
    across = swap(
        sums("far", [(2, KV, HALF)], [(keep_a1, far_a, None, None, 0, 0), (keep_b1, far_b, None, None, 0, 1)]), "z"
    )
    send_0, send_1, stay_0, stay_1 = other(
        "other_1",
        [
            dest(2, 0, ROWS, [(0, 1, *lo), (1, 1, *hi)]),
            dest(1, 0, 0, [(0, 0, *lo), (3, None, *hi)]),
            dest(3, 0, 2 * ROWS, [(1, 0, *hi), (2, None, *lo)]),
        ],
        [pair, pair, half, half],
        (got_z1,),
        10**10,
    )
    got_0, got_1 = swap(send_0, "a"), swap(send_1, "b")
    near = sums("near", [(2, KV, HALF)], [(keep_a2, near_a, None, None, 0, 0), (keep_b2, near_b, None, None, 0, 1)])

    inner_s, send_s = inner_sync(plan, w, near, across)
    send, keep = sum_x(inner_s, swap(send_s, "core"), "sync_x1")
    recv = swap(send, "x1")
    last_0, last_1 = sums(
        "last", [half, half], [(stay_0, got_0, None, 1, 0, None), (stay_1, got_1, None, 1, 1, None)]
    )
    last_0, last_1 = swap(last_0, "b"), swap(last_1, "a")
    send, keep = halve("sync_x3", QUAD, keep, recv)
    sent = sync_z1(plan, anchors, momentum, keep, swap(send, "x3"))
    recv = swap(sent, "z1")
    mine_0, mine_1 = other("other_3", [dest(0, 1, 0, [(0, None, *lo), (1, None, *hi)])], [half, half], (got_z1, got_z3))
    sent = sync_z3(sent, recv)
    recv = swap(sent, "z3")
    row = new_rows(sent, recv)
    row_far = swap(row, "x3")
    anchor_new, momentum_new = outer_sync(plan, anchors, momentum, sent, recv)

    inner_o, send_o, new = inner_other(plan, w, (mine_0, got_0, last_0), (mine_1, got_1, last_1))
    core_o = swap(send_o, "core")
    own = join(row, row_far, 10**11)
    got = swap(own, "x1")
    send, keep = sum_x(inner_o, core_o, "other_x1")
    recv = swap(send, "x1")
    block = block_of(own, got)
    block_far = swap(block, "core")
    send, keep = halve("other_x3", QUAD, keep, recv)
    recv = swap(send, "x3")
    new = mix(plan, inner_s, block, block_far, new)
    send, keep = sum_z(keep, recv, "other_z1")
    recv = swap(send, "z1")
    send, keep = halve("other_z3", (32, KV), keep, recv)
    recv = swap(send, "z3")
    pending = outer_other(plan, anchors, keep, recv)
    return (new.reshape(1, 2, ROWS, KV), anchor_new, momentum_new, pending)


def solution(mesh):
    return jax.shard_map(
        body,
        mesh=mesh,
        in_specs=(
            P(("worker", "fsdp")),
            P(None, ("worker", "fsdp"), None),
            P(None, ("worker", "fsdp"), None),
            P("worker", None, "fsdp", None),
            P(None, ("fsdp", "worker"), None),
            P(("fsdp", "worker"), None),
            P(),
        ),
        out_specs=(
            P("worker", None, "fsdp", None),
            P(("fsdp", "worker"), None),
            P(("fsdp", "worker"), None),
            P(("fsdp", "worker"), None),
        ),
        check_vma=False,
    )
```

```python
import jax
import jax.numpy as jnp
from jax import lax
from jax.experimental import pallas as pl
from jax.experimental.pallas import tpu as pltpu
from jax.sharding import PartitionSpec as P

inner_rate = 0.25
decay_rate = 0.1
outer_rate = 0.7
outer_beta = 0.9
mix_weight = 0.5

TOK = 256
KV = 512
ROWS = 1024
HALF = 512
F32 = jnp.float32
BF16 = jnp.bfloat16

HBM = pl.BlockSpec(memory_space=pltpu.HBM)
ANY = pl.BlockSpec(memory_space=pl.ANY)
VM = pl.BlockSpec(memory_space=pltpu.VMEM)
SM = pl.BlockSpec(memory_space=pltpu.SMEM)
MIB = 1024 * 1024
BIG = 24
LONG = 2 * 10**10
SHORT = 3 * 10**9


def place():
    w = lax.axis_index("worker")
    f = lax.axis_index("fsdp")
    return w // 8, (w // 2) % 4, w % 2, f // 4, f % 4


def shape(*dims, dtype=BF16):
    return jax.ShapeDtypeStruct(dims, dtype)


def in_vmem(*dims):
    return pltpu.VMEM(dims, BF16)


def in_hbm(*dims):
    return pltpu.HBM(dims, BF16)


def pinned(value):
    return pltpu.with_memory_space_constraint(value, pltpu.HBM)


class Chain:
    def __init__(self):
        self.token = None


CHAIN = Chain()


def call(kernel, outs, args, specs, out_specs, scratch=(), aliases=None, name=None, vmem=16, hint=0):
    outs, out_specs = list(outs), list(out_specs)
    tokens = [] if CHAIN.token is None else [CHAIN.token]
    count = len(args)

    def chained(*refs):
        rest = refs[count + len(tokens) :]
        kernel(*refs[:count], *rest[: len(outs)], *rest[len(outs) + 1 :])

    *results, CHAIN.token = pl.pallas_call(
        chained,
        out_shape=outs + [in_hbm(8, 128)],
        in_specs=list(specs) + [HBM] * len(tokens),
        out_specs=out_specs + [HBM],
        scratch_shapes=list(scratch),
        compiler_params=pltpu.CompilerParams(vmem_limit_bytes=vmem * MIB),
        cost_estimate=pl.CostEstimate(flops=hint, bytes_accessed=0, transcendentals=0),
        input_output_aliases=aliases or {},
        name=name,
    )(*(pinned(a) if spec is HBM else a for a, spec in zip(args, specs)), *(pinned(t) for t in tokens))
    return results[0] if len(results) == 1 else results


def columns(start, width):
    return pl.ds(pl.multiple_of(start, width), width)


def pack(name, fragment, plan, ids, x, g, outs, pieces, g_to):
    def kernel(plan_ref, ids_ref, x_ref, g_ref, *rest):
        bufs, gt_ref = rest[: len(outs)], rest[len(outs)]
        gin, tok, sems = rest[len(outs) + 1 :]
        _, _, _, z, y = place()
        s = lax.rem(plan_ref[0], 2)
        layers = (s, 1 - s)
        first = [
            pltpu.make_async_copy(ids_ref, tok, sems.at[0]),
            pltpu.make_async_copy(g_ref.at[layers[fragment]], gin, sems.at[1]),
        ]
        copies = []
        for layer, start, width, out, at in pieces:
            col = pl.multiple_of(start(z, y), HALF)
            copies.append(
                pltpu.make_async_copy(
                    x_ref.at[layers[layer], :, pl.ds(col, width)],
                    bufs[out].at[:, pl.ds(at, width)],
                    sems.at[2 + len(copies)],
                )
            )
        for c in first + copies:
            c.start()
        for c in first:
            c.wait()
        gt = (gin[...].astype(F32).T * (tok[...] != 0).astype(F32)).astype(BF16)
        gt_ref[...] = gt
        for out, at in g_to:
            for h in range(2):
                bufs[out][:, at + h * TOK : at + (h + 1) * TOK] = gt[h * TOK : (h + 1) * TOK]
        for c in copies:
            c.wait()

    return call(
        kernel,
        [in_vmem(TOK, n) for n in outs] + [in_vmem(KV, TOK)],
        (plan, ids, x, g),
        [SM, HBM, HBM, HBM],
        [VM] * (len(outs) + 1),
        [
            pltpu.VMEM((TOK, KV), BF16),
            pltpu.VMEM((1, TOK), jnp.int32),
            pltpu.SemaphoreType.DMA((2 + len(pieces),)),
        ],
        name=name,
        vmem=BIG,
    )


def pack_all(plan, ids, x, g):
    def sync(far, flip_y, offset, out, at):
        return (0, lambda z, y: ((1 - z if far else z) * 4 + (y ^ flip_y)) * ROWS + offset, HALF, out, at * HALF)

    def other(j, out, at):
        return (1, lambda z, y: ((1 - z) * 4 + (y ^ j)) * ROWS, ROWS, out, at * ROWS)

    def pair(far, out):
        return [
            sync(far, 1, 0, out, 0),
            sync(far, 2, 0, out, 1),
            sync(far, 3, HALF, out + 1, 0),
            sync(far, 2, HALF, out + 1, 1),
        ]

    wide, half = 2 * HALF + KV, 2 * HALF
    a1, b1, gt_s = pack("pack_1", 0, plan, ids, x, g, [wide, wide], pair(True, 0), [(0, half), (1, half)])
    z1, a2, b2, z3, gt_o = pack(
        "pack_2",
        1,
        plan,
        ids,
        x,
        g,
        [3 * ROWS + KV, half, half, ROWS],
        [other(1, 0, 0), other(2, 0, 1), other(3, 0, 2), *pair(False, 1), other(0, 3, 0)],
        [(0, 3 * ROWS)],
    )
    return a1, b1, z1, a2, b2, z3, gt_s, gt_o


def product(name, fragment, pieces, width, out_shapes, g_at, plan, x, gt, recvs, hint=0):
    count = len(pieces)
    number = len(recvs)
    total = sum(len(p[3]) for p in pieces)

    def kernel(plan_ref, x_ref, gt_ref, *rest):
        recv_refs = rest[:number]
        outs = rest[number : number + len(out_shapes)]
        stage = rest[number + len(out_shapes) : number + 2 * len(out_shapes)]
        gts, xs, sems, out_sems = rest[number + 2 * len(out_shapes) :]
        _, _, _, z, y = place()
        s = lax.rem(plan_ref[0], 2)
        layer = s if fragment == 0 else 1 - s
        g_copies = [
            pltpu.make_async_copy(gt_ref, gts.at[:, pl.ds(0, TOK)], sems.at[2 * count]),
            *(
                pltpu.make_async_copy(
                    recv_refs[0].at[:, pl.ds(g_at + h * TOK, TOK)],
                    gts.at[pl.ds(h * TOK, TOK), pl.ds(TOK, TOK)],
                    sems.at[2 * count + 1 + h],
                )
                for h in range(2)
            ),
        ]
        copies = []
        for p, (own, source, at, _) in enumerate(pieces):
            copies.append(
                (
                    pltpu.make_async_copy(
                        x_ref.at[layer, :, columns(own(z, y), width)], xs.at[p, pl.ds(0, TOK)], sems.at[2 * p]
                    ),
                    pltpu.make_async_copy(
                        recv_refs[source].at[:, pl.ds(at, width)], xs.at[p, pl.ds(TOK, TOK)], sems.at[2 * p + 1]
                    ),
                )
            )
        for c in g_copies:
            c.start()
        for pair in copies:
            for c in pair:
                c.start()
        for c in g_copies:
            c.wait()
        done = []
        for p, (_, _, _, targets) in enumerate(pieces):
            for c in copies[p]:
                c.wait()
            for out, slot, k0, k1 in targets:
                src = stage[out] if slot is None else stage[out].at[slot]
                dst = outs[out] if slot is None else outs[out].at[slot]
                src[...] = jnp.dot(gts[k0:k1], xs[p], preferred_element_type=F32).astype(BF16)
                c = pltpu.make_async_copy(src, dst, out_sems.at[len(done)])
                c.start()
                done.append(c)
        for c in done:
            c.wait()

    return call(
        kernel,
        tuple(shape(*d) for d in out_shapes),
        (plan, x, gt, *recvs),
        [SM, ANY, ANY] + [ANY] * number,
        [ANY] * len(out_shapes),
        [
            *(pltpu.VMEM(d, BF16) for d in out_shapes),
            pltpu.VMEM((KV, 2 * TOK), BF16),
            pltpu.VMEM((count, 2 * TOK, width), BF16),
            pltpu.SemaphoreType.DMA((2 * count + 3,)),
            pltpu.SemaphoreType.DMA((total,)),
        ],
        name=name,
        vmem=BIG,
        hint=hint,
    )


def flip(*terms):
    return sum(t.astype(F32) for t in terms).T


def stepped(w, gradient):
    return (w.astype(F32) * (1.0 - inner_rate * decay_rate) - inner_rate * gradient).astype(BF16)


WORKERS = (16, 2, 32, KV)


def inner_sync(plan, w, near, across):
    def kernel(plan_ref, w_ref, near_ref, z_ref, inner_ref, send_ref, wv, sem, sem2):
        s = lax.rem(plan_ref[0], 2)
        core = place()[2]
        load = pltpu.make_async_copy(w_ref.at[s], wv, sem)
        load.start()
        load.wait()
        for h in range(2):
            for q in range(4):
                cols = pl.ds(q * 128, 128)
                i = h * 8 + q * 2
                gradient = flip(near_ref[h, :, cols], z_ref[h, :, cols])
                inner_ref[i : i + 2] = stepped(wv[i : i + 2].reshape(128, KV), gradient).reshape(2, 2, 32, KV)
        out = pltpu.make_async_copy(inner_ref.at[:, 1 - core], send_ref, sem2)
        out.start()
        out.wait()

    return call(
        kernel,
        (shape(*WORKERS), shape(16, 32, KV)),
        (plan, w, near, across),
        [SM, HBM] + [VM] * 2,
        [VM, ANY],
        [pltpu.VMEM(WORKERS, BF16), pltpu.SemaphoreType.DMA, pltpu.SemaphoreType.DMA],
        name="inner_sync",
    )


def inner_other(plan, w, first, second):
    def kernel(plan_ref, w_ref, *rest):
        k0, r0, l0, k1, r1, l1, inner_ref, send_ref, new_ref, wv, sem, sem2 = rest
        other = 1 - lax.rem(plan_ref[0], 2)
        core = place()[2]
        load = pltpu.make_async_copy(w_ref.at[other], wv, sem)
        load.start()
        load.wait()
        for q in range(8):
            cols = pl.ds(q * 128, 128)
            i = q * 2
            gradient = jnp.concatenate(
                [flip(k[:, cols], r[0, :, cols], l[:, cols]) for k, r, l in ((k0, r0, l0), (k1, r1, l1))], axis=1
            )
            inner_ref[i : i + 2] = stepped(wv[i : i + 2].reshape(128, KV), gradient).reshape(2, 2, 32, KV)
        out = pltpu.make_async_copy(inner_ref.at[:, 1 - core], send_ref, sem2.at[0])
        keep = pltpu.make_async_copy(inner_ref, new_ref.at[other], sem2.at[1])
        out.start()
        keep.start()
        out.wait()
        keep.wait()

    return call(
        kernel,
        (shape(*WORKERS), shape(16, 32, KV), shape(2, *WORKERS)),
        (plan, w, *first, *second),
        [SM, HBM] + [VM] * 6,
        [VM, ANY, ANY],
        [pltpu.VMEM(WORKERS, BF16), pltpu.SemaphoreType.DMA, pltpu.SemaphoreType.DMA((2,))],
        name="inner_other",
    )


def plus(a, b):
    return (a.astype(F32) + b.astype(F32)).astype(BF16)


def to_x(inner_ref, recv_ref, send_ref, keep_ref):
    x, _, core, _, _ = place()
    for ref, at, j in ((send_ref, 0, 1), (send_ref, 1, 2), (keep_ref, 0, 0), (keep_ref, 1, 3)):
        block = pl.ds((x ^ j) * 4, 4)
        ref[at] = plus(inner_ref[block, core], recv_ref[block])


def to_z(keep_ref, recv_ref, send_ref, stay_ref):
    zh = place()[1]
    for ref, at, j in ((send_ref, 0, 1), (send_ref, 1, 2), (stay_ref, 0, 0), (stay_ref, 1, 3)):
        ref[at] = plus(keep_ref[zh ^ j], recv_ref[zh ^ j])


QUAD = (4, 32, KV)


def sums(name, outs, pairs, hint=0):
    def kernel(*refs):
        out_refs = refs[2 * len(pairs) :]
        for i, (_, _, at_a, at_b, out, slot) in enumerate(pairs):
            a, b = refs[2 * i], refs[2 * i + 1]
            total = plus(a[...] if at_a is None else a[at_a], b[...] if at_b is None else b[at_b])
            if slot is None:
                out_refs[out][...] = total
            else:
                out_refs[out][slot] = total

    args = [t for p in pairs for t in p[:2]]
    return call(
        kernel,
        [shape(*d) for d in outs],
        args,
        [VM] * len(args),
        [VM] * len(outs),
        name=name,
        hint=hint,
    )


def halve(name, dims, keep, recv, hint=0):
    return sums(name, [dims] * 2, [(keep, recv, 1, 1, 0, None), (keep, recv, 0, 0, 1, None)], hint)


def sum_x(inner, recv, name):
    return call(to_x, (shape(2, *QUAD),) * 2, (inner, recv), [VM] * 2, [VM] * 2, name=name)


def sum_z(keep, recv, name):
    return call(to_z, (shape(2, 32, KV),) * 2, (keep, recv), [VM] * 2, [VM] * 2, name=name)


def both_z1(keep, recv, short):
    def kernel(keep_ref, recv_ref, short_ref, send_ref, stay_ref):
        to_z(keep_ref, recv_ref, send_ref, stay_ref)
        send_ref[2] = short_ref[...]

    return call(
        kernel,
        (shape(3, 32, KV), shape(2, 32, KV)),
        (keep, recv, short),
        [VM] * 3,
        [VM] * 2,
        name="both_z1",
    )


def both_z3(stay, sent, recv):
    def kernel(stay_ref, sent_ref, recv_ref, send_ref, keep_ref):
        send_ref[0] = plus(stay_ref[1], recv_ref[1])
        send_ref[1] = sent_ref[2]
        send_ref[2] = recv_ref[2]
        keep_ref[...] = plus(stay_ref[0], recv_ref[0])

    return call(
        kernel, (shape(3, 32, KV), shape(32, KV)), (stay, sent, recv), [VM] * 3, [VM] * 2, name="both_z3"
    )


def row_of(sent, recv):
    def kernel(sent_ref, recv_ref, out_ref):
        zh = place()[1]
        for ref, at, j in ((sent_ref, 1, 0), (sent_ref, 2, 1), (recv_ref, 1, 3), (recv_ref, 2, 2)):
            out_ref[zh ^ j] = ref[at]

    return call(kernel, (shape(*QUAD),), (sent, recv), [VM] * 2, [VM], name="row")


def join(a, b, hint=0):
    def kernel(a_ref, b_ref, out_ref):
        out_ref[0] = a_ref[...]
        out_ref[1] = b_ref[...]

    return call(kernel, (shape(2, *a.shape),), (a, b), [VM] * 2, [VM], name="join", hint=hint)


def block_of(own, got):
    def kernel(own_ref, got_ref, out_ref):
        x = place()[0]
        for ref, at, j in ((own_ref, 0, 0), (own_ref, 1, 3), (got_ref, 0, 1), (got_ref, 1, 2)):
            out_ref[pl.ds((x ^ j) * 4, 4)] = ref[at]

    return call(kernel, (shape(16, 32, KV),), (own, got), [VM] * 2, [VM], name="block")


def outer_sync(plan, anchors, momentum, keep, recv):
    def kernel(plan_ref, anchor_ref, momentum_ref, a, b, new_ref, moment_ref, short_ref):
        s = lax.rem(plan_ref[0], 2)
        mean = (a[...].astype(F32) + b[...].astype(F32)) / 32
        anchor = anchor_ref[s]
        outer_grad = anchor - mean
        moment = outer_beta * momentum_ref[...] + outer_grad
        new = anchor - outer_rate * (outer_grad + outer_beta * moment)
        new_ref[...] = new
        moment_ref[...] = moment
        short_ref[...] = new.astype(BF16)

    return call(
        kernel,
        (shape(32, KV, dtype=F32), shape(32, KV, dtype=F32), shape(32, KV)),
        (plan, anchors, momentum, keep, recv),
        [SM] + [VM] * 4,
        [VM] * 3,
        name="outer_sync",
        hint=LONG,
    )


def outer_other(plan, anchors, keep, recv):
    def kernel(plan_ref, anchor_ref, a, b, out_ref):
        other = 1 - lax.rem(plan_ref[0], 2)
        out_ref[...] = anchor_ref[other] - (a[...].astype(F32) + b[0].astype(F32)) / 32

    return call(
        kernel,
        (shape(32, KV, dtype=F32),),
        (plan, anchors, keep, recv),
        [SM] + [VM] * 3,
        [VM],
        name="outer_other",
    )


def mix(plan, inner, own, recv, new):
    def kernel(plan_ref, inner_ref, own_ref, recv_ref, _, out_ref, stage, sems):
        s = lax.rem(plan_ref[0], 2)
        core = place()[2]
        for t, c in ((own_ref, core), (recv_ref, 1 - core)):
            stage[:, c] = (
                mix_weight * inner_ref[:, c].astype(F32) + (1.0 - mix_weight) * t[...].astype(F32)
            ).astype(BF16)
        out = pltpu.make_async_copy(stage, out_ref.at[s], sems)
        out.start()
        out.wait()

    return call(
        kernel,
        (shape(2, *WORKERS),),
        (plan, inner, own, recv, new),
        [SM, VM, VM, VM, ANY],
        [ANY],
        [pltpu.VMEM(WORKERS, BF16), pltpu.SemaphoreType.DMA],
        aliases={4: 0},
        name="mix",
    )


def along_fsdp(move):
    return [(z * 4 + y, move(z, y)) for z in range(2) for y in range(4)]


def along_worker(move):
    def index(x, z, c):
        return (x * 4 + z) * 2 + c

    return [(index(x, z, c), index(*move(x, z, c))) for x in range(4) for z in range(4) for c in range(2)]


MOVES = {
    "a": ("fsdp", along_fsdp(lambda z, y: z * 4 + (y ^ 1))),
    "b": ("fsdp", along_fsdp(lambda z, y: z * 4 + (y ^ 3))),
    "z": ("fsdp", along_fsdp(lambda z, y: (1 - z) * 4 + y)),
    "core": ("worker", along_worker(lambda x, z, c: (x, z, 1 - c))),
    "x1": ("worker", along_worker(lambda x, z, c: (x ^ 1, z, c))),
    "x3": ("worker", along_worker(lambda x, z, c: (x ^ 3, z, c))),
    "z1": ("worker", along_worker(lambda x, z, c: (x, z ^ 1, c))),
    "z3": ("worker", along_worker(lambda x, z, c: (x, z ^ 3, c))),
}


def swap(value, move):
    return lax.ppermute(value, *MOVES[move])


def body(token_ids, layer_inputs, key_grads, weights, anchors, momentum, plan):
    CHAIN.token = None
    x = layer_inputs
    w = weights.reshape(2, *WORKERS)
    a1, b1, z1, a2, b2, z3, gt_s, gt_o = pack_all(plan, token_ids.reshape(1, TOK), x, key_grads)
    got_a1 = swap(a1, "a")
    got_b1 = swap(b1, "b")
    got_z1 = swap(z1, "z")
    got_a2 = swap(a2, "a")
    got_b2 = swap(b2, "b")
    got_z3 = swap(z3, "z")

    def tile(name, far, flip_y, offset, at, recvs, hint=0):
        piece = (
            lambda z, y: ((1 - z if far else z) * 4 + (y ^ flip_y)) * ROWS + offset,
            len(recvs) - 1,
            at * HALF,
            [(0, None, 0, KV)],
        )
        return product(name, 0, [piece], HALF, [(KV, HALF)], 2 * HALF, plan, x, gt_s, recvs, hint)

    def dest(j, source, at, targets):
        return (lambda z, y: (z * 4 + (y ^ j)) * ROWS, source, at, targets)

    def other(name, pieces, outs, recvs, hint=0):
        return product(name, 1, pieces, ROWS, outs, 3 * ROWS, plan, x, gt_o, recvs, hint)

    lo, hi = (0, 256), (256, 512)
    half, pair = (256, ROWS), (2, 256, ROWS)

    far_a = swap(tile("send_a1", True, 3, 0, 1, (got_a1,)), "b")
    far_b = swap(tile("send_b1", True, 1, HALF, 1, (got_b1,)), "a")
    keep_a1 = tile("keep_a1", True, 0, 0, 0, (got_a1,))
    keep_b1 = tile("keep_b1", True, 0, HALF, 0, (got_b1,))
    near_a = swap(tile("send_a2", False, 3, 0, 1, (got_a1, got_a2)), "b")
    near_b = swap(tile("send_b2", False, 1, HALF, 1, (got_b1, got_b2)), "a")
    keep_a2 = tile("keep_a2", False, 0, 0, 0, (got_a1, got_a2))
    keep_b2 = tile("keep_b2", False, 0, HALF, 0, (got_b1, got_b2), 2 * LONG)
    across = swap(
        sums("far", [(2, KV, HALF)], [(keep_a1, far_a, None, None, 0, 0), (keep_b1, far_b, None, None, 0, 1)]), "z"
    )
    send_0, send_1, stay_0, stay_1 = other(
        "other_1",
        [
            dest(2, 0, ROWS, [(0, 1, *lo), (1, 1, *hi)]),
            dest(1, 0, 0, [(0, 0, *lo), (3, None, *hi)]),
            dest(3, 0, 2 * ROWS, [(1, 0, *hi), (2, None, *lo)]),
        ],
        [pair, pair, half, half],
        (got_z1,),
        LONG,
    )
    got_0, got_1 = swap(send_0, "a"), swap(send_1, "b")
    near = sums("near", [(2, KV, HALF)], [(keep_a2, near_a, None, None, 0, 0), (keep_b2, near_b, None, None, 0, 1)])

    inner_s, send_s = inner_sync(plan, w, near, across)
    send, keep = sum_x(inner_s, swap(send_s, "core"), "sync_x1")
    recv = swap(send, "x1")
    last_0, last_1 = sums(
        "last", [half, half], [(stay_0, got_0, None, 1, 0, None), (stay_1, got_1, None, 1, 1, None)]
    )
    last_0, last_1 = swap(last_0, "b"), swap(last_1, "a")
    send, keep = halve("sync_x3", QUAD, keep, recv)
    send, keep = sum_z(keep, swap(send, "x3"), "sync_z1")
    recv = swap(send, "z1")
    mine_0, mine_1 = other("other_3", [dest(0, 1, 0, [(0, None, *lo), (1, None, *hi)])], [half, half], (got_z1, got_z3), SHORT)
    inner_o, send_o, new = inner_other(plan, w, (mine_0, got_0, last_0), (mine_1, got_1, last_1))
    core_o = swap(send_o, "core")
    send, keep = halve("sync_z3", (32, KV), keep, recv, LONG)
    recv = swap(send, "z3")
    send_o, keep_o = sum_x(inner_o, core_o, "other_x1")
    recv_o = swap(send_o, "x1")
    anchor_new, momentum_new, short = outer_sync(plan, anchors, momentum, keep, recv)
    send_o, keep_o = halve("other_x3", QUAD, keep_o, recv_o)
    recv_o = swap(send_o, "x3")
    sent, keep = both_z1(keep_o, recv_o, short)
    recv = swap(sent, "z1")
    sent, keep = both_z3(keep, sent, recv)
    recv = swap(sent, "z3")
    row = row_of(sent, recv)
    row_far = swap(row, "x3")
    pending = outer_other(plan, anchors, keep, recv)
    own = join(row, row_far)
    block = block_of(own, swap(own, "x1"))
    new = mix(plan, inner_s, block, swap(block, "core"), new)
    return (new.reshape(1, 2, ROWS, KV), anchor_new, momentum_new, pending)


def solution(mesh):
    return jax.shard_map(
        body,
        mesh=mesh,
        in_specs=(
            P(("worker", "fsdp")),
            P(None, ("worker", "fsdp"), None),
            P(None, ("worker", "fsdp"), None),
            P("worker", None, "fsdp", None),
            P(None, ("fsdp", "worker"), None),
            P(("fsdp", "worker"), None),
            P(),
        ),
        out_specs=(
            P("worker", None, "fsdp", None),
            P(("fsdp", "worker"), None),
            P(("fsdp", "worker"), None),
            P(("fsdp", "worker"), None),
        ),
        check_vma=False,
    )
```

```python
import jax
import jax.numpy as jnp
from jax import lax
from jax.experimental import pallas as pl
from jax.experimental.pallas import tpu as pltpu
from jax.sharding import PartitionSpec as P

inner_rate = 0.25
decay_rate = 0.1
outer_rate = 0.7
outer_beta = 0.9
mix_weight = 0.5

TOK = 256
KV = 512
ROWS = 1024
HALF = 512
F32 = jnp.float32
BF16 = jnp.bfloat16

HBM = pl.BlockSpec(memory_space=pltpu.HBM)
ANY = pl.BlockSpec(memory_space=pl.ANY)
VM = pl.BlockSpec(memory_space=pltpu.VMEM)
SM = pl.BlockSpec(memory_space=pltpu.SMEM)
MIB = 1024 * 1024
BIG = 24
LONG = 2 * 10**10
SHORT = 3 * 10**9


def place():
    w = lax.axis_index("worker")
    f = lax.axis_index("fsdp")
    return w // 8, (w // 2) % 4, w % 2, f // 4, f % 4


def shape(*dims, dtype=BF16):
    return jax.ShapeDtypeStruct(dims, dtype)


def in_vmem(*dims):
    return pltpu.VMEM(dims, BF16)


def in_hbm(*dims):
    return pltpu.HBM(dims, BF16)


def pinned(value):
    return pltpu.with_memory_space_constraint(value, pltpu.HBM)


class Chain:
    def __init__(self):
        self.token = None


CHAIN = Chain()


def call(kernel, outs, args, specs, out_specs, scratch=(), aliases=None, name=None, vmem=16, hint=0):
    outs, out_specs = list(outs), list(out_specs)
    tokens = [] if CHAIN.token is None else [CHAIN.token]
    count = len(args)

    def chained(*refs):
        rest = refs[count + len(tokens) :]
        kernel(*refs[:count], *rest[: len(outs)], *rest[len(outs) + 1 :])

    *results, CHAIN.token = pl.pallas_call(
        chained,
        out_shape=outs + [in_hbm(8, 128)],
        in_specs=list(specs) + [HBM] * len(tokens),
        out_specs=out_specs + [HBM],
        scratch_shapes=list(scratch),
        compiler_params=pltpu.CompilerParams(vmem_limit_bytes=vmem * MIB),
        cost_estimate=pl.CostEstimate(flops=hint, bytes_accessed=0, transcendentals=0),
        input_output_aliases=aliases or {},
        name=name,
    )(*(pinned(a) if spec is HBM else a for a, spec in zip(args, specs)), *(pinned(t) for t in tokens))
    return results[0] if len(results) == 1 else results


def columns(start, width):
    return pl.ds(pl.multiple_of(start, width), width)


def pack(name, fragment, plan, ids, x, g, outs, pieces, g_to):
    def kernel(plan_ref, ids_ref, x_ref, g_ref, *rest):
        bufs, gt_ref = rest[: len(outs)], rest[len(outs)]
        gin, tok, sems = rest[len(outs) + 1 :]
        _, _, _, z, y = place()
        s = lax.rem(plan_ref[0], 2)
        layers = (s, 1 - s)
        first = [
            pltpu.make_async_copy(ids_ref, tok, sems.at[0]),
            pltpu.make_async_copy(g_ref.at[layers[fragment]], gin, sems.at[1]),
        ]
        copies = []
        for layer, start, width, out, at in pieces:
            col = pl.multiple_of(start(z, y), HALF)
            copies.append(
                pltpu.make_async_copy(
                    x_ref.at[layers[layer], :, pl.ds(col, width)],
                    bufs[out].at[:, pl.ds(at, width)],
                    sems.at[2 + len(copies)],
                )
            )
        for c in first + copies:
            c.start()
        for c in first:
            c.wait()
        gt = (gin[...].astype(F32).T * (tok[...] != 0).astype(F32)).astype(BF16)
        gt_ref[...] = gt
        for out, at in g_to:
            for h in range(2):
                bufs[out][:, at + h * TOK : at + (h + 1) * TOK] = gt[h * TOK : (h + 1) * TOK]
        for c in copies:
            c.wait()

    return call(
        kernel,
        [in_vmem(TOK, n) for n in outs] + [in_vmem(KV, TOK)],
        (plan, ids, x, g),
        [SM, HBM, HBM, HBM],
        [VM] * (len(outs) + 1),
        [
            pltpu.VMEM((TOK, KV), BF16),
            pltpu.VMEM((1, TOK), jnp.int32),
            pltpu.SemaphoreType.DMA((2 + len(pieces),)),
        ],
        name=name,
        vmem=BIG,
    )


def pack_all(plan, ids, x, g):
    def sync(far, flip_y, offset, out, at):
        return (0, lambda z, y: ((1 - z if far else z) * 4 + (y ^ flip_y)) * ROWS + offset, HALF, out, at * HALF)

    def other(j, out, at):
        return (1, lambda z, y: ((1 - z) * 4 + (y ^ j)) * ROWS, ROWS, out, at * ROWS)

    def pair(far, out):
        return [
            sync(far, 1, 0, out, 0),
            sync(far, 2, 0, out, 1),
            sync(far, 3, HALF, out + 1, 0),
            sync(far, 2, HALF, out + 1, 1),
        ]

    wide, half = 2 * HALF + KV, 2 * HALF
    a1, b1, gt_s = pack("pack_1", 0, plan, ids, x, g, [wide, wide], pair(True, 0), [(0, half), (1, half)])
    z1, a2, b2, z3, gt_o = pack(
        "pack_2",
        1,
        plan,
        ids,
        x,
        g,
        [3 * ROWS + KV, half, half, ROWS],
        [other(1, 0, 0), other(2, 0, 1), other(3, 0, 2), *pair(False, 1), other(0, 3, 0)],
        [(0, 3 * ROWS)],
    )
    return a1, b1, z1, a2, b2, z3, gt_s, gt_o


def product(name, fragment, pieces, width, out_shapes, g_at, plan, x, gt, recvs, hint=0):
    count = len(pieces)
    number = len(recvs)
    total = sum(len(p[3]) for p in pieces)

    def kernel(plan_ref, x_ref, gt_ref, *rest):
        recv_refs = rest[:number]
        outs = rest[number : number + len(out_shapes)]
        stage = rest[number + len(out_shapes) : number + 2 * len(out_shapes)]
        gts, xs, sems, out_sems = rest[number + 2 * len(out_shapes) :]
        _, _, _, z, y = place()
        s = lax.rem(plan_ref[0], 2)
        layer = s if fragment == 0 else 1 - s
        g_copies = [
            pltpu.make_async_copy(gt_ref, gts.at[:, pl.ds(0, TOK)], sems.at[2 * count]),
            *(
                pltpu.make_async_copy(
                    recv_refs[0].at[:, pl.ds(g_at + h * TOK, TOK)],
                    gts.at[pl.ds(h * TOK, TOK), pl.ds(TOK, TOK)],
                    sems.at[2 * count + 1 + h],
                )
                for h in range(2)
            ),
        ]
        copies = []
        for p, (own, source, at, _) in enumerate(pieces):
            copies.append(
                (
                    pltpu.make_async_copy(
                        x_ref.at[layer, :, columns(own(z, y), width)], xs.at[p, pl.ds(0, TOK)], sems.at[2 * p]
                    ),
                    pltpu.make_async_copy(
                        recv_refs[source].at[:, pl.ds(at, width)], xs.at[p, pl.ds(TOK, TOK)], sems.at[2 * p + 1]
                    ),
                )
            )
        for c in g_copies:
            c.start()
        for pair in copies:
            for c in pair:
                c.start()
        for c in g_copies:
            c.wait()
        done = []
        for p, (_, _, _, targets) in enumerate(pieces):
            for c in copies[p]:
                c.wait()
            for out, slot, k0, k1 in targets:
                src = stage[out] if slot is None else stage[out].at[slot]
                dst = outs[out] if slot is None else outs[out].at[slot]
                src[...] = jnp.dot(gts[k0:k1], xs[p], preferred_element_type=F32).astype(BF16)
                c = pltpu.make_async_copy(src, dst, out_sems.at[len(done)])
                c.start()
                done.append(c)
        for c in done:
            c.wait()

    return call(
        kernel,
        tuple(shape(*d) for d in out_shapes),
        (plan, x, gt, *recvs),
        [SM, ANY, ANY] + [ANY] * number,
        [ANY] * len(out_shapes),
        [
            *(pltpu.VMEM(d, BF16) for d in out_shapes),
            pltpu.VMEM((KV, 2 * TOK), BF16),
            pltpu.VMEM((count, 2 * TOK, width), BF16),
            pltpu.SemaphoreType.DMA((2 * count + 3,)),
            pltpu.SemaphoreType.DMA((total,)),
        ],
        name=name,
        vmem=BIG,
        hint=hint,
    )


def flip(*terms):
    return sum(t.astype(F32) for t in terms).T


def stepped(w, gradient):
    return (w.astype(F32) * (1.0 - inner_rate * decay_rate) - inner_rate * gradient).astype(BF16)


WORKERS = (16, 2, 32, KV)


def inner_sync(plan, w, near, across):
    def kernel(plan_ref, w_ref, near_ref, z_ref, inner_ref, send_ref, wv, sem, sem2):
        s = lax.rem(plan_ref[0], 2)
        core = place()[2]
        load = pltpu.make_async_copy(w_ref.at[s], wv, sem)
        load.start()
        load.wait()
        for h in range(2):
            for q in range(4):
                cols = pl.ds(q * 128, 128)
                i = h * 8 + q * 2
                gradient = flip(near_ref[h, :, cols], z_ref[h, :, cols])
                inner_ref[i : i + 2] = stepped(wv[i : i + 2].reshape(128, KV), gradient).reshape(2, 2, 32, KV)
        out = pltpu.make_async_copy(inner_ref.at[:, 1 - core], send_ref, sem2)
        out.start()
        out.wait()

    return call(
        kernel,
        (shape(*WORKERS), shape(16, 32, KV)),
        (plan, w, near, across),
        [SM, HBM] + [VM] * 2,
        [VM, ANY],
        [pltpu.VMEM(WORKERS, BF16), pltpu.SemaphoreType.DMA, pltpu.SemaphoreType.DMA],
        name="inner_sync",
    )


def inner_other(plan, w, first, second):
    def kernel(plan_ref, w_ref, *rest):
        k0, r0, l0, k1, r1, l1, inner_ref, send_ref, new_ref, wv, sem, sem2 = rest
        other = 1 - lax.rem(plan_ref[0], 2)
        core = place()[2]
        load = pltpu.make_async_copy(w_ref.at[other], wv, sem)
        load.start()
        load.wait()
        for q in range(8):
            cols = pl.ds(q * 128, 128)
            i = q * 2
            gradient = jnp.concatenate(
                [flip(k[:, cols], r[0, :, cols], l[:, cols]) for k, r, l in ((k0, r0, l0), (k1, r1, l1))], axis=1
            )
            inner_ref[i : i + 2] = stepped(wv[i : i + 2].reshape(128, KV), gradient).reshape(2, 2, 32, KV)
        out = pltpu.make_async_copy(inner_ref.at[:, 1 - core], send_ref, sem2.at[0])
        keep = pltpu.make_async_copy(inner_ref, new_ref.at[other], sem2.at[1])
        out.start()
        keep.start()
        out.wait()
        keep.wait()

    return call(
        kernel,
        (shape(*WORKERS), shape(16, 32, KV), shape(2, *WORKERS)),
        (plan, w, *first, *second),
        [SM, HBM] + [VM] * 6,
        [VM, ANY, ANY],
        [pltpu.VMEM(WORKERS, BF16), pltpu.SemaphoreType.DMA, pltpu.SemaphoreType.DMA((2,))],
        name="inner_other",
    )


def plus(a, b):
    return (a.astype(F32) + b.astype(F32)).astype(BF16)


def to_x(inner_ref, recv_ref, send_ref, keep_ref):
    x, _, core, _, _ = place()
    for ref, at, j in ((send_ref, 0, 1), (send_ref, 1, 2), (keep_ref, 0, 0), (keep_ref, 1, 3)):
        block = pl.ds((x ^ j) * 4, 4)
        ref[at] = plus(inner_ref[block, core], recv_ref[block])


def to_z(keep_ref, recv_ref, send_ref, stay_ref):
    zh = place()[1]
    for ref, at, j in ((send_ref, 0, 1), (send_ref, 1, 2), (stay_ref, 0, 0), (stay_ref, 1, 3)):
        ref[at] = plus(keep_ref[zh ^ j], recv_ref[zh ^ j])


QUAD = (4, 32, KV)


def sums(name, outs, pairs, hint=0):
    def kernel(*refs):
        out_refs = refs[2 * len(pairs) :]
        for i, (_, _, at_a, at_b, out, slot) in enumerate(pairs):
            a, b = refs[2 * i], refs[2 * i + 1]
            total = plus(a[...] if at_a is None else a[at_a], b[...] if at_b is None else b[at_b])
            if slot is None:
                out_refs[out][...] = total
            else:
                out_refs[out][slot] = total

    args = [t for p in pairs for t in p[:2]]
    return call(
        kernel,
        [shape(*d) for d in outs],
        args,
        [VM] * len(args),
        [VM] * len(outs),
        name=name,
        hint=hint,
    )


def halve(name, dims, keep, recv, hint=0):
    return sums(name, [dims] * 2, [(keep, recv, 1, 1, 0, None), (keep, recv, 0, 0, 1, None)], hint)


def sum_x(inner, recv, name):
    return call(to_x, (shape(2, *QUAD),) * 2, (inner, recv), [VM] * 2, [VM] * 2, name=name)


def sum_z(keep, recv, name):
    return call(to_z, (shape(2, 32, KV),) * 2, (keep, recv), [VM] * 2, [VM] * 2, name=name)


def plane_sums(inner, recv, after):
    def kernel(inner_ref, recv_ref, _, out_ref):
        out_ref[...] = plus(inner_ref[:, place()[2]], recv_ref[...])

    return call(kernel, (shape(16, 32, KV),), (inner, recv, after), [VM, VM, ANY], [VM], name="plane_sums")


def outer_sync(plan, anchors, momentum, keep, recv):
    def kernel(plan_ref, anchor_ref, momentum_ref, a, b, new_ref, moment_ref, short_ref):
        s = lax.rem(plan_ref[0], 2)
        mean = (a[...].astype(F32) + b[...].astype(F32)) / 32
        anchor = anchor_ref[s]
        outer_grad = anchor - mean
        moment = outer_beta * momentum_ref[...] + outer_grad
        new = anchor - outer_rate * (outer_grad + outer_beta * moment)
        new_ref[...] = new
        moment_ref[...] = moment
        for i in range(16):
            short_ref[i] = new.astype(BF16)

    return call(
        kernel,
        (shape(32, KV, dtype=F32), shape(32, KV, dtype=F32), shape(16, 32, KV)),
        (plan, anchors, momentum, keep, recv),
        [SM] + [VM] * 4,
        [VM] * 3,
        name="outer_sync",
        hint=LONG,
    )


def outer_other(plan, anchors, parts):
    def kernel(plan_ref, anchor_ref, parts_ref, out_ref):
        other = 1 - lax.rem(plan_ref[0], 2)
        out_ref[...] = anchor_ref[other] - sum(parts_ref[i].astype(F32) for i in range(16)) / 32

    return call(
        kernel,
        (shape(32, KV, dtype=F32),),
        (plan, anchors, parts),
        [SM] + [VM] * 2,
        [VM],
        name="outer_other",
    )


def mix(plan, inner, own, recv, new):
    def kernel(plan_ref, inner_ref, own_ref, recv_ref, _, out_ref, stage, sems):
        s = lax.rem(plan_ref[0], 2)
        core = place()[2]
        for t, c in ((own_ref, core), (recv_ref, 1 - core)):
            stage[:, c] = (
                mix_weight * inner_ref[:, c].astype(F32) + (1.0 - mix_weight) * t[...].astype(F32)
            ).astype(BF16)
        out = pltpu.make_async_copy(stage, out_ref.at[s], sems)
        out.start()
        out.wait()

    return call(
        kernel,
        (shape(2, *WORKERS),),
        (plan, inner, own, recv, new),
        [SM, VM, VM, VM, ANY],
        [ANY],
        [pltpu.VMEM(WORKERS, BF16), pltpu.SemaphoreType.DMA],
        aliases={4: 0},
        name="mix",
    )


def along_fsdp(move):
    return [(z * 4 + y, move(z, y)) for z in range(2) for y in range(4)]


def along_worker(move):
    def index(x, z, c):
        return (x * 4 + z) * 2 + c

    return [(index(x, z, c), index(*move(x, z, c))) for x in range(4) for z in range(4) for c in range(2)]


MOVES = {
    "a": ("fsdp", along_fsdp(lambda z, y: z * 4 + (y ^ 1))),
    "b": ("fsdp", along_fsdp(lambda z, y: z * 4 + (y ^ 3))),
    "z": ("fsdp", along_fsdp(lambda z, y: (1 - z) * 4 + y)),
    "core": ("worker", along_worker(lambda x, z, c: (x, z, 1 - c))),
    "x1": ("worker", along_worker(lambda x, z, c: (x ^ 1, z, c))),
    "x3": ("worker", along_worker(lambda x, z, c: (x ^ 3, z, c))),
    "z1": ("worker", along_worker(lambda x, z, c: (x, z ^ 1, c))),
    "z3": ("worker", along_worker(lambda x, z, c: (x, z ^ 3, c))),
}


PLANES = [[i * 2 + c for i in range(16)] for c in range(2)]


def exchange(value):
    return lax.all_to_all(value, "worker", 0, 0, axis_index_groups=PLANES, tiled=True)


def swap(value, move):
    return lax.ppermute(value, *MOVES[move])


def body(token_ids, layer_inputs, key_grads, weights, anchors, momentum, plan):
    CHAIN.token = None
    x = layer_inputs
    w = weights.reshape(2, *WORKERS)
    a1, b1, z1, a2, b2, z3, gt_s, gt_o = pack_all(plan, token_ids.reshape(1, TOK), x, key_grads)
    got_a1 = swap(a1, "a")
    got_b1 = swap(b1, "b")
    got_z1 = swap(z1, "z")
    got_a2 = swap(a2, "a")
    got_b2 = swap(b2, "b")
    got_z3 = swap(z3, "z")

    def tile(name, far, flip_y, offset, at, recvs, hint=0):
        piece = (
            lambda z, y: ((1 - z if far else z) * 4 + (y ^ flip_y)) * ROWS + offset,
            len(recvs) - 1,
            at * HALF,
            [(0, None, 0, KV)],
        )
        return product(name, 0, [piece], HALF, [(KV, HALF)], 2 * HALF, plan, x, gt_s, recvs, hint)

    def dest(j, source, at, targets):
        return (lambda z, y: (z * 4 + (y ^ j)) * ROWS, source, at, targets)

    def other(name, pieces, outs, recvs, hint=0):
        return product(name, 1, pieces, ROWS, outs, 3 * ROWS, plan, x, gt_o, recvs, hint)

    lo, hi = (0, 256), (256, 512)
    half, pair = (256, ROWS), (2, 256, ROWS)

    far_a = swap(tile("send_a1", True, 3, 0, 1, (got_a1,)), "b")
    far_b = swap(tile("send_b1", True, 1, HALF, 1, (got_b1,)), "a")
    keep_a1 = tile("keep_a1", True, 0, 0, 0, (got_a1,))
    keep_b1 = tile("keep_b1", True, 0, HALF, 0, (got_b1,))
    near_a = swap(tile("send_a2", False, 3, 0, 1, (got_a1, got_a2)), "b")
    near_b = swap(tile("send_b2", False, 1, HALF, 1, (got_b1, got_b2)), "a")
    keep_a2 = tile("keep_a2", False, 0, 0, 0, (got_a1, got_a2))
    keep_b2 = tile("keep_b2", False, 0, HALF, 0, (got_b1, got_b2), 2 * LONG)
    across = swap(
        sums("far", [(2, KV, HALF)], [(keep_a1, far_a, None, None, 0, 0), (keep_b1, far_b, None, None, 0, 1)]), "z"
    )
    send_0, send_1, stay_0, stay_1 = other(
        "other_1",
        [
            dest(2, 0, ROWS, [(0, 1, *lo), (1, 1, *hi)]),
            dest(1, 0, 0, [(0, 0, *lo), (3, None, *hi)]),
            dest(3, 0, 2 * ROWS, [(1, 0, *hi), (2, None, *lo)]),
        ],
        [pair, pair, half, half],
        (got_z1,),
        LONG,
    )
    got_0, got_1 = swap(send_0, "a"), swap(send_1, "b")
    near = sums("near", [(2, KV, HALF)], [(keep_a2, near_a, None, None, 0, 0), (keep_b2, near_b, None, None, 0, 1)])

    inner_s, send_s = inner_sync(plan, w, near, across)
    send, keep = sum_x(inner_s, swap(send_s, "core"), "sync_x1")
    recv = swap(send, "x1")
    last_0, last_1 = sums(
        "last", [half, half], [(stay_0, got_0, None, 1, 0, None), (stay_1, got_1, None, 1, 1, None)]
    )
    last_0, last_1 = swap(last_0, "b"), swap(last_1, "a")
    send, keep = halve("sync_x3", QUAD, keep, recv)
    send, keep = sum_z(keep, swap(send, "x3"), "sync_z1")
    recv = swap(send, "z1")
    mine_0, mine_1 = other("other_3", [dest(0, 1, 0, [(0, None, *lo), (1, None, *hi)])], [half, half], (got_z1, got_z3), SHORT)
    inner_o, send_o, new = inner_other(plan, w, (mine_0, got_0, last_0), (mine_1, got_1, last_1))
    core_o = swap(send_o, "core")
    send, keep = halve("sync_z3", (32, KV), keep, recv, LONG)
    recv = swap(send, "z3")
    anchor_new, momentum_new, short = outer_sync(plan, anchors, momentum, keep, recv)
    block = exchange(short)
    block_far = swap(block, "core")
    parts = exchange(plane_sums(inner_o, core_o, block))
    new = mix(plan, inner_s, block, block_far, new)
    pending = outer_other(plan, anchors, parts)
    return (new.reshape(1, 2, ROWS, KV), anchor_new, momentum_new, pending)


def solution(mesh):
    return jax.shard_map(
        body,
        mesh=mesh,
        in_specs=(
            P(("worker", "fsdp")),
            P(None, ("worker", "fsdp"), None),
            P(None, ("worker", "fsdp"), None),
            P("worker", None, "fsdp", None),
            P(None, ("fsdp", "worker"), None),
            P(("fsdp", "worker"), None),
            P(),
        ),
        out_specs=(
            P("worker", None, "fsdp", None),
            P(("fsdp", "worker"), None),
            P(("fsdp", "worker"), None),
            P(("fsdp", "worker"), None),
        ),
        check_vma=False,
    )
```

```python
import jax
import jax.numpy as jnp
from jax import lax
from jax.experimental import pallas as pl
from jax.experimental.pallas import tpu as pltpu
from jax.sharding import PartitionSpec as P

inner_rate = 0.25
decay_rate = 0.1
outer_rate = 0.7
outer_beta = 0.9
mix_weight = 0.5

TOK = 256
KV = 512
ROWS = 1024
HALF = 512
F32 = jnp.float32
BF16 = jnp.bfloat16

HBM = pl.BlockSpec(memory_space=pltpu.HBM)
ANY = pl.BlockSpec(memory_space=pl.ANY)
VM = pl.BlockSpec(memory_space=pltpu.VMEM)
SM = pl.BlockSpec(memory_space=pltpu.SMEM)
MIB = 1024 * 1024
BIG = 24
LONG = 2 * 10**10
SHORT = 3 * 10**9


def place():
    w = lax.axis_index("worker")
    f = lax.axis_index("fsdp")
    return w // 8, (w // 2) % 4, w % 2, f // 4, f % 4


def shape(*dims, dtype=BF16):
    return jax.ShapeDtypeStruct(dims, dtype)


def in_vmem(*dims):
    return pltpu.VMEM(dims, BF16)


def in_hbm(*dims):
    return pltpu.HBM(dims, BF16)


def pinned(value):
    return pltpu.with_memory_space_constraint(value, pltpu.HBM)


class Chain:
    def __init__(self):
        self.token = None


CHAIN = Chain()


def call(kernel, outs, args, specs, out_specs, scratch=(), aliases=None, name=None, vmem=16, hint=0):
    outs, out_specs = list(outs), list(out_specs)
    tokens = [] if CHAIN.token is None else [CHAIN.token]
    count = len(args)

    def chained(*refs):
        rest = refs[count + len(tokens) :]
        kernel(*refs[:count], *rest[: len(outs)], *rest[len(outs) + 1 :])

    *results, CHAIN.token = pl.pallas_call(
        chained,
        out_shape=outs + [in_hbm(8, 128)],
        in_specs=list(specs) + [HBM] * len(tokens),
        out_specs=out_specs + [HBM],
        scratch_shapes=list(scratch),
        compiler_params=pltpu.CompilerParams(vmem_limit_bytes=vmem * MIB),
        cost_estimate=pl.CostEstimate(flops=hint, bytes_accessed=0, transcendentals=0),
        input_output_aliases=aliases or {},
        name=name,
    )(*(pinned(a) if spec is HBM else a for a, spec in zip(args, specs)), *(pinned(t) for t in tokens))
    return results[0] if len(results) == 1 else results


def columns(start, width):
    return pl.ds(pl.multiple_of(start, width), width)


def pack(name, fragment, plan, ids, x, g, outs, pieces, g_to):
    def kernel(plan_ref, ids_ref, x_ref, g_ref, *rest):
        bufs, gt_ref = rest[: len(outs)], rest[len(outs)]
        gin, tok, sems = rest[len(outs) + 1 :]
        _, _, _, z, y = place()
        s = lax.rem(plan_ref[0], 2)
        layers = (s, 1 - s)
        first = [
            pltpu.make_async_copy(ids_ref, tok, sems.at[0]),
            pltpu.make_async_copy(g_ref.at[layers[fragment]], gin, sems.at[1]),
        ]
        copies = []
        for layer, start, width, out, at in pieces:
            col = pl.multiple_of(start(z, y), HALF)
            copies.append(
                pltpu.make_async_copy(
                    x_ref.at[layers[layer], :, pl.ds(col, width)],
                    bufs[out].at[:, pl.ds(at, width)],
                    sems.at[2 + len(copies)],
                )
            )
        for c in first + copies:
            c.start()
        for c in first:
            c.wait()
        gt = (gin[...].astype(F32).T * (tok[...] != 0).astype(F32)).astype(BF16)
        gt_ref[...] = gt
        for out, at in g_to:
            for h in range(2):
                bufs[out][:, at + h * TOK : at + (h + 1) * TOK] = gt[h * TOK : (h + 1) * TOK]
        for c in copies:
            c.wait()

    return call(
        kernel,
        [in_vmem(TOK, n) for n in outs] + [in_vmem(KV, TOK)],
        (plan, ids, x, g),
        [SM, HBM, HBM, HBM],
        [VM] * (len(outs) + 1),
        [
            pltpu.VMEM((TOK, KV), BF16),
            pltpu.VMEM((1, TOK), jnp.int32),
            pltpu.SemaphoreType.DMA((2 + len(pieces),)),
        ],
        name=name,
        vmem=BIG,
    )


def pack_all(plan, ids, x, g):
    def sync(far, flip_y, offset, out, at):
        return (0, lambda z, y: ((1 - z if far else z) * 4 + (y ^ flip_y)) * ROWS + offset, HALF, out, at * HALF)

    def other(j, out, at):
        return (1, lambda z, y: ((1 - z) * 4 + (y ^ j)) * ROWS, ROWS, out, at * ROWS)

    def pair(far, out):
        return [
            sync(far, 1, 0, out, 0),
            sync(far, 2, 0, out, 1),
            sync(far, 3, HALF, out + 1, 0),
            sync(far, 2, HALF, out + 1, 1),
        ]

    wide, half = 2 * HALF + KV, 2 * HALF
    a1, b1, gt_s = pack("pack_1", 0, plan, ids, x, g, [wide, wide], pair(True, 0), [(0, half), (1, half)])
    z1, a2, b2, z3, gt_o = pack(
        "pack_2",
        1,
        plan,
        ids,
        x,
        g,
        [3 * ROWS + KV, half, half, ROWS],
        [other(1, 0, 0), other(2, 0, 1), other(3, 0, 2), *pair(False, 1), other(0, 3, 0)],
        [(0, 3 * ROWS)],
    )
    return a1, b1, z1, a2, b2, z3, gt_s, gt_o


def product(name, fragment, pieces, width, out_shapes, g_at, plan, x, gt, recvs, hint=0):
    count = len(pieces)
    number = len(recvs)
    total = sum(len(p[3]) for p in pieces)

    def kernel(plan_ref, x_ref, gt_ref, *rest):
        recv_refs = rest[:number]
        outs = rest[number : number + len(out_shapes)]
        stage = rest[number + len(out_shapes) : number + 2 * len(out_shapes)]
        gts, xs, sems, out_sems = rest[number + 2 * len(out_shapes) :]
        _, _, _, z, y = place()
        s = lax.rem(plan_ref[0], 2)
        layer = s if fragment == 0 else 1 - s
        g_copies = [
            pltpu.make_async_copy(gt_ref, gts.at[:, pl.ds(0, TOK)], sems.at[2 * count]),
            *(
                pltpu.make_async_copy(
                    recv_refs[0].at[:, pl.ds(g_at + h * TOK, TOK)],
                    gts.at[pl.ds(h * TOK, TOK), pl.ds(TOK, TOK)],
                    sems.at[2 * count + 1 + h],
                )
                for h in range(2)
            ),
        ]
        copies = []
        for p, (own, source, at, _) in enumerate(pieces):
            copies.append(
                (
                    pltpu.make_async_copy(
                        x_ref.at[layer, :, columns(own(z, y), width)], xs.at[p, pl.ds(0, TOK)], sems.at[2 * p]
                    ),
                    pltpu.make_async_copy(
                        recv_refs[source].at[:, pl.ds(at, width)], xs.at[p, pl.ds(TOK, TOK)], sems.at[2 * p + 1]
                    ),
                )
            )
        for c in g_copies:
            c.start()
        for pair in copies:
            for c in pair:
                c.start()
        for c in g_copies:
            c.wait()
        done = []
        for p, (_, _, _, targets) in enumerate(pieces):
            for c in copies[p]:
                c.wait()
            for out, slot, k0, k1 in targets:
                src = stage[out] if slot is None else stage[out].at[slot]
                dst = outs[out] if slot is None else outs[out].at[slot]
                src[...] = jnp.dot(gts[k0:k1], xs[p], preferred_element_type=F32).astype(BF16)
                c = pltpu.make_async_copy(src, dst, out_sems.at[len(done)])
                c.start()
                done.append(c)
        for c in done:
            c.wait()

    return call(
        kernel,
        tuple(shape(*d) for d in out_shapes),
        (plan, x, gt, *recvs),
        [SM, ANY, ANY] + [ANY] * number,
        [ANY] * len(out_shapes),
        [
            *(pltpu.VMEM(d, BF16) for d in out_shapes),
            pltpu.VMEM((KV, 2 * TOK), BF16),
            pltpu.VMEM((count, 2 * TOK, width), BF16),
            pltpu.SemaphoreType.DMA((2 * count + 3,)),
            pltpu.SemaphoreType.DMA((total,)),
        ],
        name=name,
        vmem=BIG,
        hint=hint,
    )


def flip(*terms):
    return sum(t.astype(F32) for t in terms).T


def stepped(w, gradient):
    return (w.astype(F32) * (1.0 - inner_rate * decay_rate) - inner_rate * gradient).astype(BF16)


WORKERS = (16, 2, 32, KV)


def inner_sync(plan, w, near, across):
    def kernel(plan_ref, w_ref, near_ref, z_ref, inner_ref, send_ref, wv, sem, sem2):
        s = lax.rem(plan_ref[0], 2)
        core = place()[2]
        load = pltpu.make_async_copy(w_ref.at[s], wv, sem)
        load.start()
        load.wait()
        for h in range(2):
            for q in range(4):
                cols = pl.ds(q * 128, 128)
                i = h * 8 + q * 2
                gradient = flip(near_ref[h, :, cols], z_ref[h, :, cols])
                inner_ref[i : i + 2] = stepped(wv[i : i + 2].reshape(128, KV), gradient).reshape(2, 2, 32, KV)
        out = pltpu.make_async_copy(inner_ref.at[:, 1 - core], send_ref, sem2)
        out.start()
        out.wait()

    return call(
        kernel,
        (shape(*WORKERS), shape(16, 32, KV)),
        (plan, w, near, across),
        [SM, HBM] + [VM] * 2,
        [VM, ANY],
        [pltpu.VMEM(WORKERS, BF16), pltpu.SemaphoreType.DMA, pltpu.SemaphoreType.DMA],
        name="inner_sync",
    )


def inner_other(plan, w, first, second):
    def kernel(plan_ref, w_ref, *rest):
        k0, r0, l0, k1, r1, l1, inner_ref, send_ref, new_ref, wv, sem, sem2 = rest
        other = 1 - lax.rem(plan_ref[0], 2)
        core = place()[2]
        load = pltpu.make_async_copy(w_ref.at[other], wv, sem)
        load.start()
        load.wait()
        for q in range(8):
            cols = pl.ds(q * 128, 128)
            i = q * 2
            gradient = jnp.concatenate(
                [flip(k[:, cols], r[0, :, cols], l[:, cols]) for k, r, l in ((k0, r0, l0), (k1, r1, l1))], axis=1
            )
            inner_ref[i : i + 2] = stepped(wv[i : i + 2].reshape(128, KV), gradient).reshape(2, 2, 32, KV)
        out = pltpu.make_async_copy(inner_ref.at[:, 1 - core], send_ref, sem2.at[0])
        keep = pltpu.make_async_copy(inner_ref, new_ref.at[other], sem2.at[1])
        out.start()
        keep.start()
        out.wait()
        keep.wait()

    return call(
        kernel,
        (shape(*WORKERS), shape(16, 32, KV), shape(2, *WORKERS)),
        (plan, w, *first, *second),
        [SM, HBM] + [VM] * 6,
        [VM, ANY, ANY],
        [pltpu.VMEM(WORKERS, BF16), pltpu.SemaphoreType.DMA, pltpu.SemaphoreType.DMA((2,))],
        name="inner_other",
    )


def plus(a, b):
    return (a.astype(F32) + b.astype(F32)).astype(BF16)


def to_x(inner_ref, recv_ref, send_ref, keep_ref):
    x, _, core, _, _ = place()
    for ref, at, j in ((send_ref, 0, 1), (send_ref, 1, 2), (keep_ref, 0, 0), (keep_ref, 1, 3)):
        block = pl.ds((x ^ j) * 4, 4)
        ref[at] = plus(inner_ref[block, core], recv_ref[block])


def to_z(keep_ref, recv_ref, send_ref, stay_ref):
    zh = place()[1]
    for ref, at, j in ((send_ref, 0, 1), (send_ref, 1, 2), (stay_ref, 0, 0), (stay_ref, 1, 3)):
        ref[at] = plus(keep_ref[zh ^ j], recv_ref[zh ^ j])


QUAD = (4, 32, KV)


def sums(name, outs, pairs, hint=0):
    def kernel(*refs):
        out_refs = refs[2 * len(pairs) :]
        for i, (_, _, at_a, at_b, out, slot) in enumerate(pairs):
            a, b = refs[2 * i], refs[2 * i + 1]
            total = plus(a[...] if at_a is None else a[at_a], b[...] if at_b is None else b[at_b])
            if slot is None:
                out_refs[out][...] = total
            else:
                out_refs[out][slot] = total

    args = [t for p in pairs for t in p[:2]]
    return call(
        kernel,
        [shape(*d) for d in outs],
        args,
        [VM] * len(args),
        [VM] * len(outs),
        name=name,
        hint=hint,
    )


def halve(name, dims, keep, recv, hint=0):
    return sums(name, [dims] * 2, [(keep, recv, 1, 1, 0, None), (keep, recv, 0, 0, 1, None)], hint)


def sum_x(inner, recv, name):
    return call(to_x, (shape(2, *QUAD),) * 2, (inner, recv), [VM] * 2, [VM] * 2, name=name)


def sum_z(keep, recv, name):
    return call(to_z, (shape(2, 32, KV),) * 2, (keep, recv), [VM] * 2, [VM] * 2, name=name)


def outer_sync(plan, anchors, momentum, keep, recv):
    def kernel(plan_ref, anchor_ref, momentum_ref, a, b, new_ref, moment_ref, short_ref):
        s = lax.rem(plan_ref[0], 2)
        mean = (a[...].astype(F32) + b[...].astype(F32)) / 32
        anchor = anchor_ref[s]
        outer_grad = anchor - mean
        moment = outer_beta * momentum_ref[...] + outer_grad
        new = anchor - outer_rate * (outer_grad + outer_beta * moment)
        new_ref[...] = new
        moment_ref[...] = moment
        for i in range(16):
            short_ref[i] = new.astype(BF16)

    return call(
        kernel,
        (shape(32, KV, dtype=F32), shape(32, KV, dtype=F32), shape(16, 32, KV)),
        (plan, anchors, momentum, keep, recv),
        [SM] + [VM] * 4,
        [VM] * 3,
        name="outer_sync",
        hint=LONG,
    )


def relay(value):
    def kernel(value_ref, out_ref):
        out_ref[...] = value_ref[...]

    return call(kernel, (shape(*value.shape),), (value,), [VM], [VM], name="relay")


def outer_other(plan, anchors, keep, recv):
    def kernel(plan_ref, anchor_ref, a, b, out_ref):
        other = 1 - lax.rem(plan_ref[0], 2)
        out_ref[...] = anchor_ref[other] - (a[...].astype(F32) + b[...].astype(F32)) / 32

    return call(
        kernel,
        (shape(32, KV, dtype=F32),),
        (plan, anchors, keep, recv),
        [SM] + [VM] * 3,
        [VM],
        name="outer_other",
    )


def mix(plan, inner, own, recv, new):
    def kernel(plan_ref, inner_ref, own_ref, recv_ref, _, out_ref, stage, sems):
        s = lax.rem(plan_ref[0], 2)
        core = place()[2]
        for t, c in ((own_ref, core), (recv_ref, 1 - core)):
            stage[:, c] = (
                mix_weight * inner_ref[:, c].astype(F32) + (1.0 - mix_weight) * t[...].astype(F32)
            ).astype(BF16)
        out = pltpu.make_async_copy(stage, out_ref.at[s], sems)
        out.start()
        out.wait()

    return call(
        kernel,
        (shape(2, *WORKERS),),
        (plan, inner, own, recv, new),
        [SM, VM, VM, VM, ANY],
        [ANY],
        [pltpu.VMEM(WORKERS, BF16), pltpu.SemaphoreType.DMA],
        aliases={4: 0},
        name="mix",
    )


def along_fsdp(move):
    return [(z * 4 + y, move(z, y)) for z in range(2) for y in range(4)]


def along_worker(move):
    def index(x, z, c):
        return (x * 4 + z) * 2 + c

    return [(index(x, z, c), index(*move(x, z, c))) for x in range(4) for z in range(4) for c in range(2)]


MOVES = {
    "a": ("fsdp", along_fsdp(lambda z, y: z * 4 + (y ^ 1))),
    "b": ("fsdp", along_fsdp(lambda z, y: z * 4 + (y ^ 3))),
    "z": ("fsdp", along_fsdp(lambda z, y: (1 - z) * 4 + y)),
    "core": ("worker", along_worker(lambda x, z, c: (x, z, 1 - c))),
    "x1": ("worker", along_worker(lambda x, z, c: (x ^ 1, z, c))),
    "x3": ("worker", along_worker(lambda x, z, c: (x ^ 3, z, c))),
    "z1": ("worker", along_worker(lambda x, z, c: (x, z ^ 1, c))),
    "z3": ("worker", along_worker(lambda x, z, c: (x, z ^ 3, c))),
}


PLANES = [[i * 2 + c for i in range(16)] for c in range(2)]


def exchange(value):
    return lax.all_to_all(value, "worker", 0, 0, axis_index_groups=PLANES, tiled=True)


def swap(value, move):
    return lax.ppermute(value, *MOVES[move])


def body(token_ids, layer_inputs, key_grads, weights, anchors, momentum, plan):
    CHAIN.token = None
    x = layer_inputs
    w = weights.reshape(2, *WORKERS)
    a1, b1, z1, a2, b2, z3, gt_s, gt_o = pack_all(plan, token_ids.reshape(1, TOK), x, key_grads)
    got_a1 = swap(a1, "a")
    got_b1 = swap(b1, "b")
    got_z1 = swap(z1, "z")
    got_a2 = swap(a2, "a")
    got_b2 = swap(b2, "b")
    got_z3 = swap(z3, "z")

    def tile(name, far, flip_y, offset, at, recvs, hint=0):
        piece = (
            lambda z, y: ((1 - z if far else z) * 4 + (y ^ flip_y)) * ROWS + offset,
            len(recvs) - 1,
            at * HALF,
            [(0, None, 0, KV)],
        )
        return product(name, 0, [piece], HALF, [(KV, HALF)], 2 * HALF, plan, x, gt_s, recvs, hint)

    def dest(j, source, at, targets):
        return (lambda z, y: (z * 4 + (y ^ j)) * ROWS, source, at, targets)

    def other(name, pieces, outs, recvs, hint=0):
        return product(name, 1, pieces, ROWS, outs, 3 * ROWS, plan, x, gt_o, recvs, hint)

    lo, hi = (0, 256), (256, 512)
    half, pair = (256, ROWS), (2, 256, ROWS)

    far_a = swap(tile("send_a1", True, 3, 0, 1, (got_a1,)), "b")
    far_b = swap(tile("send_b1", True, 1, HALF, 1, (got_b1,)), "a")
    keep_a1 = tile("keep_a1", True, 0, 0, 0, (got_a1,))
    keep_b1 = tile("keep_b1", True, 0, HALF, 0, (got_b1,))
    near_a = swap(tile("send_a2", False, 3, 0, 1, (got_a1, got_a2)), "b")
    near_b = swap(tile("send_b2", False, 1, HALF, 1, (got_b1, got_b2)), "a")
    keep_a2 = tile("keep_a2", False, 0, 0, 0, (got_a1, got_a2))
    keep_b2 = tile("keep_b2", False, 0, HALF, 0, (got_b1, got_b2), 2 * LONG)
    across = swap(
        sums("far", [(2, KV, HALF)], [(keep_a1, far_a, None, None, 0, 0), (keep_b1, far_b, None, None, 0, 1)]), "z"
    )
    send_0, send_1, stay_0, stay_1 = other(
        "other_1",
        [
            dest(2, 0, ROWS, [(0, 1, *lo), (1, 1, *hi)]),
            dest(1, 0, 0, [(0, 0, *lo), (3, None, *hi)]),
            dest(3, 0, 2 * ROWS, [(1, 0, *hi), (2, None, *lo)]),
        ],
        [pair, pair, half, half],
        (got_z1,),
        LONG,
    )
    got_0, got_1 = swap(send_0, "a"), swap(send_1, "b")
    near = sums("near", [(2, KV, HALF)], [(keep_a2, near_a, None, None, 0, 0), (keep_b2, near_b, None, None, 0, 1)])

    inner_s, send_s = inner_sync(plan, w, near, across)
    send, keep = sum_x(inner_s, swap(send_s, "core"), "sync_x1")
    recv = swap(send, "x1")
    last_0, last_1 = sums(
        "last", [half, half], [(stay_0, got_0, None, 1, 0, None), (stay_1, got_1, None, 1, 1, None)]
    )
    last_0, last_1 = swap(last_0, "b"), swap(last_1, "a")
    send, keep = halve("sync_x3", QUAD, keep, recv)
    send, keep = sum_z(keep, swap(send, "x3"), "sync_z1")
    recv = swap(send, "z1")
    mine_0, mine_1 = other("other_3", [dest(0, 1, 0, [(0, None, *lo), (1, None, *hi)])], [half, half], (got_z1, got_z3), SHORT)
    inner_o, send_o, new = inner_other(plan, w, (mine_0, got_0, last_0), (mine_1, got_1, last_1))
    core_o = swap(send_o, "core")
    send, keep = halve("sync_z3", (32, KV), keep, recv, LONG)
    recv = swap(send, "z3")
    send_o, keep_o = sum_x(inner_o, core_o, "other_x1")
    recv_o = swap(send_o, "x1")
    anchor_new, momentum_new, short = outer_sync(plan, anchors, momentum, keep, recv)
    block = exchange(short)
    send_o, keep_o = halve("other_x3", QUAD, keep_o, recv_o, LONG)
    recv_o = swap(send_o, "x3")
    send_o, keep_o = sum_z(keep_o, recv_o, "other_z1")
    recv_o = swap(send_o, "z1")
    block = relay(block)
    send_o, keep_o = halve("other_z3", (32, KV), keep_o, recv_o, LONG)
    recv_o = swap(send_o, "z3")
    new = mix(plan, inner_s, block, swap(block, "core"), new)
    pending = outer_other(plan, anchors, keep_o, recv_o)
    return (new.reshape(1, 2, ROWS, KV), anchor_new, momentum_new, pending)


def solution(mesh):
    return jax.shard_map(
        body,
        mesh=mesh,
        in_specs=(
            P(("worker", "fsdp")),
            P(None, ("worker", "fsdp"), None),
            P(None, ("worker", "fsdp"), None),
            P("worker", None, "fsdp", None),
            P(None, ("fsdp", "worker"), None),
            P(("fsdp", "worker"), None),
            P(),
        ),
        out_specs=(
            P("worker", None, "fsdp", None),
            P(("fsdp", "worker"), None),
            P(("fsdp", "worker"), None),
            P(("fsdp", "worker"), None),
        ),
        check_vma=False,
    )
```

```python
import jax
import jax.numpy as jnp
from jax import lax
from jax.experimental import pallas as pl
from jax.experimental.pallas import tpu as pltpu
from jax.sharding import PartitionSpec as P

inner_rate = 0.25
decay_rate = 0.1
outer_rate = 0.7
outer_beta = 0.9
mix_weight = 0.5

TOK = 256
KV = 512
ROWS = 1024
HALF = 512
F32 = jnp.float32
BF16 = jnp.bfloat16

HBM = pl.BlockSpec(memory_space=pltpu.HBM)
ANY = pl.BlockSpec(memory_space=pl.ANY)
VM = pl.BlockSpec(memory_space=pltpu.VMEM)
SM = pl.BlockSpec(memory_space=pltpu.SMEM)
MIB = 1024 * 1024
BIG = 24
LONG = 2 * 10**10
SHORT = 3 * 10**9


def place():
    w = lax.axis_index("worker")
    f = lax.axis_index("fsdp")
    return w // 8, (w // 2) % 4, w % 2, f // 4, f % 4


def shape(*dims, dtype=BF16):
    return jax.ShapeDtypeStruct(dims, dtype)


def in_vmem(*dims):
    return pltpu.VMEM(dims, BF16)


def in_hbm(*dims):
    return pltpu.HBM(dims, BF16)


def pinned(value):
    return pltpu.with_memory_space_constraint(value, pltpu.HBM)


class Chain:
    def __init__(self):
        self.token = None


CHAIN = Chain()


def call(kernel, outs, args, specs, out_specs, scratch=(), aliases=None, name=None, vmem=16, hint=0):
    outs, out_specs = list(outs), list(out_specs)
    tokens = [] if CHAIN.token is None else [CHAIN.token]
    count = len(args)

    def chained(*refs):
        rest = refs[count + len(tokens) :]
        kernel(*refs[:count], *rest[: len(outs)], *rest[len(outs) + 1 :])

    *results, CHAIN.token = pl.pallas_call(
        chained,
        out_shape=outs + [in_hbm(8, 128)],
        in_specs=list(specs) + [HBM] * len(tokens),
        out_specs=out_specs + [HBM],
        scratch_shapes=list(scratch),
        compiler_params=pltpu.CompilerParams(vmem_limit_bytes=vmem * MIB),
        cost_estimate=pl.CostEstimate(flops=hint, bytes_accessed=0, transcendentals=0),
        input_output_aliases=aliases or {},
        name=name,
    )(*(pinned(a) if spec is HBM else a for a, spec in zip(args, specs)), *(pinned(t) for t in tokens))
    return results[0] if len(results) == 1 else results


def columns(start, width):
    return pl.ds(pl.multiple_of(start, width), width)


def pack(name, fragment, plan, ids, x, g, outs, pieces, g_to):
    def kernel(plan_ref, ids_ref, x_ref, g_ref, *rest):
        bufs, gt_ref = rest[: len(outs)], rest[len(outs)]
        gin, tok, sems = rest[len(outs) + 1 :]
        _, _, _, z, y = place()
        s = lax.rem(plan_ref[0], 2)
        layers = (s, 1 - s)
        first = [
            pltpu.make_async_copy(ids_ref, tok, sems.at[0]),
            pltpu.make_async_copy(g_ref.at[layers[fragment]], gin, sems.at[1]),
        ]
        copies = []
        for layer, start, width, out, at in pieces:
            col = pl.multiple_of(start(z, y), HALF)
            copies.append(
                pltpu.make_async_copy(
                    x_ref.at[layers[layer], :, pl.ds(col, width)],
                    bufs[out].at[:, pl.ds(at, width)],
                    sems.at[2 + len(copies)],
                )
            )
        for c in first + copies:
            c.start()
        for c in first:
            c.wait()
        gt = (gin[...].astype(F32).T * (tok[...] != 0).astype(F32)).astype(BF16)
        gt_ref[...] = gt
        for out, at in g_to:
            for h in range(2):
                bufs[out][:, at + h * TOK : at + (h + 1) * TOK] = gt[h * TOK : (h + 1) * TOK]
        for c in copies:
            c.wait()

    return call(
        kernel,
        [in_vmem(TOK, n) for n in outs] + [in_vmem(KV, TOK)],
        (plan, ids, x, g),
        [SM, HBM, HBM, HBM],
        [VM] * (len(outs) + 1),
        [
            pltpu.VMEM((TOK, KV), BF16),
            pltpu.VMEM((1, TOK), jnp.int32),
            pltpu.SemaphoreType.DMA((2 + len(pieces),)),
        ],
        name=name,
        vmem=BIG,
    )


def pack_all(plan, ids, x, g):
    def sync(far, flip_y, offset, out, at):
        return (0, lambda z, y: ((1 - z if far else z) * 4 + (y ^ flip_y)) * ROWS + offset, HALF, out, at * HALF)

    def other(j, out, at):
        return (1, lambda z, y: ((1 - z) * 4 + (y ^ j)) * ROWS, ROWS, out, at * ROWS)

    def pair(far, out):
        return [
            sync(far, 1, 0, out, 0),
            sync(far, 2, 0, out, 1),
            sync(far, 3, HALF, out + 1, 0),
            sync(far, 2, HALF, out + 1, 1),
        ]

    wide, half = 2 * HALF + KV, 2 * HALF
    a1, b1, gt_s = pack("pack_1", 0, plan, ids, x, g, [wide, wide], pair(True, 0), [(0, half), (1, half)])
    z1, a2, b2, z3, gt_o = pack(
        "pack_2",
        1,
        plan,
        ids,
        x,
        g,
        [3 * ROWS + KV, half, half, ROWS],
        [other(1, 0, 0), other(2, 0, 1), other(3, 0, 2), *pair(False, 1), other(0, 3, 0)],
        [(0, 3 * ROWS)],
    )
    return a1, b1, z1, a2, b2, z3, gt_s, gt_o


def product(name, fragment, pieces, width, out_shapes, g_at, plan, x, gt, recvs, hint=0):
    count = len(pieces)
    number = len(recvs)
    total = sum(len(p[3]) for p in pieces)

    def kernel(plan_ref, x_ref, gt_ref, *rest):
        recv_refs = rest[:number]
        outs = rest[number : number + len(out_shapes)]
        stage = rest[number + len(out_shapes) : number + 2 * len(out_shapes)]
        gts, xs, sems, out_sems = rest[number + 2 * len(out_shapes) :]
        _, _, _, z, y = place()
        s = lax.rem(plan_ref[0], 2)
        layer = s if fragment == 0 else 1 - s
        g_copies = [
            pltpu.make_async_copy(gt_ref, gts.at[:, pl.ds(0, TOK)], sems.at[2 * count]),
            *(
                pltpu.make_async_copy(
                    recv_refs[0].at[:, pl.ds(g_at + h * TOK, TOK)],
                    gts.at[pl.ds(h * TOK, TOK), pl.ds(TOK, TOK)],
                    sems.at[2 * count + 1 + h],
                )
                for h in range(2)
            ),
        ]
        copies = []
        for p, (own, source, at, _) in enumerate(pieces):
            copies.append(
                (
                    pltpu.make_async_copy(
                        x_ref.at[layer, :, columns(own(z, y), width)], xs.at[p, pl.ds(0, TOK)], sems.at[2 * p]
                    ),
                    pltpu.make_async_copy(
                        recv_refs[source].at[:, pl.ds(at, width)], xs.at[p, pl.ds(TOK, TOK)], sems.at[2 * p + 1]
                    ),
                )
            )
        for c in g_copies:
            c.start()
        for pair in copies:
            for c in pair:
                c.start()
        for c in g_copies:
            c.wait()
        done = []
        for p, (_, _, _, targets) in enumerate(pieces):
            for c in copies[p]:
                c.wait()
            for out, slot, k0, k1 in targets:
                src = stage[out] if slot is None else stage[out].at[slot]
                dst = outs[out] if slot is None else outs[out].at[slot]
                src[...] = jnp.dot(gts[k0:k1], xs[p], preferred_element_type=F32).astype(BF16)
                c = pltpu.make_async_copy(src, dst, out_sems.at[len(done)])
                c.start()
                done.append(c)
        for c in done:
            c.wait()

    return call(
        kernel,
        tuple(shape(*d) for d in out_shapes),
        (plan, x, gt, *recvs),
        [SM, ANY, ANY] + [ANY] * number,
        [ANY] * len(out_shapes),
        [
            *(pltpu.VMEM(d, BF16) for d in out_shapes),
            pltpu.VMEM((KV, 2 * TOK), BF16),
            pltpu.VMEM((count, 2 * TOK, width), BF16),
            pltpu.SemaphoreType.DMA((2 * count + 3,)),
            pltpu.SemaphoreType.DMA((total,)),
        ],
        name=name,
        vmem=BIG,
        hint=hint,
    )


def flip(*terms):
    return sum(t.astype(F32) for t in terms).T


def stepped(w, gradient):
    return (w.astype(F32) * (1.0 - inner_rate * decay_rate) - inner_rate * gradient).astype(BF16)


WORKERS = (16, 2, 32, KV)


def take(plan, w):
    def kernel(plan_ref, w_ref, sync_ref, other_ref, sems):
        s = lax.rem(plan_ref[0], 2)
        copies = [
            pltpu.make_async_copy(w_ref.at[layer], out, sems.at[i])
            for i, (layer, out) in enumerate(((s, sync_ref), (1 - s, other_ref)))
        ]
        for c in copies:
            c.start()
        for c in copies:
            c.wait()

    return call(
        kernel,
        (in_vmem(*WORKERS),) * 2,
        (plan, w),
        [SM, HBM],
        [VM] * 2,
        [pltpu.SemaphoreType.DMA((2,))],
        name="take",
    )


def inner_sync(w, near, across):
    def kernel(w_ref, near_ref, z_ref, inner_ref, send_ref, sem):
        for h in range(2):
            for q in range(4):
                cols = pl.ds(q * 128, 128)
                i = h * 8 + q * 2
                gradient = flip(near_ref[h, :, cols], z_ref[h, :, cols])
                inner_ref[i : i + 2] = stepped(w_ref[i : i + 2].reshape(128, KV), gradient).reshape(2, 2, 32, KV)
        out = pltpu.make_async_copy(inner_ref.at[:, 1 - place()[2]], send_ref, sem)
        out.start()
        out.wait()

    return call(
        kernel,
        (shape(*WORKERS), shape(16, 32, KV)),
        (w, near, across),
        [VM] * 3,
        [VM, ANY],
        [pltpu.SemaphoreType.DMA],
        name="inner_sync",
    )


def inner_other(w, first, second):
    def kernel(w_ref, k0, r0, l0, k1, r1, l1, inner_ref, send_ref, sem):
        for q in range(8):
            cols = pl.ds(q * 128, 128)
            i = q * 2
            gradient = jnp.concatenate(
                [flip(k[:, cols], r[0, :, cols], l[:, cols]) for k, r, l in ((k0, r0, l0), (k1, r1, l1))], axis=1
            )
            inner_ref[i : i + 2] = stepped(w_ref[i : i + 2].reshape(128, KV), gradient).reshape(2, 2, 32, KV)
        out = pltpu.make_async_copy(inner_ref.at[:, 1 - place()[2]], send_ref, sem)
        out.start()
        out.wait()

    return call(
        kernel,
        (shape(*WORKERS), shape(16, 32, KV)),
        (w, *first, *second),
        [VM] * 7,
        [VM, ANY],
        [pltpu.SemaphoreType.DMA],
        name="inner_other",
    )


def store(plan, inner):
    def kernel(plan_ref, inner_ref, new_ref, sem):
        out = pltpu.make_async_copy(inner_ref, new_ref.at[1 - lax.rem(plan_ref[0], 2)], sem)
        out.start()
        out.wait()

    return call(
        kernel,
        (shape(2, *WORKERS),),
        (plan, inner),
        [SM, VM],
        [ANY],
        [pltpu.SemaphoreType.DMA],
        name="store",
    )


def plus(a, b):
    return (a.astype(F32) + b.astype(F32)).astype(BF16)


def to_x(inner_ref, recv_ref, send_ref, keep_ref):
    x, _, core, _, _ = place()
    for ref, at, j in ((send_ref, 0, 1), (send_ref, 1, 2), (keep_ref, 0, 0), (keep_ref, 1, 3)):
        block = pl.ds((x ^ j) * 4, 4)
        ref[at] = plus(inner_ref[block, core], recv_ref[block])


def to_z(keep_ref, recv_ref, send_ref, stay_ref):
    zh = place()[1]
    for ref, at, j in ((send_ref, 0, 1), (send_ref, 1, 2), (stay_ref, 0, 0), (stay_ref, 1, 3)):
        ref[at] = plus(keep_ref[zh ^ j], recv_ref[zh ^ j])


QUAD = (4, 32, KV)


def sums(name, outs, pairs, hint=0):
    def kernel(*refs):
        out_refs = refs[2 * len(pairs) :]
        for i, (_, _, at_a, at_b, out, slot) in enumerate(pairs):
            a, b = refs[2 * i], refs[2 * i + 1]
            total = plus(a[...] if at_a is None else a[at_a], b[...] if at_b is None else b[at_b])
            if slot is None:
                out_refs[out][...] = total
            else:
                out_refs[out][slot] = total

    args = [t for p in pairs for t in p[:2]]
    return call(
        kernel,
        [shape(*d) for d in outs],
        args,
        [VM] * len(args),
        [VM] * len(outs),
        name=name,
        hint=hint,
    )


def halve(name, dims, keep, recv, hint=0):
    return sums(name, [dims] * 2, [(keep, recv, 1, 1, 0, None), (keep, recv, 0, 0, 1, None)], hint)


def sum_x(inner, recv, name):
    return call(to_x, (shape(2, *QUAD),) * 2, (inner, recv), [VM] * 2, [VM] * 2, name=name)


def sum_z(keep, recv, name):
    return call(to_z, (shape(2, 32, KV),) * 2, (keep, recv), [VM] * 2, [VM] * 2, name=name)


def outer_sync(plan, anchors, momentum, keep, recv):
    def kernel(plan_ref, anchor_ref, momentum_ref, a, b, new_ref, moment_ref, short_ref):
        s = lax.rem(plan_ref[0], 2)
        mean = (a[...].astype(F32) + b[...].astype(F32)) / 32
        anchor = anchor_ref[s]
        outer_grad = anchor - mean
        moment = outer_beta * momentum_ref[...] + outer_grad
        new = anchor - outer_rate * (outer_grad + outer_beta * moment)
        new_ref[...] = new
        moment_ref[...] = moment
        for i in range(16):
            short_ref[i] = new.astype(BF16)

    return call(
        kernel,
        (shape(32, KV, dtype=F32), shape(32, KV, dtype=F32), shape(16, 32, KV)),
        (plan, anchors, momentum, keep, recv),
        [SM] + [VM] * 4,
        [VM] * 3,
        name="outer_sync",
        hint=LONG,
    )


def relay(value):
    def kernel(value_ref, out_ref):
        out_ref[...] = value_ref[...]

    return call(kernel, (shape(*value.shape),), (value,), [VM], [VM], name="relay")


def outer_other(plan, anchors, keep, recv):
    def kernel(plan_ref, anchor_ref, a, b, out_ref):
        other = 1 - lax.rem(plan_ref[0], 2)
        out_ref[...] = anchor_ref[other] - (a[...].astype(F32) + b[...].astype(F32)) / 32

    return call(
        kernel,
        (shape(32, KV, dtype=F32),),
        (plan, anchors, keep, recv),
        [SM] + [VM] * 3,
        [VM],
        name="outer_other",
        hint=LONG,
    )


def mix(plan, inner, rows, new, far):
    def kernel(plan_ref, inner_ref, rows_ref, _, out_ref, stage, sem):
        core = place()[2]
        c = 1 - core if far else core
        stage[...] = (
            mix_weight * inner_ref[:, c].astype(F32) + (1.0 - mix_weight) * rows_ref[...].astype(F32)
        ).astype(BF16)
        out = pltpu.make_async_copy(stage, out_ref.at[lax.rem(plan_ref[0], 2), :, c], sem)
        out.start()
        out.wait()

    return call(
        kernel,
        (shape(2, *WORKERS),),
        (plan, inner, rows, new),
        [SM, VM, VM, ANY],
        [ANY],
        [pltpu.VMEM((16, 32, KV), BF16), pltpu.SemaphoreType.DMA],
        aliases={3: 0},
        name="mix_far" if far else "mix_own",
    )


def along_fsdp(move):
    return [(z * 4 + y, move(z, y)) for z in range(2) for y in range(4)]


def along_worker(move):
    def index(x, z, c):
        return (x * 4 + z) * 2 + c

    return [(index(x, z, c), index(*move(x, z, c))) for x in range(4) for z in range(4) for c in range(2)]


MOVES = {
    "a": ("fsdp", along_fsdp(lambda z, y: z * 4 + (y ^ 1))),
    "b": ("fsdp", along_fsdp(lambda z, y: z * 4 + (y ^ 3))),
    "z": ("fsdp", along_fsdp(lambda z, y: (1 - z) * 4 + y)),
    "core": ("worker", along_worker(lambda x, z, c: (x, z, 1 - c))),
    "x1": ("worker", along_worker(lambda x, z, c: (x ^ 1, z, c))),
    "x3": ("worker", along_worker(lambda x, z, c: (x ^ 3, z, c))),
    "z1": ("worker", along_worker(lambda x, z, c: (x, z ^ 1, c))),
    "z3": ("worker", along_worker(lambda x, z, c: (x, z ^ 3, c))),
}


PLANES = [[i * 2 + c for i in range(16)] for c in range(2)]


def exchange(value):
    return lax.all_to_all(value, "worker", 0, 0, axis_index_groups=PLANES, tiled=True)


def swap(value, move):
    return lax.ppermute(value, *MOVES[move])


def body(token_ids, layer_inputs, key_grads, weights, anchors, momentum, plan):
    CHAIN.token = None
    x = layer_inputs
    w = weights.reshape(2, *WORKERS)
    a1, b1, z1, a2, b2, z3, gt_s, gt_o = pack_all(plan, token_ids.reshape(1, TOK), x, key_grads)
    got_a1 = swap(a1, "a")
    got_b1 = swap(b1, "b")
    got_z1 = swap(z1, "z")
    got_a2 = swap(a2, "a")
    got_b2 = swap(b2, "b")
    got_z3 = swap(z3, "z")

    def tile(name, far, flip_y, offset, at, recvs, hint=0):
        piece = (
            lambda z, y: ((1 - z if far else z) * 4 + (y ^ flip_y)) * ROWS + offset,
            len(recvs) - 1,
            at * HALF,
            [(0, None, 0, KV)],
        )
        return product(name, 0, [piece], HALF, [(KV, HALF)], 2 * HALF, plan, x, gt_s, recvs, hint)

    def dest(j, source, at, targets):
        return (lambda z, y: (z * 4 + (y ^ j)) * ROWS, source, at, targets)

    def other(name, pieces, outs, recvs, hint=0):
        return product(name, 1, pieces, ROWS, outs, 3 * ROWS, plan, x, gt_o, recvs, hint)

    lo, hi = (0, 256), (256, 512)
    half, pair = (256, ROWS), (2, 256, ROWS)

    far_a = swap(tile("send_a1", True, 3, 0, 1, (got_a1,)), "b")
    far_b = swap(tile("send_b1", True, 1, HALF, 1, (got_b1,)), "a")
    keep_a1 = tile("keep_a1", True, 0, 0, 0, (got_a1,))
    keep_b1 = tile("keep_b1", True, 0, HALF, 0, (got_b1,))
    near_a = swap(tile("send_a2", False, 3, 0, 1, (got_a1, got_a2)), "b")
    near_b = swap(tile("send_b2", False, 1, HALF, 1, (got_b1, got_b2)), "a")
    keep_a2 = tile("keep_a2", False, 0, 0, 0, (got_a1, got_a2))
    keep_b2 = tile("keep_b2", False, 0, HALF, 0, (got_b1, got_b2), 2 * LONG)
    across = swap(
        sums("far", [(2, KV, HALF)], [(keep_a1, far_a, None, None, 0, 0), (keep_b1, far_b, None, None, 0, 1)]), "z"
    )
    send_0, send_1, stay_0, stay_1 = other(
        "other_1",
        [
            dest(2, 0, ROWS, [(0, 1, *lo), (1, 1, *hi)]),
            dest(1, 0, 0, [(0, 0, *lo), (3, None, *hi)]),
            dest(3, 0, 2 * ROWS, [(1, 0, *hi), (2, None, *lo)]),
        ],
        [pair, pair, half, half],
        (got_z1,),
        LONG,
    )
    got_0, got_1 = swap(send_0, "a"), swap(send_1, "b")
    near = sums("near", [(2, KV, HALF)], [(keep_a2, near_a, None, None, 0, 0), (keep_b2, near_b, None, None, 0, 1)])

    w_s, w_o = take(plan, w)
    inner_s, send_s = inner_sync(w_s, near, across)
    send, keep = sum_x(inner_s, swap(send_s, "core"), "sync_x1")
    recv = swap(send, "x1")
    last_0, last_1 = sums(
        "last", [half, half], [(stay_0, got_0, None, 1, 0, None), (stay_1, got_1, None, 1, 1, None)]
    )
    last_0, last_1 = swap(last_0, "b"), swap(last_1, "a")
    send, keep = halve("sync_x3", QUAD, keep, recv)
    send, keep = sum_z(keep, swap(send, "x3"), "sync_z1")
    recv = swap(send, "z1")
    mine_0, mine_1 = other("other_3", [dest(0, 1, 0, [(0, None, *lo), (1, None, *hi)])], [half, half], (got_z1, got_z3), SHORT)
    inner_o, send_o = inner_other(w_o, (mine_0, got_0, last_0), (mine_1, got_1, last_1))
    core_o = swap(send_o, "core")
    send, keep = halve("sync_z3", (32, KV), keep, recv, LONG)
    recv = swap(send, "z3")
    new = store(plan, inner_o)
    send_o, keep_o = sum_x(inner_o, core_o, "other_x1")
    recv_o = swap(send_o, "x1")
    anchor_new, momentum_new, short = outer_sync(plan, anchors, momentum, keep, recv)
    block = exchange(short)
    send_o, keep_o = halve("other_x3", QUAD, keep_o, recv_o, LONG)
    recv_o = swap(send_o, "x3")
    send_o, keep_o = sum_z(keep_o, recv_o, "other_z1")
    recv_o = swap(send_o, "z1")
    send_o, keep_o = halve("other_z3", (32, KV), keep_o, recv_o)
    recv_o = swap(send_o, "z3")
    block = relay(block)
    new = mix(plan, inner_s, block, new, 0)
    pending = outer_other(plan, anchors, keep_o, recv_o)
    new = mix(plan, inner_s, swap(block, "core"), new, 1)
    return (new.reshape(1, 2, ROWS, KV), anchor_new, momentum_new, pending)


def solution(mesh):
    return jax.shard_map(
        body,
        mesh=mesh,
        in_specs=(
            P(("worker", "fsdp")),
            P(None, ("worker", "fsdp"), None),
            P(None, ("worker", "fsdp"), None),
            P("worker", None, "fsdp", None),
            P(None, ("fsdp", "worker"), None),
            P(("fsdp", "worker"), None),
            P(),
        ),
        out_specs=(
            P("worker", None, "fsdp", None),
            P(("fsdp", "worker"), None),
            P(("fsdp", "worker"), None),
            P(("fsdp", "worker"), None),
        ),
        check_vma=False,
    )
```

```python
import jax
import jax.numpy as jnp
from jax import lax
from jax.experimental import pallas as pl
from jax.experimental.pallas import tpu as pltpu
from jax.sharding import PartitionSpec as P

inner_rate = 0.25
decay_rate = 0.1
outer_rate = 0.7
outer_beta = 0.9
mix_weight = 0.5

TOK = 256
KV = 512
ROWS = 1024
HALF = 512
F32 = jnp.float32
BF16 = jnp.bfloat16

HBM = pl.BlockSpec(memory_space=pltpu.HBM)
ANY = pl.BlockSpec(memory_space=pl.ANY)
VM = pl.BlockSpec(memory_space=pltpu.VMEM)
SM = pl.BlockSpec(memory_space=pltpu.SMEM)
MIB = 1024 * 1024
BIG = 24
LONG = 2 * 10**10
MIDDLE = 125 * 10**8
SHORT = 3 * 10**9


def place():
    w = lax.axis_index("worker")
    f = lax.axis_index("fsdp")
    return w // 8, (w // 2) % 4, w % 2, f // 4, f % 4


def shape(*dims, dtype=BF16):
    return jax.ShapeDtypeStruct(dims, dtype)


def in_vmem(*dims):
    return pltpu.VMEM(dims, BF16)


def in_hbm(*dims):
    return pltpu.HBM(dims, BF16)


def pinned(value):
    return pltpu.with_memory_space_constraint(value, pltpu.HBM)


class Chain:
    def __init__(self):
        self.token = None


CHAIN = Chain()


def call(kernel, outs, args, specs, out_specs, scratch=(), aliases=None, name=None, vmem=16, hint=0):
    outs, out_specs = list(outs), list(out_specs)
    tokens = [] if CHAIN.token is None else [CHAIN.token]
    count = len(args)

    def chained(*refs):
        rest = refs[count + len(tokens) :]
        kernel(*refs[:count], *rest[: len(outs)], *rest[len(outs) + 1 :])

    *results, CHAIN.token = pl.pallas_call(
        chained,
        out_shape=outs + [in_hbm(8, 128)],
        in_specs=list(specs) + [HBM] * len(tokens),
        out_specs=out_specs + [HBM],
        scratch_shapes=list(scratch),
        compiler_params=pltpu.CompilerParams(vmem_limit_bytes=vmem * MIB),
        cost_estimate=pl.CostEstimate(flops=hint, bytes_accessed=0, transcendentals=0),
        input_output_aliases=aliases or {},
        name=name,
    )(*(pinned(a) if spec is HBM else a for a, spec in zip(args, specs)), *(pinned(t) for t in tokens))
    return results[0] if len(results) == 1 else results


def columns(start, width):
    return pl.ds(pl.multiple_of(start, width), width)


def pack(name, fragment, plan, ids, x, g, outs, pieces, g_to):
    def kernel(plan_ref, ids_ref, x_ref, g_ref, *rest):
        bufs = rest[: len(outs)]
        sems = rest[-1]
        _, _, _, z, y = place()
        s = lax.rem(plan_ref[0], 2)
        layers = (s, 1 - s)
        copies = []
        for layer, start, width, out, at in pieces:
            col = pl.multiple_of(start(z, y), HALF)
            copies.append(
                pltpu.make_async_copy(
                    x_ref.at[layers[layer], :, pl.ds(col, width)],
                    bufs[out].at[:, pl.ds(at, width)],
                    sems.at[2 + len(copies)],
                )
            )
        if fragment is not None:
            gt_ref, gin, tok = rest[len(outs) : -1]
            first = [
                pltpu.make_async_copy(ids_ref, tok, sems.at[0]),
                pltpu.make_async_copy(g_ref.at[layers[fragment]], gin, sems.at[1]),
            ]
            for c in first:
                c.start()
        for c in copies:
            c.start()
        if fragment is not None:
            for c in first:
                c.wait()
            gt = (gin[...].astype(F32).T * (tok[...] != 0).astype(F32)).astype(BF16)
            gt_ref[...] = gt
            for out, at in g_to:
                for h in range(2):
                    bufs[out][:, at + h * TOK : at + (h + 1) * TOK] = gt[h * TOK : (h + 1) * TOK]
        for c in copies:
            c.wait()

    has = fragment is not None
    return call(
        kernel,
        [in_vmem(TOK, n) for n in outs] + [in_vmem(KV, TOK)] * has,
        (plan, ids, x, g),
        [SM, HBM, HBM, HBM],
        [VM] * (len(outs) + has),
        [pltpu.VMEM((TOK, KV), BF16), pltpu.VMEM((1, TOK), jnp.int32)] * has
        + [pltpu.SemaphoreType.DMA((2 + len(pieces),))],
        name=name,
        vmem=BIG,
    )


def pack_all(plan, ids, x, g):
    def sync(far, flip_y, offset, out, at):
        return (0, lambda z, y: ((1 - z if far else z) * 4 + (y ^ flip_y)) * ROWS + offset, HALF, out, at * HALF)

    def other(j, out, at):
        return (1, lambda z, y: ((1 - z) * 4 + (y ^ j)) * ROWS, ROWS, out, at * ROWS)

    def pair(far, out):
        return [
            sync(far, 1, 0, out, 0),
            sync(far, 2, 0, out, 1),
            sync(far, 3, HALF, out + 1, 0),
            sync(far, 2, HALF, out + 1, 1),
        ]

    wide, half = 2 * HALF + KV, 2 * HALF
    a1, b1, gt_s = pack("pack_1", 0, plan, ids, x, g, [wide, wide], pair(True, 0), [(0, half), (1, half)])
    z1, gt_o = pack(
        "pack_2", 1, plan, ids, x, g, [3 * ROWS + KV], [other(1, 0, 0), other(2, 0, 1), other(3, 0, 2)], [(0, 3 * ROWS)]
    )
    a2, b2, z3 = pack("pack_3", None, plan, ids, x, g, [half, half, ROWS], [*pair(False, 0), other(0, 2, 0)], [])
    return a1, b1, z1, a2, b2, z3, gt_s, gt_o


def product(name, fragment, pieces, width, out_shapes, g_at, plan, x, gt, recvs, hint=0):
    count = len(pieces)
    number = len(recvs)
    total = sum(len(p[3]) for p in pieces)

    def kernel(plan_ref, x_ref, gt_ref, *rest):
        recv_refs = rest[:number]
        outs = rest[number : number + len(out_shapes)]
        stage = rest[number + len(out_shapes) : number + 2 * len(out_shapes)]
        gts, xs, sems, out_sems = rest[number + 2 * len(out_shapes) :]
        _, _, _, z, y = place()
        s = lax.rem(plan_ref[0], 2)
        layer = s if fragment == 0 else 1 - s
        g_copies = [
            pltpu.make_async_copy(gt_ref, gts.at[:, pl.ds(0, TOK)], sems.at[2 * count]),
            *(
                pltpu.make_async_copy(
                    recv_refs[0].at[:, pl.ds(g_at + h * TOK, TOK)],
                    gts.at[pl.ds(h * TOK, TOK), pl.ds(TOK, TOK)],
                    sems.at[2 * count + 1 + h],
                )
                for h in range(2)
            ),
        ]
        copies = []
        for p, (own, source, at, _) in enumerate(pieces):
            copies.append(
                (
                    pltpu.make_async_copy(
                        x_ref.at[layer, :, columns(own(z, y), width)], xs.at[p, pl.ds(0, TOK)], sems.at[2 * p]
                    ),
                    pltpu.make_async_copy(
                        recv_refs[source].at[:, pl.ds(at, width)], xs.at[p, pl.ds(TOK, TOK)], sems.at[2 * p + 1]
                    ),
                )
            )
        for c in g_copies:
            c.start()
        for pair in copies:
            for c in pair:
                c.start()
        for c in g_copies:
            c.wait()
        done = []
        for p, (_, _, _, targets) in enumerate(pieces):
            for c in copies[p]:
                c.wait()
            for out, slot, k0, k1 in targets:
                src = stage[out] if slot is None else stage[out].at[slot]
                dst = outs[out] if slot is None else outs[out].at[slot]
                src[...] = jnp.dot(gts[k0:k1], xs[p], preferred_element_type=F32).astype(BF16)
                c = pltpu.make_async_copy(src, dst, out_sems.at[len(done)])
                c.start()
                done.append(c)
        for c in done:
            c.wait()

    return call(
        kernel,
        tuple(shape(*d) for d in out_shapes),
        (plan, x, gt, *recvs),
        [SM, ANY, ANY] + [ANY] * number,
        [ANY] * len(out_shapes),
        [
            *(pltpu.VMEM(d, BF16) for d in out_shapes),
            pltpu.VMEM((KV, 2 * TOK), BF16),
            pltpu.VMEM((count, 2 * TOK, width), BF16),
            pltpu.SemaphoreType.DMA((2 * count + 3,)),
            pltpu.SemaphoreType.DMA((total,)),
        ],
        name=name,
        vmem=BIG,
        hint=hint,
    )


def flip(*terms):
    return sum(t.astype(F32) for t in terms).T


def stepped(w, gradient):
    return (w.astype(F32) * (1.0 - inner_rate * decay_rate) - inner_rate * gradient).astype(BF16)


WORKERS = (16, 2, 32, KV)


def take(plan, w):
    def kernel(plan_ref, w_ref, sync_ref, other_ref, sems):
        s = lax.rem(plan_ref[0], 2)
        copies = [
            pltpu.make_async_copy(w_ref.at[layer], out, sems.at[i])
            for i, (layer, out) in enumerate(((s, sync_ref), (1 - s, other_ref)))
        ]
        for c in copies:
            c.start()
        for c in copies:
            c.wait()

    return call(
        kernel,
        (in_vmem(*WORKERS),) * 2,
        (plan, w),
        [SM, HBM],
        [VM] * 2,
        [pltpu.SemaphoreType.DMA((2,))],
        name="take",
    )


def inner_sync(w, near, across):
    def kernel(w_ref, near_ref, z_ref, inner_ref, send_ref, sem):
        for h in range(2):
            for q in range(4):
                cols = pl.ds(q * 128, 128)
                i = h * 8 + q * 2
                gradient = flip(near_ref[h, :, cols], z_ref[h, :, cols])
                inner_ref[i : i + 2] = stepped(w_ref[i : i + 2].reshape(128, KV), gradient).reshape(2, 2, 32, KV)
        out = pltpu.make_async_copy(inner_ref.at[:, 1 - place()[2]], send_ref, sem)
        out.start()
        out.wait()

    return call(
        kernel,
        (shape(*WORKERS), shape(16, 32, KV)),
        (w, near, across),
        [VM] * 3,
        [VM, ANY],
        [pltpu.SemaphoreType.DMA],
        name="inner_sync",
    )


def inner_other(w, first, second):
    def kernel(w_ref, k0, r0, l0, k1, r1, l1, inner_ref, send_ref, sem):
        for q in range(8):
            cols = pl.ds(q * 128, 128)
            i = q * 2
            gradient = jnp.concatenate(
                [flip(k[:, cols], r[0, :, cols], l[:, cols]) for k, r, l in ((k0, r0, l0), (k1, r1, l1))], axis=1
            )
            inner_ref[i : i + 2] = stepped(w_ref[i : i + 2].reshape(128, KV), gradient).reshape(2, 2, 32, KV)
        out = pltpu.make_async_copy(inner_ref.at[:, 1 - place()[2]], send_ref, sem)
        out.start()
        out.wait()

    return call(
        kernel,
        (shape(*WORKERS), shape(16, 32, KV)),
        (w, *first, *second),
        [VM] * 7,
        [VM, ANY],
        [pltpu.SemaphoreType.DMA],
        name="inner_other",
    )


def store(plan, inner):
    def kernel(plan_ref, inner_ref, new_ref, sem):
        out = pltpu.make_async_copy(inner_ref, new_ref.at[1 - lax.rem(plan_ref[0], 2)], sem)
        out.start()
        out.wait()

    return call(
        kernel,
        (shape(2, *WORKERS),),
        (plan, inner),
        [SM, VM],
        [ANY],
        [pltpu.SemaphoreType.DMA],
        name="store",
    )


def plus(a, b):
    return (a.astype(F32) + b.astype(F32)).astype(BF16)


def to_x(inner_ref, recv_ref, send_ref, keep_ref):
    x, _, core, _, _ = place()
    for ref, at, j in ((send_ref, 0, 1), (send_ref, 1, 2), (keep_ref, 0, 0), (keep_ref, 1, 3)):
        block = pl.ds((x ^ j) * 4, 4)
        ref[at] = plus(inner_ref[block, core], recv_ref[block])


def to_z(keep_ref, recv_ref, send_ref, stay_ref):
    zh = place()[1]
    for ref, at, j in ((send_ref, 0, 1), (send_ref, 1, 2), (stay_ref, 0, 0), (stay_ref, 1, 3)):
        ref[at] = plus(keep_ref[zh ^ j], recv_ref[zh ^ j])


QUAD = (4, 32, KV)


def sums(name, outs, pairs, hint=0):
    def kernel(*refs):
        out_refs = refs[2 * len(pairs) :]
        for i, (_, _, at_a, at_b, out, slot) in enumerate(pairs):
            a, b = refs[2 * i], refs[2 * i + 1]
            total = plus(a[...] if at_a is None else a[at_a], b[...] if at_b is None else b[at_b])
            if slot is None:
                out_refs[out][...] = total
            else:
                out_refs[out][slot] = total

    args = [t for p in pairs for t in p[:2]]
    return call(
        kernel,
        [shape(*d) for d in outs],
        args,
        [VM] * len(args),
        [VM] * len(outs),
        name=name,
        hint=hint,
    )


def halve(name, dims, keep, recv, hint=0):
    return sums(name, [dims] * 2, [(keep, recv, 1, 1, 0, None), (keep, recv, 0, 0, 1, None)], hint)


def sum_x(inner, recv, name):
    return call(to_x, (shape(2, *QUAD),) * 2, (inner, recv), [VM] * 2, [VM] * 2, name=name)


def sum_z(keep, recv, name):
    return call(to_z, (shape(2, 32, KV),) * 2, (keep, recv), [VM] * 2, [VM] * 2, name=name)


def outer_sync(plan, anchors, momentum, keep, recv):
    def kernel(plan_ref, anchor_ref, momentum_ref, a, b, new_ref, moment_ref, short_ref):
        s = lax.rem(plan_ref[0], 2)
        mean = (a[...].astype(F32) + b[...].astype(F32)) / 32
        anchor = anchor_ref[s]
        outer_grad = anchor - mean
        moment = outer_beta * momentum_ref[...] + outer_grad
        new = anchor - outer_rate * (outer_grad + outer_beta * moment)
        new_ref[...] = new
        moment_ref[...] = moment
        for i in range(16):
            short_ref[i] = new.astype(BF16)

    return call(
        kernel,
        (shape(32, KV, dtype=F32), shape(32, KV, dtype=F32), shape(16, 32, KV)),
        (plan, anchors, momentum, keep, recv),
        [SM] + [VM] * 4,
        [VM] * 3,
        name="outer_sync",
        hint=LONG,
    )


def relay(value):
    def kernel(value_ref, out_ref):
        out_ref[...] = value_ref[...]

    return call(kernel, (shape(*value.shape),), (value,), [VM], [VM], name="relay")


def outer_other(plan, anchors, keep, recv):
    def kernel(plan_ref, anchor_ref, a, b, out_ref):
        other = 1 - lax.rem(plan_ref[0], 2)
        out_ref[...] = anchor_ref[other] - (a[...].astype(F32) + b[...].astype(F32)) / 32

    return call(
        kernel,
        (shape(32, KV, dtype=F32),),
        (plan, anchors, keep, recv),
        [SM] + [VM] * 3,
        [VM],
        name="outer_other",
        hint=LONG,
    )


def mix(plan, inner, rows, new, far):
    def kernel(plan_ref, inner_ref, rows_ref, _, out_ref, stage, sem):
        core = place()[2]
        c = 1 - core if far else core
        stage[...] = (
            mix_weight * inner_ref[:, c].astype(F32) + (1.0 - mix_weight) * rows_ref[...].astype(F32)
        ).astype(BF16)
        out = pltpu.make_async_copy(stage, out_ref.at[lax.rem(plan_ref[0], 2), :, c], sem)
        out.start()
        out.wait()

    return call(
        kernel,
        (shape(2, *WORKERS),),
        (plan, inner, rows, new),
        [SM, VM, VM, ANY],
        [ANY],
        [pltpu.VMEM((16, 32, KV), BF16), pltpu.SemaphoreType.DMA],
        aliases={3: 0},
        name="mix_far" if far else "mix_own",
    )


def along_fsdp(move):
    return [(z * 4 + y, move(z, y)) for z in range(2) for y in range(4)]


def along_worker(move):
    def index(x, z, c):
        return (x * 4 + z) * 2 + c

    return [(index(x, z, c), index(*move(x, z, c))) for x in range(4) for z in range(4) for c in range(2)]


MOVES = {
    "a": ("fsdp", along_fsdp(lambda z, y: z * 4 + (y ^ 1))),
    "b": ("fsdp", along_fsdp(lambda z, y: z * 4 + (y ^ 3))),
    "z": ("fsdp", along_fsdp(lambda z, y: (1 - z) * 4 + y)),
    "core": ("worker", along_worker(lambda x, z, c: (x, z, 1 - c))),
    "x1": ("worker", along_worker(lambda x, z, c: (x ^ 1, z, c))),
    "x3": ("worker", along_worker(lambda x, z, c: (x ^ 3, z, c))),
    "z1": ("worker", along_worker(lambda x, z, c: (x, z ^ 1, c))),
    "z3": ("worker", along_worker(lambda x, z, c: (x, z ^ 3, c))),
}


PLANES = [[i * 2 + c for i in range(16)] for c in range(2)]


def exchange(value):
    return lax.all_to_all(value, "worker", 0, 0, axis_index_groups=PLANES, tiled=True)


def swap(value, move):
    return lax.ppermute(value, *MOVES[move])


def body(token_ids, layer_inputs, key_grads, weights, anchors, momentum, plan):
    CHAIN.token = None
    x = layer_inputs
    w = weights.reshape(2, *WORKERS)
    a1, b1, z1, a2, b2, z3, gt_s, gt_o = pack_all(plan, token_ids.reshape(1, TOK), x, key_grads)
    got_a1 = swap(a1, "a")
    got_b1 = swap(b1, "b")
    got_z1 = swap(z1, "z")
    got_a2 = swap(a2, "a")
    got_b2 = swap(b2, "b")
    got_z3 = swap(z3, "z")

    def tile(name, far, flip_y, offset, at, recvs, hint=0):
        piece = (
            lambda z, y: ((1 - z if far else z) * 4 + (y ^ flip_y)) * ROWS + offset,
            len(recvs) - 1,
            at * HALF,
            [(0, None, 0, KV)],
        )
        return product(name, 0, [piece], HALF, [(KV, HALF)], 2 * HALF, plan, x, gt_s, recvs, hint)

    def dest(j, source, at, targets):
        return (lambda z, y: (z * 4 + (y ^ j)) * ROWS, source, at, targets)

    def other(name, pieces, outs, recvs, hint=0):
        return product(name, 1, pieces, ROWS, outs, 3 * ROWS, plan, x, gt_o, recvs, hint)

    lo, hi = (0, 256), (256, 512)
    half, pair = (256, ROWS), (2, 256, ROWS)

    far_a = swap(tile("send_a1", True, 3, 0, 1, (got_a1,)), "b")
    far_b = swap(tile("send_b1", True, 1, HALF, 1, (got_b1,)), "a")
    keep_a1 = tile("keep_a1", True, 0, 0, 0, (got_a1,))
    keep_b1 = tile("keep_b1", True, 0, HALF, 0, (got_b1,))
    near_a = swap(tile("send_a2", False, 3, 0, 1, (got_a1, got_a2)), "b")
    near_b = swap(tile("send_b2", False, 1, HALF, 1, (got_b1, got_b2)), "a")
    keep_a2 = tile("keep_a2", False, 0, 0, 0, (got_a1, got_a2))
    keep_b2 = tile("keep_b2", False, 0, HALF, 0, (got_b1, got_b2), MIDDLE)
    across = swap(
        sums("far", [(2, KV, HALF)], [(keep_a1, far_a, None, None, 0, 0), (keep_b1, far_b, None, None, 0, 1)]), "z"
    )
    send_0, send_1, stay_0, stay_1 = other(
        "other_1",
        [
            dest(2, 0, ROWS, [(0, 1, *lo), (1, 1, *hi)]),
            dest(1, 0, 0, [(0, 0, *lo), (3, None, *hi)]),
            dest(3, 0, 2 * ROWS, [(1, 0, *hi), (2, None, *lo)]),
        ],
        [pair, pair, half, half],
        (got_z1,),
        LONG,
    )
    got_0, got_1 = swap(send_0, "a"), swap(send_1, "b")
    near = sums("near", [(2, KV, HALF)], [(keep_a2, near_a, None, None, 0, 0), (keep_b2, near_b, None, None, 0, 1)])

    w_s, w_o = take(plan, w)
    inner_s, send_s = inner_sync(w_s, near, across)
    send, keep = sum_x(inner_s, swap(send_s, "core"), "sync_x1")
    recv = swap(send, "x1")
    last_0, last_1 = sums(
        "last", [half, half], [(stay_0, got_0, None, 1, 0, None), (stay_1, got_1, None, 1, 1, None)]
    )
    last_0, last_1 = swap(last_0, "b"), swap(last_1, "a")
    send, keep = halve("sync_x3", QUAD, keep, recv)
    recv = swap(send, "x3")
    mine_0, mine_1 = other("other_3", [dest(0, 1, 0, [(0, None, *lo), (1, None, *hi)])], [half, half], (got_z1, got_z3), SHORT)
    send, keep = sum_z(keep, recv, "sync_z1")
    recv = swap(send, "z1")
    inner_o, send_o = inner_other(w_o, (mine_0, got_0, last_0), (mine_1, got_1, last_1))
    core_o = swap(send_o, "core")
    send, keep = halve("sync_z3", (32, KV), keep, recv, LONG)
    recv = swap(send, "z3")
    new = store(plan, inner_o)
    send_o, keep_o = sum_x(inner_o, core_o, "other_x1")
    recv_o = swap(send_o, "x1")
    anchor_new, momentum_new, short = outer_sync(plan, anchors, momentum, keep, recv)
    block = exchange(short)
    send_o, keep_o = halve("other_x3", QUAD, keep_o, recv_o, LONG)
    recv_o = swap(send_o, "x3")
    send_o, keep_o = sum_z(keep_o, recv_o, "other_z1")
    recv_o = swap(send_o, "z1")
    send_o, keep_o = halve("other_z3", (32, KV), keep_o, recv_o)
    recv_o = swap(send_o, "z3")
    block = relay(block)
    new = mix(plan, inner_s, block, new, 0)
    pending = outer_other(plan, anchors, keep_o, recv_o)
    new = mix(plan, inner_s, swap(block, "core"), new, 1)
    return (new.reshape(1, 2, ROWS, KV), anchor_new, momentum_new, pending)


def solution(mesh):
    return jax.shard_map(
        body,
        mesh=mesh,
        in_specs=(
            P(("worker", "fsdp")),
            P(None, ("worker", "fsdp"), None),
            P(None, ("worker", "fsdp"), None),
            P("worker", None, "fsdp", None),
            P(None, ("fsdp", "worker"), None),
            P(("fsdp", "worker"), None),
            P(),
        ),
        out_specs=(
            P("worker", None, "fsdp", None),
            P(("fsdp", "worker"), None),
            P(("fsdp", "worker"), None),
            P(("fsdp", "worker"), None),
        ),
        check_vma=False,
    )
```

```python
import jax
import jax.numpy as jnp
from jax import lax
from jax.experimental import pallas as pl
from jax.experimental.pallas import tpu as pltpu
from jax.sharding import PartitionSpec as P

inner_rate = 0.25
decay_rate = 0.1
outer_rate = 0.7
outer_beta = 0.9
mix_weight = 0.5

TOK = 256
KV = 512
ROWS = 1024
HALF = 512
F32 = jnp.float32
BF16 = jnp.bfloat16

HBM = pl.BlockSpec(memory_space=pltpu.HBM)
ANY = pl.BlockSpec(memory_space=pl.ANY)
VM = pl.BlockSpec(memory_space=pltpu.VMEM)
SM = pl.BlockSpec(memory_space=pltpu.SMEM)
MIB = 1024 * 1024
BIG = 24
LONG = 2 * 10**10
MIDDLE = 125 * 10**8
SHORT = 3 * 10**9


def place():
    w = lax.axis_index("worker")
    f = lax.axis_index("fsdp")
    return w // 8, (w // 2) % 4, w % 2, f // 4, f % 4


def shape(*dims, dtype=BF16):
    return jax.ShapeDtypeStruct(dims, dtype)


def in_vmem(*dims):
    return pltpu.VMEM(dims, BF16)


def in_hbm(*dims):
    return pltpu.HBM(dims, BF16)


def pinned(value):
    return pltpu.with_memory_space_constraint(value, pltpu.HBM)


class Chain:
    def __init__(self):
        self.token = None


CHAIN = Chain()


def call(kernel, outs, args, specs, out_specs, scratch=(), aliases=None, name=None, vmem=16, hint=0):
    outs, out_specs = list(outs), list(out_specs)
    tokens = [] if CHAIN.token is None else [CHAIN.token]
    count = len(args)

    def chained(*refs):
        rest = refs[count + len(tokens) :]
        kernel(*refs[:count], *rest[: len(outs)], *rest[len(outs) + 1 :])

    *results, CHAIN.token = pl.pallas_call(
        chained,
        out_shape=outs + [in_hbm(8, 128)],
        in_specs=list(specs) + [HBM] * len(tokens),
        out_specs=out_specs + [HBM],
        scratch_shapes=list(scratch),
        compiler_params=pltpu.CompilerParams(vmem_limit_bytes=vmem * MIB),
        cost_estimate=pl.CostEstimate(flops=hint, bytes_accessed=0, transcendentals=0),
        input_output_aliases=aliases or {},
        name=name,
    )(*(pinned(a) if spec is HBM else a for a, spec in zip(args, specs)), *(pinned(t) for t in tokens))
    return results[0] if len(results) == 1 else results


def columns(start, width):
    return pl.ds(pl.multiple_of(start, width), width)


def pack(name, fragment, plan, ids, x, g, outs, pieces, g_to):
    def kernel(plan_ref, ids_ref, x_ref, g_ref, *rest):
        bufs = rest[: len(outs)]
        sems = rest[-1]
        _, _, _, z, y = place()
        s = lax.rem(plan_ref[0], 2)
        layers = (s, 1 - s)
        copies = []
        for layer, start, width, out, at in pieces:
            col = pl.multiple_of(start(z, y), HALF)
            copies.append(
                pltpu.make_async_copy(
                    x_ref.at[layers[layer], :, pl.ds(col, width)],
                    bufs[out].at[:, pl.ds(at, width)],
                    sems.at[2 + len(copies)],
                )
            )
        if fragment is not None:
            gt_ref, gin, tok = rest[len(outs) : -1]
            first = [
                pltpu.make_async_copy(ids_ref, tok, sems.at[0]),
                pltpu.make_async_copy(g_ref.at[layers[fragment]], gin, sems.at[1]),
            ]
            for c in first:
                c.start()
        for c in copies:
            c.start()
        if fragment is not None:
            for c in first:
                c.wait()
            gt = (gin[...].astype(F32).T * (tok[...] != 0).astype(F32)).astype(BF16)
            gt_ref[...] = gt
            for out, at in g_to:
                for h in range(2):
                    bufs[out][:, at + h * TOK : at + (h + 1) * TOK] = gt[h * TOK : (h + 1) * TOK]
        for c in copies:
            c.wait()

    has = fragment is not None
    return call(
        kernel,
        [in_vmem(TOK, n) for n in outs] + [in_vmem(KV, TOK)] * has,
        (plan, ids, x, g),
        [SM, HBM, HBM, HBM],
        [VM] * (len(outs) + has),
        [pltpu.VMEM((TOK, KV), BF16), pltpu.VMEM((1, TOK), jnp.int32)] * has
        + [pltpu.SemaphoreType.DMA((2 + len(pieces),))],
        name=name,
        vmem=BIG,
    )


def pack_all(plan, ids, x, g):
    def sync(far, flip_y, offset, out, at):
        return (0, lambda z, y: ((1 - z if far else z) * 4 + (y ^ flip_y)) * ROWS + offset, HALF, out, at * HALF)

    def other(j, out, at):
        return (1, lambda z, y: ((1 - z) * 4 + (y ^ j)) * ROWS, ROWS, out, at * ROWS)

    def pair(far, out):
        return [
            sync(far, 1, 0, out, 0),
            sync(far, 2, 0, out, 1),
            sync(far, 3, HALF, out + 1, 0),
            sync(far, 2, HALF, out + 1, 1),
        ]

    wide, half = 2 * HALF + KV, 2 * HALF
    a1, b1, gt_s = pack("pack_1", 0, plan, ids, x, g, [wide, wide], pair(True, 0), [(0, half), (1, half)])
    z1, gt_o = pack(
        "pack_2", 1, plan, ids, x, g, [3 * ROWS + KV], [other(1, 0, 0), other(2, 0, 1), other(3, 0, 2)], [(0, 3 * ROWS)]
    )
    a2, b2, z3 = pack("pack_3", None, plan, ids, x, g, [half, half, ROWS], [*pair(False, 0), other(0, 2, 0)], [])
    return a1, b1, z1, a2, b2, z3, gt_s, gt_o


def product(name, fragment, pieces, width, out_shapes, g_at, plan, x, gt, recvs, hint=0):
    count = len(pieces)
    number = len(recvs)
    total = sum(len(p[3]) for p in pieces)

    def kernel(plan_ref, x_ref, gt_ref, *rest):
        recv_refs = rest[:number]
        outs = rest[number : number + len(out_shapes)]
        stage = rest[number + len(out_shapes) : number + 2 * len(out_shapes)]
        gts, xs, sems, out_sems = rest[number + 2 * len(out_shapes) :]
        _, _, _, z, y = place()
        s = lax.rem(plan_ref[0], 2)
        layer = s if fragment == 0 else 1 - s
        g_copies = [
            pltpu.make_async_copy(gt_ref, gts.at[:, pl.ds(0, TOK)], sems.at[2 * count]),
            *(
                pltpu.make_async_copy(
                    recv_refs[0].at[:, pl.ds(g_at + h * TOK, TOK)],
                    gts.at[pl.ds(h * TOK, TOK), pl.ds(TOK, TOK)],
                    sems.at[2 * count + 1 + h],
                )
                for h in range(2)
            ),
        ]
        copies = []
        for p, (own, source, at, _) in enumerate(pieces):
            copies.append(
                (
                    pltpu.make_async_copy(
                        x_ref.at[layer, :, columns(own(z, y), width)], xs.at[p, pl.ds(0, TOK)], sems.at[2 * p]
                    ),
                    pltpu.make_async_copy(
                        recv_refs[source].at[:, pl.ds(at, width)], xs.at[p, pl.ds(TOK, TOK)], sems.at[2 * p + 1]
                    ),
                )
            )
        for c in g_copies:
            c.start()
        for pair in copies:
            for c in pair:
                c.start()
        for c in g_copies:
            c.wait()
        done = []
        for p, (_, _, _, targets) in enumerate(pieces):
            for c in copies[p]:
                c.wait()
            for out, slot, k0, k1 in targets:
                src = stage[out] if slot is None else stage[out].at[slot]
                dst = outs[out] if slot is None else outs[out].at[slot]
                src[...] = jnp.dot(gts[k0:k1], xs[p], preferred_element_type=F32).astype(BF16)
                c = pltpu.make_async_copy(src, dst, out_sems.at[len(done)])
                c.start()
                done.append(c)
        for c in done:
            c.wait()

    return call(
        kernel,
        tuple(shape(*d) for d in out_shapes),
        (plan, x, gt, *recvs),
        [SM, ANY, ANY] + [ANY] * number,
        [ANY] * len(out_shapes),
        [
            *(pltpu.VMEM(d, BF16) for d in out_shapes),
            pltpu.VMEM((KV, 2 * TOK), BF16),
            pltpu.VMEM((count, 2 * TOK, width), BF16),
            pltpu.SemaphoreType.DMA((2 * count + 3,)),
            pltpu.SemaphoreType.DMA((total,)),
        ],
        name=name,
        vmem=BIG,
        hint=hint,
    )


def flip(*terms):
    return sum(t.astype(F32) for t in terms).T


def stepped(w, gradient):
    return (w.astype(F32) * (1.0 - inner_rate * decay_rate) - inner_rate * gradient).astype(BF16)


WORKERS = (16, 2, 32, KV)


def take(plan, w):
    def kernel(plan_ref, w_ref, sync_ref, other_ref, sems):
        s = lax.rem(plan_ref[0], 2)
        copies = [
            pltpu.make_async_copy(w_ref.at[layer], out, sems.at[i])
            for i, (layer, out) in enumerate(((s, sync_ref), (1 - s, other_ref)))
        ]
        for c in copies:
            c.start()
        for c in copies:
            c.wait()

    return call(
        kernel,
        (in_vmem(*WORKERS),) * 2,
        (plan, w),
        [SM, HBM],
        [VM] * 2,
        [pltpu.SemaphoreType.DMA((2,))],
        name="take",
    )


def inner_sync(w, near, across):
    def kernel(w_ref, near_ref, z_ref, inner_ref, send_ref, sem):
        for h in range(2):
            for q in range(4):
                cols = pl.ds(q * 128, 128)
                i = h * 8 + q * 2
                gradient = flip(near_ref[h, :, cols], z_ref[h, :, cols])
                inner_ref[i : i + 2] = stepped(w_ref[i : i + 2].reshape(128, KV), gradient).reshape(2, 2, 32, KV)
        out = pltpu.make_async_copy(inner_ref.at[:, 1 - place()[2]], send_ref, sem)
        out.start()
        out.wait()

    return call(
        kernel,
        (shape(*WORKERS), shape(16, 32, KV)),
        (w, near, across),
        [VM] * 3,
        [VM, ANY],
        [pltpu.SemaphoreType.DMA],
        name="inner_sync",
    )


def inner_other(w, first, second):
    def kernel(w_ref, k0, r0, l0, k1, r1, l1, inner_ref, send_ref, sem):
        for q in range(8):
            cols = pl.ds(q * 128, 128)
            i = q * 2
            gradient = jnp.concatenate(
                [flip(k[:, cols], r[0, :, cols], l[:, cols]) for k, r, l in ((k0, r0, l0), (k1, r1, l1))], axis=1
            )
            inner_ref[i : i + 2] = stepped(w_ref[i : i + 2].reshape(128, KV), gradient).reshape(2, 2, 32, KV)
        out = pltpu.make_async_copy(inner_ref.at[:, 1 - place()[2]], send_ref, sem)
        out.start()
        out.wait()

    return call(
        kernel,
        (shape(*WORKERS), shape(16, 32, KV)),
        (w, *first, *second),
        [VM] * 7,
        [VM, ANY],
        [pltpu.SemaphoreType.DMA],
        name="inner_other",
    )


def store(plan, inner):
    def kernel(plan_ref, inner_ref, new_ref, sem):
        out = pltpu.make_async_copy(inner_ref, new_ref.at[1 - lax.rem(plan_ref[0], 2)], sem)
        out.start()
        out.wait()

    return call(
        kernel,
        (shape(2, *WORKERS),),
        (plan, inner),
        [SM, VM],
        [ANY],
        [pltpu.SemaphoreType.DMA],
        name="store",
    )


def plus(a, b):
    return (a.astype(F32) + b.astype(F32)).astype(BF16)


def to_x(inner_ref, recv_ref, send_ref, keep_ref):
    x, _, core, _, _ = place()
    for ref, at, j in ((send_ref, 0, 1), (send_ref, 1, 2), (keep_ref, 0, 0), (keep_ref, 1, 3)):
        block = pl.ds((x ^ j) * 4, 4)
        ref[at] = plus(inner_ref[block, core], recv_ref[block])


def to_z(keep_ref, recv_ref, send_ref, stay_ref):
    zh = place()[1]
    for ref, at, j in ((send_ref, 0, 1), (send_ref, 1, 2), (stay_ref, 0, 0), (stay_ref, 1, 3)):
        ref[at] = plus(keep_ref[zh ^ j], recv_ref[zh ^ j])


QUAD = (4, 32, KV)


def sums(name, outs, pairs, hint=0):
    def kernel(*refs):
        out_refs = refs[2 * len(pairs) :]
        for i, (_, _, at_a, at_b, out, slot) in enumerate(pairs):
            a, b = refs[2 * i], refs[2 * i + 1]
            total = plus(a[...] if at_a is None else a[at_a], b[...] if at_b is None else b[at_b])
            if slot is None:
                out_refs[out][...] = total
            else:
                out_refs[out][slot] = total

    args = [t for p in pairs for t in p[:2]]
    return call(
        kernel,
        [shape(*d) for d in outs],
        args,
        [VM] * len(args),
        [VM] * len(outs),
        name=name,
        hint=hint,
    )


def halve(name, dims, keep, recv, hint=0):
    return sums(name, [dims] * 2, [(keep, recv, 1, 1, 0, None), (keep, recv, 0, 0, 1, None)], hint)


def sum_x(inner, recv, name):
    return call(to_x, (shape(2, *QUAD),) * 2, (inner, recv), [VM] * 2, [VM] * 2, name=name)


def sum_z(keep, recv, name):
    return call(to_z, (shape(2, 32, KV),) * 2, (keep, recv), [VM] * 2, [VM] * 2, name=name)


def outer_sync(plan, anchors, momentum, keep, recv):
    def kernel(plan_ref, anchor_ref, momentum_ref, a, b, new_ref, moment_ref, short_ref):
        s = lax.rem(plan_ref[0], 2)
        mean = (a[...].astype(F32) + b[...].astype(F32)) / 32
        anchor = anchor_ref[s]
        outer_grad = anchor - mean
        moment = outer_beta * momentum_ref[...] + outer_grad
        new = anchor - outer_rate * (outer_grad + outer_beta * moment)
        new_ref[...] = new
        moment_ref[...] = moment
        for i in range(16):
            short_ref[i] = new.astype(BF16)

    return call(
        kernel,
        (shape(32, KV, dtype=F32), shape(32, KV, dtype=F32), shape(16, 32, KV)),
        (plan, anchors, momentum, keep, recv),
        [SM] + [VM] * 4,
        [VM] * 3,
        name="outer_sync",
        hint=LONG,
    )


def relay(value):
    def kernel(value_ref, out_ref):
        out_ref[...] = value_ref[...]

    return call(kernel, (shape(*value.shape),), (value,), [VM], [VM], name="relay")


def outer_other(plan, anchors, keep, recv):
    def kernel(plan_ref, anchor_ref, a, b, out_ref):
        other = 1 - lax.rem(plan_ref[0], 2)
        out_ref[...] = anchor_ref[other] - (a[...].astype(F32) + b[...].astype(F32)) / 32

    return call(
        kernel,
        (shape(32, KV, dtype=F32),),
        (plan, anchors, keep, recv),
        [SM] + [VM] * 3,
        [VM],
        name="outer_other",
        hint=LONG,
    )


def mix(plan, inner, rows, new, far):
    def kernel(plan_ref, inner_ref, rows_ref, _, out_ref, stage, sem):
        core = place()[2]
        c = 1 - core if far else core
        stage[...] = (
            mix_weight * inner_ref[:, c].astype(F32) + (1.0 - mix_weight) * rows_ref[...].astype(F32)
        ).astype(BF16)
        out = pltpu.make_async_copy(stage, out_ref.at[lax.rem(plan_ref[0], 2), :, c], sem)
        out.start()
        out.wait()

    return call(
        kernel,
        (shape(2, *WORKERS),),
        (plan, inner, rows, new),
        [SM, VM, VM, ANY],
        [ANY],
        [pltpu.VMEM((16, 32, KV), BF16), pltpu.SemaphoreType.DMA],
        aliases={3: 0},
        name="mix_far" if far else "mix_own",
    )


def along_fsdp(move):
    return [(z * 4 + y, move(z, y)) for z in range(2) for y in range(4)]


def along_worker(move):
    def index(x, z, c):
        return (x * 4 + z) * 2 + c

    return [(index(x, z, c), index(*move(x, z, c))) for x in range(4) for z in range(4) for c in range(2)]


MOVES = {
    "a": ("fsdp", along_fsdp(lambda z, y: z * 4 + (y ^ 1))),
    "b": ("fsdp", along_fsdp(lambda z, y: z * 4 + (y ^ 3))),
    "z": ("fsdp", along_fsdp(lambda z, y: (1 - z) * 4 + y)),
    "core": ("worker", along_worker(lambda x, z, c: (x, z, 1 - c))),
    "x1": ("worker", along_worker(lambda x, z, c: (x ^ 1, z, c))),
    "x3": ("worker", along_worker(lambda x, z, c: (x ^ 3, z, c))),
    "z1": ("worker", along_worker(lambda x, z, c: (x, z ^ 1, c))),
    "z3": ("worker", along_worker(lambda x, z, c: (x, z ^ 3, c))),
}


PLANES = [[i * 2 + c for i in range(16)] for c in range(2)]


def exchange(value):
    return lax.all_to_all(value, "worker", 0, 0, axis_index_groups=PLANES, tiled=True)


def swap(value, move):
    return lax.ppermute(value, *MOVES[move])


def body(token_ids, layer_inputs, key_grads, weights, anchors, momentum, plan):
    CHAIN.token = None
    x = layer_inputs
    w = weights.reshape(2, *WORKERS)
    a1, b1, z1, a2, b2, z3, gt_s, gt_o = pack_all(plan, token_ids.reshape(1, TOK), x, key_grads)
    got_a1 = swap(a1, "a")
    got_b1 = swap(b1, "b")
    got_z1 = swap(z1, "z")
    got_a2 = swap(a2, "a")
    got_b2 = swap(b2, "b")
    got_z3 = swap(z3, "z")

    def tile(name, far, flip_y, offset, at, recvs, hint=0):
        piece = (
            lambda z, y: ((1 - z if far else z) * 4 + (y ^ flip_y)) * ROWS + offset,
            len(recvs) - 1,
            at * HALF,
            [(0, None, 0, KV)],
        )
        return product(name, 0, [piece], HALF, [(KV, HALF)], 2 * HALF, plan, x, gt_s, recvs, hint)

    def dest(j, source, at, targets):
        return (lambda z, y: (z * 4 + (y ^ j)) * ROWS, source, at, targets)

    def other(name, pieces, outs, recvs, hint=0):
        return product(name, 1, pieces, ROWS, outs, 3 * ROWS, plan, x, gt_o, recvs, hint)

    lo, hi = (0, 256), (256, 512)
    half, pair = (256, ROWS), (2, 256, ROWS)

    far_a = swap(tile("send_a1", True, 3, 0, 1, (got_a1,)), "b")
    far_b = swap(tile("send_b1", True, 1, HALF, 1, (got_b1,)), "a")
    keep_a1 = tile("keep_a1", True, 0, 0, 0, (got_a1,))
    keep_b1 = tile("keep_b1", True, 0, HALF, 0, (got_b1,))
    near_a = swap(tile("send_a2", False, 3, 0, 1, (got_a1, got_a2)), "b")
    near_b = swap(tile("send_b2", False, 1, HALF, 1, (got_b1, got_b2)), "a")
    keep_a2 = tile("keep_a2", False, 0, 0, 0, (got_a1, got_a2))
    keep_b2 = tile("keep_b2", False, 0, HALF, 0, (got_b1, got_b2), MIDDLE)
    across = swap(
        sums("far", [(2, KV, HALF)], [(keep_a1, far_a, None, None, 0, 0), (keep_b1, far_b, None, None, 0, 1)]), "z"
    )
    send_0, send_1, stay_0, stay_1 = other(
        "other_1",
        [
            dest(2, 0, ROWS, [(0, 1, *lo), (1, 1, *hi)]),
            dest(1, 0, 0, [(0, 0, *lo), (3, None, *hi)]),
            dest(3, 0, 2 * ROWS, [(1, 0, *hi), (2, None, *lo)]),
        ],
        [pair, pair, half, half],
        (got_z1,),
        LONG,
    )
    got_0, got_1 = swap(send_0, "a"), swap(send_1, "b")
    near = sums("near", [(2, KV, HALF)], [(keep_a2, near_a, None, None, 0, 0), (keep_b2, near_b, None, None, 0, 1)])

    w_s, w_o = take(plan, w)
    inner_s, send_s = inner_sync(w_s, near, across)
    send, keep = sum_x(inner_s, swap(send_s, "core"), "sync_x1")
    recv = swap(send, "x1")
    last_0, last_1 = sums(
        "last", [half, half], [(stay_0, got_0, None, 1, 0, None), (stay_1, got_1, None, 1, 1, None)]
    )
    last_0, last_1 = swap(last_0, "b"), swap(last_1, "a")
    send, keep = halve("sync_x3", QUAD, keep, recv)
    recv = swap(send, "x3")
    mine_0, mine_1 = other("other_3", [dest(0, 1, 0, [(0, None, *lo), (1, None, *hi)])], [half, half], (got_z1, got_z3), SHORT)
    send, keep = sum_z(keep, recv, "sync_z1")
    recv = swap(send, "z1")
    send, keep = halve("sync_z3", (32, KV), keep, recv)
    recv = swap(send, "z3")
    inner_o, send_o = inner_other(w_o, (mine_0, got_0, last_0), (mine_1, got_1, last_1))
    core_o = swap(send_o, "core")
    anchor_new, momentum_new, short = outer_sync(plan, anchors, momentum, keep, recv)
    block = exchange(short)
    new = store(plan, inner_o)
    send_o, keep_o = sum_x(inner_o, core_o, "other_x1")
    recv_o = swap(send_o, "x1")
    send_o, keep_o = halve("other_x3", QUAD, keep_o, recv_o, LONG)
    recv_o = swap(send_o, "x3")
    send_o, keep_o = sum_z(keep_o, recv_o, "other_z1")
    recv_o = swap(send_o, "z1")
    send_o, keep_o = halve("other_z3", (32, KV), keep_o, recv_o)
    recv_o = swap(send_o, "z3")
    block = relay(block)
    new = mix(plan, inner_s, block, new, 0)
    pending = outer_other(plan, anchors, keep_o, recv_o)
    new = mix(plan, inner_s, swap(block, "core"), new, 1)
    return (new.reshape(1, 2, ROWS, KV), anchor_new, momentum_new, pending)


def solution(mesh):
    return jax.shard_map(
        body,
        mesh=mesh,
        in_specs=(
            P(("worker", "fsdp")),
            P(None, ("worker", "fsdp"), None),
            P(None, ("worker", "fsdp"), None),
            P("worker", None, "fsdp", None),
            P(None, ("fsdp", "worker"), None),
            P(("fsdp", "worker"), None),
            P(),
        ),
        out_specs=(
            P("worker", None, "fsdp", None),
            P(("fsdp", "worker"), None),
            P(("fsdp", "worker"), None),
            P(("fsdp", "worker"), None),
        ),
        check_vma=False,
    )
```

```python
import jax
import jax.numpy as jnp
from jax import lax
from jax.experimental import pallas as pl
from jax.experimental.pallas import tpu as pltpu
from jax.sharding import PartitionSpec as P

inner_rate = 0.25
decay_rate = 0.1
outer_rate = 0.7
outer_beta = 0.9
mix_weight = 0.5

TOK = 256
KV = 512
ROWS = 1024
HALF = 512
F32 = jnp.float32
BF16 = jnp.bfloat16

HBM = pl.BlockSpec(memory_space=pltpu.HBM)
ANY = pl.BlockSpec(memory_space=pl.ANY)
VM = pl.BlockSpec(memory_space=pltpu.VMEM)
SM = pl.BlockSpec(memory_space=pltpu.SMEM)
MIB = 1024 * 1024
BIG = 24
LONG = 2 * 10**10
SHORT = 3 * 10**9


def place():
    w = lax.axis_index("worker")
    f = lax.axis_index("fsdp")
    return w // 8, (w // 2) % 4, w % 2, f // 4, f % 4


def shape(*dims, dtype=BF16):
    return jax.ShapeDtypeStruct(dims, dtype)


def in_vmem(*dims):
    return pltpu.VMEM(dims, BF16)


def in_hbm(*dims):
    return pltpu.HBM(dims, BF16)


def pinned(value):
    return pltpu.with_memory_space_constraint(value, pltpu.HBM)


class Chain:
    def __init__(self):
        self.token = None


CHAIN = Chain()


def call(kernel, outs, args, specs, out_specs, scratch=(), aliases=None, name=None, vmem=16, hint=0):
    outs, out_specs = list(outs), list(out_specs)
    tokens = [] if CHAIN.token is None else [CHAIN.token]
    count = len(args)

    def chained(*refs):
        rest = refs[count + len(tokens) :]
        kernel(*refs[:count], *rest[: len(outs)], *rest[len(outs) + 1 :])

    *results, CHAIN.token = pl.pallas_call(
        chained,
        out_shape=outs + [in_hbm(8, 128)],
        in_specs=list(specs) + [HBM] * len(tokens),
        out_specs=out_specs + [HBM],
        scratch_shapes=list(scratch),
        compiler_params=pltpu.CompilerParams(vmem_limit_bytes=vmem * MIB),
        cost_estimate=pl.CostEstimate(flops=hint, bytes_accessed=0, transcendentals=0),
        input_output_aliases=aliases or {},
        name=name,
    )(*(pinned(a) if spec is HBM else a for a, spec in zip(args, specs)), *(pinned(t) for t in tokens))
    return results[0] if len(results) == 1 else results


def columns(start, width):
    return pl.ds(pl.multiple_of(start, width), width)


def pack(name, fragment, plan, ids, x, g, outs, pieces, g_to):
    def kernel(plan_ref, ids_ref, x_ref, g_ref, *rest):
        bufs, gt_ref = rest[: len(outs)], rest[len(outs)]
        gin, tok, sems = rest[len(outs) + 1 :]
        _, _, _, z, y = place()
        s = lax.rem(plan_ref[0], 2)
        layers = (s, 1 - s)
        first = [
            pltpu.make_async_copy(ids_ref, tok, sems.at[0]),
            pltpu.make_async_copy(g_ref.at[layers[fragment]], gin, sems.at[1]),
        ]
        copies = []
        for layer, start, width, out, at in pieces:
            col = pl.multiple_of(start(z, y), HALF)
            copies.append(
                pltpu.make_async_copy(
                    x_ref.at[layers[layer], :, pl.ds(col, width)],
                    bufs[out].at[:, pl.ds(at, width)],
                    sems.at[2 + len(copies)],
                )
            )
        for c in first + copies:
            c.start()
        for c in first:
            c.wait()
        gt = (gin[...].astype(F32).T * (tok[...] != 0).astype(F32)).astype(BF16)
        gt_ref[...] = gt
        for out, at in g_to:
            for h in range(2):
                bufs[out][:, at + h * TOK : at + (h + 1) * TOK] = gt[h * TOK : (h + 1) * TOK]
        for c in copies:
            c.wait()

    return call(
        kernel,
        [in_vmem(TOK, n) for n in outs] + [in_vmem(KV, TOK)],
        (plan, ids, x, g),
        [SM, HBM, HBM, HBM],
        [VM] * (len(outs) + 1),
        [
            pltpu.VMEM((TOK, KV), BF16),
            pltpu.VMEM((1, TOK), jnp.int32),
            pltpu.SemaphoreType.DMA((2 + len(pieces),)),
        ],
        name=name,
        vmem=BIG,
    )


def pack_all(plan, ids, x, g):
    def sync(far, flip_y, offset, out, at):
        return (0, lambda z, y: ((1 - z if far else z) * 4 + (y ^ flip_y)) * ROWS + offset, HALF, out, at * HALF)

    def other(j, out, at):
        return (1, lambda z, y: ((1 - z) * 4 + (y ^ j)) * ROWS, ROWS, out, at * ROWS)

    def pair(far, out):
        return [
            sync(far, 1, 0, out, 0),
            sync(far, 2, 0, out, 1),
            sync(far, 3, HALF, out + 1, 0),
            sync(far, 2, HALF, out + 1, 1),
        ]

    wide, half = 2 * HALF + KV, 2 * HALF
    a1, b1, gt_s = pack("pack_1", 0, plan, ids, x, g, [wide, wide], pair(True, 0), [(0, half), (1, half)])
    z1, a2, b2, z3, gt_o = pack(
        "pack_2",
        1,
        plan,
        ids,
        x,
        g,
        [3 * ROWS + KV, half, half, ROWS],
        [other(1, 0, 0), other(2, 0, 1), other(3, 0, 2), *pair(False, 1), other(0, 3, 0)],
        [(0, 3 * ROWS)],
    )
    return a1, b1, z1, a2, b2, z3, gt_s, gt_o


def product(name, fragment, pieces, width, out_shapes, g_at, plan, x, gt, recvs, hint=0):
    count = len(pieces)
    number = len(recvs)
    total = sum(len(p[3]) for p in pieces)

    def kernel(plan_ref, x_ref, gt_ref, *rest):
        recv_refs = rest[:number]
        outs = rest[number : number + len(out_shapes)]
        stage = rest[number + len(out_shapes) : number + 2 * len(out_shapes)]
        gts, xs, sems, out_sems = rest[number + 2 * len(out_shapes) :]
        _, _, _, z, y = place()
        s = lax.rem(plan_ref[0], 2)
        layer = s if fragment == 0 else 1 - s
        g_copies = [
            pltpu.make_async_copy(gt_ref, gts.at[:, pl.ds(0, TOK)], sems.at[2 * count]),
            *(
                pltpu.make_async_copy(
                    recv_refs[0].at[:, pl.ds(g_at + h * TOK, TOK)],
                    gts.at[pl.ds(h * TOK, TOK), pl.ds(TOK, TOK)],
                    sems.at[2 * count + 1 + h],
                )
                for h in range(2)
            ),
        ]
        copies = []
        for p, (own, source, at, _) in enumerate(pieces):
            copies.append(
                (
                    pltpu.make_async_copy(
                        x_ref.at[layer, :, columns(own(z, y), width)], xs.at[p, pl.ds(0, TOK)], sems.at[2 * p]
                    ),
                    pltpu.make_async_copy(
                        recv_refs[source].at[:, pl.ds(at, width)], xs.at[p, pl.ds(TOK, TOK)], sems.at[2 * p + 1]
                    ),
                )
            )
        for c in g_copies:
            c.start()
        for pair in copies:
            for c in pair:
                c.start()
        for c in g_copies:
            c.wait()
        done = []
        for p, (_, _, _, targets) in enumerate(pieces):
            for c in copies[p]:
                c.wait()
            for out, slot, k0, k1 in targets:
                src = stage[out] if slot is None else stage[out].at[slot]
                dst = outs[out] if slot is None else outs[out].at[slot]
                src[...] = jnp.dot(gts[k0:k1], xs[p], preferred_element_type=F32).astype(BF16)
                c = pltpu.make_async_copy(src, dst, out_sems.at[len(done)])
                c.start()
                done.append(c)
        for c in done:
            c.wait()

    return call(
        kernel,
        tuple(shape(*d) for d in out_shapes),
        (plan, x, gt, *recvs),
        [SM, ANY, ANY] + [ANY] * number,
        [ANY] * len(out_shapes),
        [
            *(pltpu.VMEM(d, BF16) for d in out_shapes),
            pltpu.VMEM((KV, 2 * TOK), BF16),
            pltpu.VMEM((count, 2 * TOK, width), BF16),
            pltpu.SemaphoreType.DMA((2 * count + 3,)),
            pltpu.SemaphoreType.DMA((total,)),
        ],
        name=name,
        vmem=BIG,
        hint=hint,
    )


def flip(*terms):
    return sum(t.astype(F32) for t in terms).T


def stepped(w, gradient):
    return (w.astype(F32) * (1.0 - inner_rate * decay_rate) - inner_rate * gradient).astype(BF16)


WORKERS = (16, 2, 32, KV)


def take(plan, w):
    def kernel(plan_ref, w_ref, sync_ref, other_ref, sems):
        s = lax.rem(plan_ref[0], 2)
        copies = [
            pltpu.make_async_copy(w_ref.at[layer], out, sems.at[i])
            for i, (layer, out) in enumerate(((s, sync_ref), (1 - s, other_ref)))
        ]
        for c in copies:
            c.start()
        for c in copies:
            c.wait()

    return call(
        kernel,
        (in_vmem(*WORKERS),) * 2,
        (plan, w),
        [SM, HBM],
        [VM] * 2,
        [pltpu.SemaphoreType.DMA((2,))],
        name="take",
    )


def inner_sync(w, near, across):
    def kernel(w_ref, near_ref, z_ref, inner_ref, send_ref, sem):
        for h in range(2):
            for q in range(4):
                cols = pl.ds(q * 128, 128)
                i = h * 8 + q * 2
                gradient = flip(near_ref[h, :, cols], z_ref[h, :, cols])
                inner_ref[i : i + 2] = stepped(w_ref[i : i + 2].reshape(128, KV), gradient).reshape(2, 2, 32, KV)
        out = pltpu.make_async_copy(inner_ref.at[:, 1 - place()[2]], send_ref, sem)
        out.start()
        out.wait()

    return call(
        kernel,
        (shape(*WORKERS), shape(16, 32, KV)),
        (w, near, across),
        [VM] * 3,
        [VM, ANY],
        [pltpu.SemaphoreType.DMA],
        name="inner_sync",
    )


def inner_other(w, first, second):
    def kernel(w_ref, k0, r0, l0, k1, r1, l1, inner_ref, send_ref, sem):
        for q in range(8):
            cols = pl.ds(q * 128, 128)
            i = q * 2
            gradient = jnp.concatenate(
                [flip(k[:, cols], r[0, :, cols], l[:, cols]) for k, r, l in ((k0, r0, l0), (k1, r1, l1))], axis=1
            )
            inner_ref[i : i + 2] = stepped(w_ref[i : i + 2].reshape(128, KV), gradient).reshape(2, 2, 32, KV)
        out = pltpu.make_async_copy(inner_ref.at[:, 1 - place()[2]], send_ref, sem)
        out.start()
        out.wait()

    return call(
        kernel,
        (shape(*WORKERS), shape(16, 32, KV)),
        (w, *first, *second),
        [VM] * 7,
        [VM, ANY],
        [pltpu.SemaphoreType.DMA],
        name="inner_other",
    )


def store(plan, inner):
    def kernel(plan_ref, inner_ref, new_ref, sem):
        out = pltpu.make_async_copy(inner_ref, new_ref.at[1 - lax.rem(plan_ref[0], 2)], sem)
        out.start()
        out.wait()

    return call(
        kernel,
        (shape(2, *WORKERS),),
        (plan, inner),
        [SM, VM],
        [ANY],
        [pltpu.SemaphoreType.DMA],
        name="store",
    )


def plus(a, b):
    return (a.astype(F32) + b.astype(F32)).astype(BF16)


def to_x(inner_ref, recv_ref, send_ref, keep_ref):
    x, _, core, _, _ = place()
    for ref, at, j in ((send_ref, 0, 1), (send_ref, 1, 2), (keep_ref, 0, 0), (keep_ref, 1, 3)):
        block = pl.ds((x ^ j) * 4, 4)
        ref[at] = plus(inner_ref[block, core], recv_ref[block])


def to_z(keep_ref, recv_ref, send_ref, stay_ref):
    zh = place()[1]
    for ref, at, j in ((send_ref, 0, 1), (send_ref, 1, 2), (stay_ref, 0, 0), (stay_ref, 1, 3)):
        ref[at] = plus(keep_ref[zh ^ j], recv_ref[zh ^ j])


QUAD = (4, 32, KV)


def sums(name, outs, pairs, hint=0):
    def kernel(*refs):
        out_refs = refs[2 * len(pairs) :]
        for i, (_, _, at_a, at_b, out, slot) in enumerate(pairs):
            a, b = refs[2 * i], refs[2 * i + 1]
            total = plus(a[...] if at_a is None else a[at_a], b[...] if at_b is None else b[at_b])
            if slot is None:
                out_refs[out][...] = total
            else:
                out_refs[out][slot] = total

    args = [t for p in pairs for t in p[:2]]
    return call(
        kernel,
        [shape(*d) for d in outs],
        args,
        [VM] * len(args),
        [VM] * len(outs),
        name=name,
        hint=hint,
    )


def halve(name, dims, keep, recv, hint=0):
    return sums(name, [dims] * 2, [(keep, recv, 1, 1, 0, None), (keep, recv, 0, 0, 1, None)], hint)


def sum_x(inner, recv, name):
    return call(to_x, (shape(2, *QUAD),) * 2, (inner, recv), [VM] * 2, [VM] * 2, name=name)


def sum_z(keep, recv, name):
    return call(to_z, (shape(2, 32, KV),) * 2, (keep, recv), [VM] * 2, [VM] * 2, name=name)


def outer_sync(plan, anchors, momentum, keep, recv):
    def kernel(plan_ref, anchor_ref, momentum_ref, a, b, new_ref, moment_ref, short_ref):
        s = lax.rem(plan_ref[0], 2)
        mean = (a[...].astype(F32) + b[...].astype(F32)) / 32
        anchor = anchor_ref[s]
        outer_grad = anchor - mean
        moment = outer_beta * momentum_ref[...] + outer_grad
        new = anchor - outer_rate * (outer_grad + outer_beta * moment)
        new_ref[...] = new
        moment_ref[...] = moment
        for i in range(16):
            short_ref[i] = new.astype(BF16)

    return call(
        kernel,
        (shape(32, KV, dtype=F32), shape(32, KV, dtype=F32), shape(16, 32, KV)),
        (plan, anchors, momentum, keep, recv),
        [SM] + [VM] * 4,
        [VM] * 3,
        name="outer_sync",
        hint=LONG,
    )


def relay(value):
    def kernel(value_ref, out_ref):
        out_ref[...] = value_ref[...]

    return call(kernel, (shape(*value.shape),), (value,), [VM], [VM], name="relay")


def outer_other(plan, anchors, keep, recv):
    def kernel(plan_ref, anchor_ref, a, b, out_ref):
        other = 1 - lax.rem(plan_ref[0], 2)
        out_ref[...] = anchor_ref[other] - (a[...].astype(F32) + b[...].astype(F32)) / 32

    return call(
        kernel,
        (shape(32, KV, dtype=F32),),
        (plan, anchors, keep, recv),
        [SM] + [VM] * 3,
        [VM],
        name="outer_other",
        hint=LONG,
    )


def mix(plan, inner, rows, new, far):
    def kernel(plan_ref, inner_ref, rows_ref, _, out_ref, stage, sem):
        core = place()[2]
        c = 1 - core if far else core
        stage[...] = (
            mix_weight * inner_ref[:, c].astype(F32) + (1.0 - mix_weight) * rows_ref[...].astype(F32)
        ).astype(BF16)
        out = pltpu.make_async_copy(stage, out_ref.at[lax.rem(plan_ref[0], 2), :, c], sem)
        out.start()
        out.wait()

    return call(
        kernel,
        (shape(2, *WORKERS),),
        (plan, inner, rows, new),
        [SM, VM, VM, ANY],
        [ANY],
        [pltpu.VMEM((16, 32, KV), BF16), pltpu.SemaphoreType.DMA],
        aliases={3: 0},
        name="mix_far" if far else "mix_own",
    )


def along_fsdp(move):
    return [(z * 4 + y, move(z, y)) for z in range(2) for y in range(4)]


def along_worker(move):
    def index(x, z, c):
        return (x * 4 + z) * 2 + c

    return [(index(x, z, c), index(*move(x, z, c))) for x in range(4) for z in range(4) for c in range(2)]


MOVES = {
    "a": ("fsdp", along_fsdp(lambda z, y: z * 4 + (y ^ 1))),
    "b": ("fsdp", along_fsdp(lambda z, y: z * 4 + (y ^ 3))),
    "z": ("fsdp", along_fsdp(lambda z, y: (1 - z) * 4 + y)),
    "core": ("worker", along_worker(lambda x, z, c: (x, z, 1 - c))),
    "x1": ("worker", along_worker(lambda x, z, c: (x ^ 1, z, c))),
    "x3": ("worker", along_worker(lambda x, z, c: (x ^ 3, z, c))),
    "z1": ("worker", along_worker(lambda x, z, c: (x, z ^ 1, c))),
    "z3": ("worker", along_worker(lambda x, z, c: (x, z ^ 3, c))),
}


PLANES = [[i * 2 + c for i in range(16)] for c in range(2)]


def exchange(value):
    return lax.all_to_all(value, "worker", 0, 0, axis_index_groups=PLANES, tiled=True)


def swap(value, move):
    return lax.ppermute(value, *MOVES[move])


def body(token_ids, layer_inputs, key_grads, weights, anchors, momentum, plan):
    CHAIN.token = None
    x = layer_inputs
    w = weights.reshape(2, *WORKERS)
    a1, b1, z1, a2, b2, z3, gt_s, gt_o = pack_all(plan, token_ids.reshape(1, TOK), x, key_grads)
    got_a1 = swap(a1, "a")
    got_b1 = swap(b1, "b")
    got_z1 = swap(z1, "z")
    got_a2 = swap(a2, "a")
    got_b2 = swap(b2, "b")
    got_z3 = swap(z3, "z")

    def tile(name, far, flip_y, offset, at, recvs, hint=0):
        piece = (
            lambda z, y: ((1 - z if far else z) * 4 + (y ^ flip_y)) * ROWS + offset,
            len(recvs) - 1,
            at * HALF,
            [(0, None, 0, KV)],
        )
        return product(name, 0, [piece], HALF, [(KV, HALF)], 2 * HALF, plan, x, gt_s, recvs, hint)

    def dest(j, source, at, targets):
        return (lambda z, y: (z * 4 + (y ^ j)) * ROWS, source, at, targets)

    def other(name, pieces, outs, recvs, hint=0):
        return product(name, 1, pieces, ROWS, outs, 3 * ROWS, plan, x, gt_o, recvs, hint)

    lo, hi = (0, 256), (256, 512)
    half, pair = (256, ROWS), (2, 256, ROWS)

    far_a = swap(tile("send_a1", True, 3, 0, 1, (got_a1,)), "b")
    far_b = swap(tile("send_b1", True, 1, HALF, 1, (got_b1,)), "a")
    keep_a1 = tile("keep_a1", True, 0, 0, 0, (got_a1,))
    keep_b1 = tile("keep_b1", True, 0, HALF, 0, (got_b1,))
    near_a = swap(tile("send_a2", False, 3, 0, 1, (got_a1, got_a2)), "b")
    near_b = swap(tile("send_b2", False, 1, HALF, 1, (got_b1, got_b2)), "a")
    keep_a2 = tile("keep_a2", False, 0, 0, 0, (got_a1, got_a2))
    keep_b2 = tile("keep_b2", False, 0, HALF, 0, (got_b1, got_b2), 2 * LONG)
    across = swap(
        sums("far", [(2, KV, HALF)], [(keep_a1, far_a, None, None, 0, 0), (keep_b1, far_b, None, None, 0, 1)]), "z"
    )
    send_0, send_1, stay_0, stay_1 = other(
        "other_1",
        [
            dest(2, 0, ROWS, [(0, 1, *lo), (1, 1, *hi)]),
            dest(1, 0, 0, [(0, 0, *lo), (3, None, *hi)]),
            dest(3, 0, 2 * ROWS, [(1, 0, *hi), (2, None, *lo)]),
        ],
        [pair, pair, half, half],
        (got_z1,),
        LONG,
    )
    got_0, got_1 = swap(send_0, "a"), swap(send_1, "b")
    near = sums("near", [(2, KV, HALF)], [(keep_a2, near_a, None, None, 0, 0), (keep_b2, near_b, None, None, 0, 1)])

    w_s, w_o = take(plan, w)
    inner_s, send_s = inner_sync(w_s, near, across)
    send, keep = sum_x(inner_s, swap(send_s, "core"), "sync_x1")
    recv = swap(send, "x1")
    last_0, last_1 = sums(
        "last", [half, half], [(stay_0, got_0, None, 1, 0, None), (stay_1, got_1, None, 1, 1, None)]
    )
    last_0, last_1 = swap(last_0, "b"), swap(last_1, "a")
    send, keep = halve("sync_x3", QUAD, keep, recv)
    recv = swap(send, "x3")
    mine_0, mine_1 = other("other_3", [dest(0, 1, 0, [(0, None, *lo), (1, None, *hi)])], [half, half], (got_z1, got_z3), SHORT)
    send, keep = sum_z(keep, recv, "sync_z1")
    recv = swap(send, "z1")
    inner_o, send_o = inner_other(w_o, (mine_0, got_0, last_0), (mine_1, got_1, last_1))
    core_o = swap(send_o, "core")
    send, keep = halve("sync_z3", (32, KV), keep, recv, LONG)
    recv = swap(send, "z3")
    send_o, keep_o = sum_x(inner_o, core_o, "other_x1")
    recv_o = swap(send_o, "x1")
    anchor_new, momentum_new, short = outer_sync(plan, anchors, momentum, keep, recv)
    block = exchange(short)
    send_o, keep_o = halve("other_x3", QUAD, keep_o, recv_o, LONG)
    recv_o = swap(send_o, "x3")
    new = store(plan, inner_o)
    send_o, keep_o = sum_z(keep_o, recv_o, "other_z1")
    recv_o = swap(send_o, "z1")
    send_o, keep_o = halve("other_z3", (32, KV), keep_o, recv_o)
    recv_o = swap(send_o, "z3")
    block = relay(block)
    new = mix(plan, inner_s, block, new, 0)
    pending = outer_other(plan, anchors, keep_o, recv_o)
    new = mix(plan, inner_s, swap(block, "core"), new, 1)
    return (new.reshape(1, 2, ROWS, KV), anchor_new, momentum_new, pending)


def solution(mesh):
    return jax.shard_map(
        body,
        mesh=mesh,
        in_specs=(
            P(("worker", "fsdp")),
            P(None, ("worker", "fsdp"), None),
            P(None, ("worker", "fsdp"), None),
            P("worker", None, "fsdp", None),
            P(None, ("fsdp", "worker"), None),
            P(("fsdp", "worker"), None),
            P(),
        ),
        out_specs=(
            P("worker", None, "fsdp", None),
            P(("fsdp", "worker"), None),
            P(("fsdp", "worker"), None),
            P(("fsdp", "worker"), None),
        ),
        check_vma=False,
    )
```
